32 devices in a mesh: exp: 8 (over z, y), hid: 4 (over x, core).
Axes of the slice: x: 2, y: 2, z: 4, core: 2. Of those that a mesh axis runs over, the one named last changes fastest.
Arguments:
- tokens: bfloat16 [8, 2048, 768], P('exp', 'hid'), may hold values from -6 to 6
- cotangent: bfloat16 [8, 2048, 768], P('exp', 'hid'), may hold values from -6 to 6
- routes: int32 [8, 2048, 2], P('exp', 'hid'), may hold values from 0 to 7, all different within a row; in each aligned block of 512 rows (0 to 511, 512 to 1023, ..., all dimensions but the last counted through in order) at most 288 rows name the same one
- segments: int32 [8, 2048], P('exp'), may hold values from 0 to 2, as said below
- lengths: int32 [8], P('exp'), may hold values from 1920 to 2048
- gain_attn: float32 [768], replicated, may hold values from 0.5 to 1.5
- gain_moe: float32 [768], replicated, may hold values from 0.5 to 1.5
- w_qkv: bfloat16 [768, 2304], replicated, may hold values from -0.21875 to 0.21875
- w_out: bfloat16 [768, 768], replicated, may hold values from -1.75 to 1.75
- router_w: float32 [768, 8], replicated, may hold values from -0.15 to 0.15
- router_first: float32 [768, 4], replicated, may hold values from -6 to 6
- router_second: float32 [768, 4], replicated, may hold values from 0.01 to 1
- up_w: float32 [8, 768, 3072], P('exp', None, 'hid'), may hold values from -0.21875 to 0.21875
- down_w: float32 [8, 3072, 768], P('exp', 'hid'), may hold values from -0.109375 to 0.109375
- up_first: float32 [8, 768, 3072], P('exp', None, 'hid'), may hold values from -6 to 6
- up_second: float32 [8, 768, 3072], P('exp', None, 'hid'), may hold values from 0.01 to 1
- down_first: float32 [8, 3072, 768], P('exp', 'hid'), may hold values from -6 to 6
- down_second: float32 [8, 3072, 768], P('exp', 'hid'), may hold values from 0.01 to 1
Outputs:
- out_tokens: bfloat16 [8, 2048, 768], P('exp', 'hid')
- grad_tokens: bfloat16 [8, 2048, 768], P('exp', 'hid')
- grad_qkv: float32 [768, 2304], replicated
- grad_out_proj: float32 [768, 768], replicated
- grad_gain_attn: float32 [768], replicated
- grad_gain_moe: float32 [768], replicated
- grad_router: float32 [768, 8], replicated
- router_next: float32 [768, 8], replicated
- router_first_next: float32 [768, 4], replicated
- router_second_next: float32 [768, 4], replicated
- grad_up: float32 [8, 768, 3072], P('exp', None, 'hid')
- grad_down: float32 [8, 3072, 768], P('exp', 'hid')
- up_next: float32 [8, 768, 3072], P('exp', None, 'hid')
- down_next: float32 [8, 3072, 768], P('exp', 'hid')
- up_first_next: float32 [8, 768, 3072], P('exp', None, 'hid')
- up_second_next: float32 [8, 768, 3072], P('exp', None, 'hid')
- down_first_next: float32 [8, 3072, 768], P('exp', 'hid')
- down_second_next: float32 [8, 3072, 768], P('exp', 'hid')
The draws below stay inside these ranges and needn't reach their ends.
Inputs may be any that keep to these rules, and one draw needn't show every extreme that they name: `routes`: each token names two different experts. Among the tokens of one device no expert is named by more than 288 tokens, and in some devices one is named by exactly 288. `segments`: each row holds three documents in order, numbered 0, 1, 2; document 1 begins within the first 256 positions and ends within the last 256.
All inputs are finite; a program needn't handle non-finite values.
Results may differ from the reference program's by a relative error of at most 0.014.
Values may be sent and summed in bfloat16 or wider, within the bound.
No kernel may reach another device: no remote copies, remote signals or barrier semaphores. Data moves between devices by JAX's collectives and lax.ppermute only.
A program may use at most 384 MiB of HBM per device.

```python
import math
import jax
import jax.numpy as jnp
import numpy as np
from jax import lax

D = 768
HEADS = 12
HEAD_DIM = 64
FF = 3072
EXPERTS = 8
FROZEN = 4
ROW_LEN = 2048
ROWS = 8
TOK_DEV = 512
CAP = 192
MOST = 288
N_EXP = 8
N_HID = 4


def draw_segments(key, part):
    key = jax.random.fold_in(key, 11)
    first_key, last_key = jax.random.split(key)
    first_cut = jax.random.randint(first_key, (ROWS, 1), 1, ROW_LEN // 8)
    last_cut = jax.random.randint(last_key, (ROWS, 1), ROW_LEN - ROW_LEN // 8, ROW_LEN)
    positions = jnp.arange(ROW_LEN, dtype=jnp.int32)[None, :]
    return (positions >= first_cut).astype(jnp.int32) + (positions >= last_cut).astype(jnp.int32)


def touch_ends(values, rng, low, top_value):
    shape = values.shape
    spot = [jax.random.randint(jax.random.fold_in(rng, axis), (), 0, shape[axis]) for axis in range(len(shape))]
    values = values.at[tuple(spot)].set(low)
    longest = shape.index(max(shape))
    spot[longest] = (spot[longest] + 1) % shape[longest]
    return values.at[tuple(spot)].set(top_value)


def steps_of(rng, dims, shards, low, high):
    def one(dim, shards_of):
        steps = jax.random.uniform(jax.random.fold_in(jax.random.fold_in(rng, 6), dim), (shards_of,), jnp.float32, low / len(shards), high / len(shards))
        return jnp.repeat(jnp.exp(steps), dims[dim] // shards_of).reshape((-1,) + (1,) * (len(dims) - dim - 1))

    factor_of = one(*shards[0])
    for cut in shards[1:]:
        factor_of = factor_of * one(*cut)
    return factor_of


def deal_out(own_key, own, number, rows, number_of, top, reach, skew):
    order = jax.random.permutation(own_key, number_of)
    crowded, ordinary = shares(number_of, rows * top, reach, skew, True), shares(number_of, rows * top, reach, skew, False)
    places = jnp.arange(number_of)

    def named(tallies, rotation):
        used = int((tallies > 0).sum())
        fixed = max(1, used // 4)
        shifted = fixed + (places - fixed + rotation * (used - fixed)) % max(1, number_of - fixed)
        return jnp.zeros((number_of,), jnp.int32).at[order[jnp.where(places < fixed, places, shifted)]].set(jnp.asarray(tallies, jnp.int32))

    tallies = jnp.where(number % 4 == 0, named(crowded, number // 4), named(ordinary, number - number // 4 - 1))
    mixed = jax.random.permutation(jax.random.fold_in(own, 3), number_of)
    donor, taker = mixed[0:number_of // 2 * 2:2], mixed[1:number_of // 2 * 2:2]
    slack = jnp.minimum(tallies[donor] - 1, reach - tallies[taker]) // 2
    slack = jnp.where((donor == order[0]) | (taker == order[0]) | (tallies[taker] == 0), 0, jnp.maximum(slack, 0))
    shifted = jax.random.randint(jax.random.fold_in(own, 4), (number_of // 2,), 0, 1 << 20) % (slack + 1)
    tallies = tallies.at[donor].add(-shifted).at[taker].add(shifted)
    labels = jnp.searchsorted(jnp.cumsum(tallies), jnp.arange(rows * top), side="right").astype(jnp.int32)
    grid = labels.reshape(top, rows).T
    grid = grid[jax.random.permutation(jax.random.fold_in(own, 1), rows)]
    rotation = jax.random.randint(jax.random.fold_in(own, 2), (rows, 1), 0, top)
    return jnp.take_along_axis(grid, (jnp.arange(top)[None, :] + rotation) % top, axis=1)


def shares(count, total, most, skew, full):
    portions = [(1 << 20) // math.isqrt(standing ** skew) + 1 for standing in range(1, count + 1)]
    largest = most if full else min(most, max(-(-total // count), total * portions[0] // sum(portions)))
    least = 1 if total - largest >= count - 1 else 0
    holding, spare = [largest] + [least] * (count - 1), total - largest - least * (count - 1)
    while spare > 0:
        movable = [i for i in range(1, count) if holding[i] < largest] or [i for i in range(1, count) if holding[i] < most]
        whole, remaining = sum([portions[i] for i in movable]), spare
        for i in movable:
            more = min(most - holding[i], max(1, remaining * portions[i] // whole), spare)
            holding[i] = holding[i] + more
            spare = spare - more
    return np.array(holding)


def scatter_about(key, dims, width, limit, cuts=(), kind=jnp.bfloat16):
    values = width * jax.random.normal(key, dims, jnp.float32)
    if cuts:
        values = values * steps_of(key, dims, cuts, -0.22, 0.18)
    return jnp.clip(values, -limit, limit).astype(kind)


def setup_inputs(seed: int = 0) -> dict:
    key_list = jax.random.split(jax.random.key(seed), 19)
    tokens = scatter_about(key_list[0], (ROWS, ROW_LEN, D), 1.0, 6.0, ((0, 8), (1, 4)))
    cotangent = scatter_about(key_list[1], (ROWS, ROW_LEN, D), 1.0, 6.0, ((0, 8), (1, 4)))
    routes_keys = jax.random.split(jax.random.fold_in(key_list[2], 1), ROWS * ROW_LEN // TOK_DEV)
    routes_turns = jax.random.permutation(jax.random.fold_in(key_list[2], 3), ROWS * ROW_LEN // TOK_DEV)
    routes = jax.vmap(lambda own, number: deal_out(jax.random.fold_in(key_list[2], 2), own, number, TOK_DEV, EXPERTS, 2, MOST, 1))(routes_keys, routes_turns).reshape((ROWS, ROW_LEN, 2))
    segments = draw_segments(jax.random.fold_in(key_list[18], 71), 0)
    lengths = touch_ends(jax.random.randint(key_list[4], (ROWS,), ROW_LEN - ROW_LEN // 16, ROW_LEN + 1), jax.random.fold_in(key_list[4], 1), ROW_LEN - ROW_LEN // 16, ROW_LEN).astype(jnp.int32)
    gain_attn = jnp.clip(1.0 + 0.1 * jax.random.normal(key_list[5], (D,), jnp.float32), 0.5, 1.5)
    gain_moe = jnp.clip(1.0 + 0.1 * jax.random.normal(key_list[6], (D,), jnp.float32), 0.5, 1.5)
    w_qkv = scatter_about(key_list[7], (D, 3 * D), D ** -0.5, 0.21875)
    w_out = scatter_about(key_list[8], (D, D), (max(1, D // 64)) ** -0.5, 1.75)
    router_w = scatter_about(key_list[9], (D, EXPERTS), 0.025, 0.15, (), jnp.float32)
    router_first = scatter_about(key_list[10], (D, EXPERTS - FROZEN), 1.0, 6.0, (), jnp.float32)
    router_second = jnp.clip(jnp.exp(jax.random.uniform(key_list[11], (D, EXPERTS - FROZEN), jnp.float32, math.log(0.01), math.log(1.0))), 0.01, 1.0)
    up_w = scatter_about(key_list[12], (EXPERTS, D, FF), D ** -0.5, 0.21875, ((0, 8), (2, 4)), jnp.float32)
    down_w = scatter_about(key_list[13], (EXPERTS, FF, D), FF ** -0.5, 0.109375, ((0, 8), (1, 4)), jnp.float32)
    up_first = scatter_about(key_list[14], (EXPERTS, D, FF), 1.0, 6.0, ((0, 8), (2, 4)), jnp.float32)
    up_second = jnp.clip(jnp.exp(math.log(1.0) - 4.6051702 * jax.random.uniform(key_list[15], (EXPERTS, D, FF), jnp.float32) ** steps_of(key_list[15], (EXPERTS, D, FF), ((0, 8), (2, 4)), -0.2, 0.2)), 0.01, 1.0)
    down_first = scatter_about(key_list[16], (EXPERTS, FF, D), 1.0, 6.0, ((0, 8), (1, 4)), jnp.float32)
    down_second = jnp.clip(jnp.exp(math.log(1.0) - 4.6051702 * jax.random.uniform(key_list[17], (EXPERTS, FF, D), jnp.float32) ** steps_of(key_list[17], (EXPERTS, FF, D), ((0, 8), (1, 4)), -0.2, 0.2)), 0.01, 1.0)
    return dict(tokens=tokens, cotangent=cotangent, routes=routes, segments=segments, lengths=lengths, gain_attn=gain_attn, gain_moe=gain_moe, w_qkv=w_qkv, w_out=w_out, router_w=router_w, router_first=router_first, router_second=router_second, up_w=up_w, down_w=down_w, up_first=up_first, up_second=up_second, down_first=down_first, down_second=down_second)


precise = lax.Precision.HIGHEST
norm_eps = 1e-06
beta_one = 0.9
beta_two = 0.999
learn_rate = 0.01
adam_eps = 1e-08
adam_steps = 10.0
masked_score = -1e+30

@jax.custom_vjp
def low(v):
    return lax.optimization_barrier(v.astype(jnp.bfloat16)).astype(jnp.float32)

@jax.custom_vjp
def low_back(v):
    return v

def low_keep(v):
    return (low(v), None)

def low_pass(kept, grad):
    return (grad,)

def back_keep(v):
    return (v, None)

def back_low(kept, grad):
    return (low(grad),)
low.defvjp(low_keep, low_pass)
low_back.defvjp(back_keep, back_low)

def rms_scale(values_in, gain_vec):
    mean_square = lax.optimization_barrier(jnp.mean(values_in * values_in, axis=-1, keepdims=True))
    return values_in * lax.rsqrt(mean_square + norm_eps) * gain_vec

def adam_update(weight, gradient, first_moment, second_moment, live_mask):
    first_next = beta_one * first_moment + (1.0 - beta_one) * gradient
    second_next = beta_two * second_moment + (1.0 - beta_two) * gradient * gradient
    first_hat = first_next / (1.0 - beta_one ** adam_steps)
    second_hat = second_next / (1.0 - beta_two ** adam_steps)
    weight_next = weight - learn_rate * first_hat / (jnp.sqrt(second_hat) + adam_eps)
    return (jnp.where(live_mask, weight_next, weight), jnp.where(live_mask, first_next, first_moment), jnp.where(live_mask, second_next, second_moment))

def slot_table(routes):
    flat_routes = routes.reshape(N_EXP * N_HID, TOK_DEV * 2)
    expert_ids = jnp.arange(EXPERTS, dtype=jnp.int32)
    hit_table = (flat_routes[:, :, None] == expert_ids).astype(jnp.int32)
    before = jnp.cumsum(hit_table, axis=1, dtype=jnp.int32) - hit_table
    return lax.optimization_barrier(jnp.sum(before * hit_table, axis=-1, dtype=jnp.int32)).reshape(ROWS, ROW_LEN, 2)

def attend_row(row_items):
    query_row, key_row, value_row, seg_row, length_row = row_items
    block_rows = min(ROW_LEN, 512)
    key_pos = jnp.arange(ROW_LEN, dtype=jnp.int32)

    def one_block(block_start):
        query_block = lax.dynamic_slice_in_dim(query_row, block_start, block_rows, 0)
        query_pos = block_start + jnp.arange(block_rows, dtype=jnp.int32)
        query_seg = lax.dynamic_slice_in_dim(seg_row, block_start, block_rows, 0)
        allowed = (query_seg[:, None] == seg_row[None, :]) & (key_pos[None, :] <= query_pos[:, None]) & ((key_pos[None, :] < length_row) | (key_pos[None, :] == query_pos[:, None]))
        raw_scores = low_back(0.125 * jnp.einsum('qhd,khd->hqk', query_block, key_row, precision=precise))
        scores = jnp.where(allowed[None], raw_scores, masked_score)
        row_top = lax.optimization_barrier(jnp.max(scores, axis=-1, keepdims=True))
        log_total = row_top + jnp.log(lax.optimization_barrier(jnp.sum(jnp.exp(scores - row_top), axis=-1, keepdims=True)))
        prob_rows = low(jnp.exp(scores - log_total))
        return jnp.einsum('hqk,khd->qhd', prob_rows, value_row, precision=precise)
    starts = jnp.arange(ROW_LEN // block_rows, dtype=jnp.int32) * block_rows
    blocks = lax.map(jax.checkpoint(one_block), starts)
    return blocks.reshape(ROW_LEN, HEADS * HEAD_DIM)

def expert_apply(expert_items):
    slot_rows, up_weight, down_weight = expert_items
    pre_act = low_back(jnp.dot(slot_rows, low(up_weight), precision=precise))
    act_rows = low(jax.nn.gelu(pre_act, approximate=True))
    return low(low_back(jnp.dot(act_rows, low(down_weight), precision=precise)))

def reference(tokens, cotangent, routes, segments, lengths, gain_attn, gain_moe, w_qkv, w_out, router_w, router_first, router_second, up_w, down_w, up_first, up_second, down_first, down_second):
    slot_pos = slot_table(routes)
    kept_mask = slot_pos < CAP
    row_ids = jnp.arange(ROWS, dtype=jnp.int32)[:, None]
    pos_ids = jnp.arange(ROW_LEN, dtype=jnp.int32)[None, :]
    source = jnp.broadcast_to((row_ids * N_HID + pos_ids // TOK_DEV)[:, :, None], (ROWS, ROW_LEN, 2))
    slot_index = jnp.where(kept_mask, slot_pos, CAP).astype(jnp.int32)
    fetch_index = jnp.minimum(slot_pos, CAP - 1).astype(jnp.int32)

    def forward(token_vals, qkv_weight, out_weight, gain_one, gain_two, route_weight, up_weight, down_weight):
        normed_one = rms_scale(token_vals, gain_one)
        qkv_vals = jnp.einsum('rld,de->rle', low(normed_one), qkv_weight, precision=precise)
        shape_heads = (ROWS, ROW_LEN, HEADS, HEAD_DIM)
        query_vals = low(low_back(qkv_vals[..., :D])).reshape(shape_heads)
        key_vals = low(low_back(qkv_vals[..., D:2 * D])).reshape(shape_heads)
        value_vals = low(low_back(qkv_vals[..., 2 * D:])).reshape(shape_heads)
        attended = lax.map(attend_row, (query_vals, key_vals, value_vals, segments, lengths))
        attended = low(low_back(attended))
        attn_out = low_back(jnp.einsum('rld,de->rle', attended, out_weight, precision=precise))
        residual = token_vals + attn_out
        normed_two = rms_scale(residual, gain_two)
        logits = jnp.einsum('rld,de->rle', normed_two, route_weight, precision=precise)
        gate_vals = jax.nn.softmax(jnp.take_along_axis(logits, routes, axis=-1), axis=-1)
        pair_rows = jnp.broadcast_to(low(normed_two)[:, :, None, :], (ROWS, ROW_LEN, 2, D))
        dispatched = jnp.zeros((EXPERTS, N_EXP * N_HID, CAP, D), jnp.float32)
        dispatched = dispatched.at[routes, source, slot_index].add(pair_rows, mode='drop')
        dispatched = low_back(dispatched)
        expert_out = lax.map(jax.checkpoint(expert_apply), (dispatched.reshape(EXPERTS, N_EXP * N_HID * CAP, D), up_weight, down_weight))
        expert_out = expert_out.reshape(EXPERTS, N_EXP * N_HID, CAP, D)
        fetched = jnp.where(kept_mask[..., None], expert_out[routes, source, fetch_index], 0.0)
        return residual + lax.optimization_barrier(jnp.sum(gate_vals[..., None] * fetched, axis=2))
    primals = (tokens.astype(jnp.float32), w_qkv.astype(jnp.float32), w_out.astype(jnp.float32), gain_attn, gain_moe, router_w, up_w, down_w)
    result, pullback = jax.vjp(forward, *primals)
    grads = pullback(cotangent.astype(jnp.float32))
    live_experts = jnp.arange(EXPERTS, dtype=jnp.int32) >= FROZEN
    live_columns = live_experts[None, :]
    live_blocks = live_experts[:, None, None]
    grad_router = jnp.where(live_columns, grads[5], 0.0)
    grad_up = jnp.where(live_blocks, grads[6], 0.0)
    grad_down = jnp.where(live_blocks, grads[7], 0.0)
    router_new, router_first_next, router_second_next = adam_update(router_w[:, FROZEN:], grad_router[:, FROZEN:], router_first, router_second, True)
    router_next = jnp.concatenate([router_w[:, :FROZEN], router_new], axis=1)
    up_next, up_first_next, up_second_next = adam_update(up_w, grad_up, up_first, up_second, live_blocks)
    down_next, down_first_next, down_second_next = adam_update(down_w, grad_down, down_first, down_second, live_blocks)
    return (result.astype(jnp.bfloat16), grads[0].astype(jnp.bfloat16), grads[1], grads[2], grads[3], grads[4], grad_router, router_next, router_first_next, router_second_next, grad_up, grad_down, up_next, down_next, up_first_next, up_second_next, down_first_next, down_second_next)
```

```python
import functools

import jax
import jax.numpy as jnp
from jax import lax
from jax.experimental import pallas as pl
from jax.experimental.pallas import tpu as pltpu
from jax.sharding import PartitionSpec as P

HEADS = 12
HEAD_DIM = 64

precise = lax.Precision.HIGHEST
norm_eps = 1e-06
beta_one = 0.9
beta_two = 0.999
learn_rate = 0.01
adam_eps = 1e-08
adam_steps = 10.0
masked_score = -1e30

bf16 = jnp.bfloat16
f32 = jnp.float32
MIB = 1 << 20


def mm(left, right, contract=((1,), (0,)), precision=None):
    return lax.dot_general(
        left, right, (contract, ((), ())), preferred_element_type=f32, precision=precision
    )


NT = ((1,), (1,))
TN = ((0,), (0,))


def swap(value, axis, distance):
    count = lax.axis_size(axis)
    return lax.ppermute(value, axis, [(i, i ^ distance) for i in range(count)])


def iota(shape, dim):
    return lax.broadcasted_iota(jnp.int32, shape, dim)


def split_three(value):
    high = value.astype(bf16)
    rest = value - high.astype(f32)
    mid = rest.astype(bf16)
    low = (rest - mid.astype(f32)).astype(bf16)
    return high, mid, low


def vmem_spec():
    return pl.BlockSpec(memory_space=pltpu.VMEM)


def smem_spec():
    return pl.BlockSpec(memory_space=pltpu.SMEM)


def params(mib):
    return pltpu.CompilerParams(vmem_limit_bytes=mib * MIB)


def cost(micros):
    return pl.CostEstimate(
        flops=int(micros * 1.1e9), bytes_accessed=int(micros * 3e6), transcendentals=0
    )


def tables_kernel(capacity, own_ref, routes_ref, dy_ref, hot_ref, pick0, pick1, *sends):
    experts = len(sends)
    count = routes_ref.shape[1]
    expert_row = iota((experts, count), 0) ^ own_ref[1]
    route_rows = [routes_ref[k : k + 1, :] for k in range(2)]
    hits = [expert_row == row for row in route_rows]
    hit = hits[0] | hits[1]
    hit_low = jnp.where(hit, 1.0, 0.0).astype(bf16)
    upper = jnp.where(iota((count, count), 0) < iota((count, count), 1), 1.0, 0.0).astype(bf16)
    slot = mm(hit_low, upper)
    slot = jnp.where(hit & (slot < capacity), slot, -1.0)
    row_id = iota((capacity, count), 0).astype(f32)
    for e in range(experts):
        hot_ref[e * capacity : (e + 1) * capacity, :] = jnp.where(
            row_id == slot[e : e + 1, :], 1.0, 0.0
        ).astype(bf16)
    rows = mm(hot_ref[...], dy_ref[...]).astype(bf16)
    for e, send in enumerate(sends):
        send[...] = rows[e * capacity : (e + 1) * capacity, :]
    index_rows = []
    for k in range(2):
        own_slot = jnp.sum(jnp.where(hits[k], slot, 0.0), axis=0, keepdims=True)
        place = (route_rows[k] ^ own_ref[1]).astype(f32) * capacity + own_slot
        index_rows.append(jnp.where(own_slot >= 0, place, -1.0))
    index_cols = jnp.concatenate(index_rows * 4, axis=0).T
    for k, pick in enumerate((pick0, pick1)):
        lane = iota(pick.shape, 1).astype(f32)
        pick[...] = jnp.where(lane == index_cols[:, k : k + 1], 1.0, 0.0).astype(bf16)


def make_tables(own, routes_t, dy, experts, capacity):
    count, width = dy.shape
    slots = experts * capacity
    shapes = [jax.ShapeDtypeStruct((slots, count), bf16)]
    shapes += [jax.ShapeDtypeStruct((count, slots), bf16)] * 2
    shapes += [jax.ShapeDtypeStruct((capacity, width), bf16)] * experts
    results = pl.pallas_call(
        functools.partial(tables_kernel, capacity),
        out_shape=shapes,
        in_specs=[smem_spec()] + [vmem_spec()] * 2,
        out_specs=[vmem_spec()] * len(shapes),
        compiler_params=params(48),
        name="slot_tables",
        cost_estimate=cost(4),
    )(own, routes_t, dy)
    return results[0], results[1:3], results[3:]


def qkv_kernel(
    own_ref, x0, x1, x2, x3, gain_ref, w_ref, a_ref, qkv_ref, k_ref, v_ref, heads_ref, x_buf, w_buf
):
    step = pl.program_id(0)
    width, cols = heads_ref.shape
    third = cols // 3

    @pl.when(step == 0)
    def turn():
        for h in range(width // third):

            @pl.when(own_ref[0] == h)
            def pick(h=h):
                for t in range(3):
                    start = t * width + h * third
                    heads_ref[:, t * third : (t + 1) * third] = w_ref[:, start : start + third]

        w_buf[...] = heads_ref[...].T

    for j, block in enumerate((x0, x1, x2, x3)):

        @pl.when(step == j)
        def take(block=block):
            x_buf[...] = block[...].astype(f32)

    x = x_buf[...]
    scale = lax.rsqrt(jnp.mean(x * x, axis=1, keepdims=True) + norm_eps)
    a = (x * scale * gain_ref[...]).astype(bf16)
    a_ref[...] = a
    qkv_t = mm(w_buf[...], a, NT).astype(bf16)
    qkv_ref[0:third, :] = qkv_t[0:third, :] * jnp.asarray(0.125, bf16)
    qkv_ref[third:, :] = qkv_t[third:, :]
    both = mm(a, heads_ref[:, third:]).astype(bf16)
    k_ref[...] = both[:, :third]
    v_ref[...] = both[:, third:]


def project_qkv(own, blocks, gain, w_qkv):
    count, width = blocks[0].shape
    parts = len(blocks)
    cols = w_qkv.shape[1] // parts
    third = cols // 3

    def whole(shape):
        return pl.BlockSpec(shape, lambda g, own_ref: (0, 0), pipeline_mode=pl.Buffered(1))

    return pl.pallas_call(
        qkv_kernel,
        out_shape=[
            jax.ShapeDtypeStruct((parts * count, width), bf16),
            jax.ShapeDtypeStruct((cols, parts * count), bf16),
            jax.ShapeDtypeStruct((parts * count, third), bf16),
            jax.ShapeDtypeStruct((parts * count, third), bf16),
            jax.ShapeDtypeStruct((width, cols), bf16),
        ],
        grid_spec=pltpu.PrefetchScalarGridSpec(
            num_scalar_prefetch=1,
            grid=(parts,),
            in_specs=[whole((count, width))] * parts
            + [whole((1, width)), whole((width, parts * cols))],
            out_specs=[
                pl.BlockSpec((count, width), lambda g, own_ref: (own_ref[0] ^ g, 0)),
                pl.BlockSpec((cols, count), lambda g, own_ref: (0, own_ref[0] ^ g)),
                pl.BlockSpec((count, third), lambda g, own_ref: (own_ref[0] ^ g, 0)),
                pl.BlockSpec((count, third), lambda g, own_ref: (own_ref[0] ^ g, 0)),
                whole((width, cols)),
            ],
            scratch_shapes=[pltpu.VMEM((count, width), f32), pltpu.VMEM((cols, width), bf16)],
        ),
        compiler_params=params(40),
        name="norm_qkv",
        cost_estimate=cost(7),
    )(own, *blocks, gain, w_qkv)


def mask_scores(scores, key_start, start_row, last_row, query_row, diagonal):
    key_col = key_start + iota(scores.shape, 0)
    valid = key_col >= start_row
    if diagonal:
        valid = (valid & (key_col <= last_row)) | (key_col == query_row)
    return jnp.where(valid, scores, masked_score)


def query_rows(info_ref, query_start, size):
    query_row = query_start + iota((1, size), 1)
    first_cut, last_cut, length = info_ref[0], info_ref[1], info_ref[2]
    start_row = jnp.where(
        query_row >= last_cut, last_cut, jnp.where(query_row >= first_cut, first_cut, 0)
    )
    last_row = jnp.minimum(query_row, length - 1)
    return query_row, start_row, last_row


def attend_kernel(block, info_ref, k_ref, q_ref, v_ref, o_ref, low_ref, log_ref, q_pad, s_buf):
    head = pl.program_id(0)
    qb = pl.program_id(1)
    q_pad[...] = jnp.zeros_like(q_pad)
    q_pad[pl.ds(pl.multiple_of(head * HEAD_DIM, HEAD_DIM), HEAD_DIM), :] = q_ref[...]
    query_row, start_row, last_row = query_rows(info_ref, qb * block, block)

    def score(j, diagonal):
        rows = pl.ds(pl.multiple_of(j * block, block), block)
        s = mm(k_ref[rows, :], q_pad[...])
        s = mask_scores(s, j * block, start_row, last_row, query_row, diagonal)
        s_buf[rows, :] = s
        return jnp.max(s, axis=0, keepdims=True)

    top = score(qb, True)
    top = lax.fori_loop(0, qb, lambda j, t: jnp.maximum(t, score(j, False)), top)

    def weigh(j, carry):
        total, out = carry
        rows = pl.ds(pl.multiple_of(j * block, block), block)
        p = jnp.exp(s_buf[rows, :] - top)
        total = total + jnp.sum(p, axis=0, keepdims=True)
        return total, out + mm(v_ref[:, rows], p.astype(bf16))

    zero = (jnp.zeros((1, block), f32), jnp.zeros((HEAD_DIM, block), f32))
    total, out = lax.fori_loop(0, qb + 1, weigh, zero)
    out = out / total
    o_ref[...] = out
    low_ref[...] = out.astype(bf16)
    log_ref[0] = top + jnp.log(total)


def attend(info, keys, qkv_t, block=512):
    row_len, group = keys.shape
    heads = group // HEAD_DIM
    return pl.pallas_call(
        functools.partial(attend_kernel, block),
        out_shape=[
            jax.ShapeDtypeStruct((group, row_len), f32),
            jax.ShapeDtypeStruct((group, row_len), bf16),
            jax.ShapeDtypeStruct((heads, 1, row_len), f32),
        ],
        grid=(heads, row_len // block),
        in_specs=[
            smem_spec(),
            pl.BlockSpec((row_len, group), lambda h, i: (0, 0)),
            pl.BlockSpec((HEAD_DIM, block), lambda h, i: (h, i)),
            pl.BlockSpec((HEAD_DIM, row_len), lambda h, i: (2 * heads + h, 0)),
        ],
        out_specs=[
            pl.BlockSpec((HEAD_DIM, block), lambda h, i: (h, i)),
            pl.BlockSpec((HEAD_DIM, block), lambda h, i: (h, i)),
            pl.BlockSpec((1, 1, block), lambda h, i: (h, 0, i)),
        ],
        scratch_shapes=[pltpu.VMEM((group, block), bf16), pltpu.VMEM((row_len, block), f32)],
        compiler_params=params(40),
        name="attend",
        cost_estimate=cost(21),
    )(info, keys, qkv_t, qkv_t)


def attend_back_kernel(
    block, info_ref, own_ref, k_ref, v_ref, q_ref, kt_ref, g0, g1, g2, g3, o_ref, log_ref,
    dq_ref, dk_ref, dv_ref, q_pad, g_pad, dk_acc, dv_acc,
):
    head = pl.program_id(0)
    qb = pl.program_id(1)
    blocks = pl.num_programs(1)
    rows_of_head = pl.ds(pl.multiple_of(head * HEAD_DIM, HEAD_DIM), HEAD_DIM)

    @pl.when(qb == 0)
    def clear():
        dk_acc[...] = jnp.zeros_like(dk_acc)
        dv_acc[...] = jnp.zeros_like(dv_acc)

    q = q_ref[...]
    q_pad[...] = jnp.zeros_like(q_pad)
    g_pad[...] = jnp.zeros_like(g_pad)
    q_pad[rows_of_head, :] = q
    for j, part in enumerate((g0, g1, g2, g3)):

        @pl.when((own_ref[0] ^ j) == qb)
        def take(part=part):
            g_pad[rows_of_head, :] = part[...]

    g = g_pad[rows_of_head, :]
    delta = jnp.sum(g.astype(f32) * o_ref[...], axis=0, keepdims=True)
    log_total = log_ref[0]
    query_row, start_row, last_row = query_rows(info_ref, qb * block, block)

    def one(j, dq, diagonal):
        rows = pl.ds(pl.multiple_of(j * block, block), block)
        s = mm(k_ref[rows, :], q_pad[...])
        s = mask_scores(s, j * block, start_row, last_row, query_row, diagonal)
        p = jnp.exp(s - log_total)
        dp = mm(v_ref[rows, :], g_pad[...])
        ds = (p * (dp - delta)).astype(bf16)
        dv_acc[:, rows] += mm(g, p.astype(bf16), NT)
        dk_acc[:, rows] += mm(q, ds, NT)
        return dq + mm(kt_ref[:, rows], ds)

    dq = one(qb, jnp.zeros((HEAD_DIM, block), f32), True)
    dq = lax.fori_loop(0, qb, lambda j, t: one(j, t, False), dq)
    dq_ref[...] = (0.125 * dq).astype(bf16)

    @pl.when(qb == blocks - 1)
    def finish():
        dk_ref[...] = dk_acc[...].astype(bf16)
        dv_ref[...] = dv_acc[...].astype(bf16)


def attend_back(info, own, keys, values, qkv_t, grads, out, logs, block=512):
    row_len, group = keys.shape
    heads = group // HEAD_DIM
    whole = pl.BlockSpec((row_len, group), lambda h, i: (0, 0))
    piece = pl.BlockSpec((HEAD_DIM, block), lambda h, i: (h, 0))
    tile = pl.BlockSpec((HEAD_DIM, block), lambda h, i: (h, i))
    full = pl.BlockSpec((HEAD_DIM, row_len), lambda h, i: (h, 0))
    return pl.pallas_call(
        functools.partial(attend_back_kernel, block),
        out_shape=[jax.ShapeDtypeStruct((group, row_len), bf16)] * 3,
        grid=(heads, row_len // block),
        in_specs=[
            smem_spec(),
            smem_spec(),
            whole,
            whole,
            tile,
            pl.BlockSpec((HEAD_DIM, row_len), lambda h, i: (heads + h, 0)),
            piece,
            piece,
            piece,
            piece,
            tile,
            pl.BlockSpec((1, 1, block), lambda h, i: (h, 0, i)),
        ],
        out_specs=[tile, full, full],
        scratch_shapes=[
            pltpu.VMEM((group, block), bf16),
            pltpu.VMEM((group, block), bf16),
            pltpu.VMEM((HEAD_DIM, row_len), f32),
            pltpu.VMEM((HEAD_DIM, row_len), f32),
        ],
        compiler_params=params(40),
        name="attend_back",
        cost_estimate=cost(30),
    )(info, own, keys, values, qkv_t, qkv_t, *grads, out, logs)


def gates_of(normed, router, route_rows):
    logits = mm(router, normed, NT, precise)
    expert_row = iota(logits.shape, 0)
    picked = [
        jnp.sum(jnp.where(expert_row == row, logits, 0.0), axis=0, keepdims=True)
        for row in route_rows
    ]
    top = jnp.maximum(picked[0], picked[1])
    raw = [jnp.exp(p - top) for p in picked]
    return [r / (raw[0] + raw[1]) for r in raw]


def dispatch_kernel(
    own_ref, t0, t1, t2, t3, x_ref, w_ref, gain_ref, router_ref, routes_ref, hot_ref,
    residual_ref, gates_ref, slot_gates_ref, *sends,
):
    residual = x_ref[...].astype(f32)
    group = t0.shape[0]
    for j, part in enumerate((t0, t1, t2, t3)):
        rows = pl.ds(pl.multiple_of((own_ref[0] ^ j) * group, group), group)
        residual = residual + mm(part[...], w_ref[rows, :], TN)
    residual_ref[...] = residual
    scale = lax.rsqrt(jnp.mean(residual * residual, axis=1, keepdims=True) + norm_eps)
    normed = residual * scale * gain_ref[...]
    capacity = sends[0].shape[0]
    one_hot = hot_ref[...]
    rows = mm(one_hot, normed.astype(bf16)).astype(bf16)
    for e, send in enumerate(sends):
        send[...] = rows[e * capacity : (e + 1) * capacity, :]
    route_rows = [routes_ref[k : k + 1, :] for k in range(2)]
    gates = gates_of(normed, router_ref[...], route_rows)
    gates_ref[0:1, :] = gates[0]
    gates_ref[1:2, :] = gates[1]
    experts = router_ref.shape[0]
    expert_row = iota((experts, x_ref.shape[0]), 0) ^ own_ref[1]
    table = jnp.where(expert_row == route_rows[0], gates[0], 0.0) + jnp.where(
        expert_row == route_rows[1], gates[1], 0.0
    )
    spread = sum(mm(piece, one_hot, NT) for piece in split_three(table))
    own = iota(spread.shape, 1) // capacity == iota(spread.shape, 0)
    slot_gates_ref[...] = jnp.sum(jnp.where(own, spread, 0.0), axis=0, keepdims=True)


def make_dispatch(own, parts, x, w_out, gain, router_t, routes_t, hot, capacity):
    count, width = x.shape
    slots = hot.shape[0]
    experts = slots // capacity
    shapes = [
        jax.ShapeDtypeStruct((count, width), f32),
        jax.ShapeDtypeStruct((2, count), f32),
        jax.ShapeDtypeStruct((1, slots), f32),
    ]
    shapes += [jax.ShapeDtypeStruct((capacity, width), bf16)] * experts
    results = pl.pallas_call(
        dispatch_kernel,
        out_shape=shapes,
        in_specs=[smem_spec()] + [vmem_spec()] * 10,
        out_specs=[vmem_spec()] * len(shapes),
        compiler_params=params(48),
        name="project_dispatch",
        cost_estimate=cost(8),
    )(own, *parts, x, w_out, gain, router_t, routes_t, hot)
    return results[0], results[1], results[2], results[3:]


def column_of(row):
    return jnp.broadcast_to(row, (128, row.shape[1])).T[:, 0:1]


def row_of(column):
    return jnp.broadcast_to(column, (column.shape[0], 128)).T[0:1, :]


GELU_SCALE = 0.7978845608028654
GELU_CUBE = 0.044715


def expert_kernel(sources, block, *refs):
    xs, dys = refs[:sources], refs[sources : 2 * sources]
    ups, downs = refs[2 * sources : 2 * sources + 4], refs[2 * sources + 4 : 2 * sources + 8]
    refs = refs[2 * sources + 8 :]
    outs, slots = refs[:sources], refs[sources : 2 * sources]
    dgate_ref, act_ref, dpre_ref, x_buf, dy_buf, up_buf, down_buf, out_acc, slot_acc, sems = refs[
        2 * sources :
    ]
    capacity = xs[0].shape[0]
    step = pl.program_id(0)
    parts = len(ups)

    def copies(j):
        return (
            pltpu.make_async_copy(ups[j], up_buf.at[j % 2], sems.at[0, j % 2]),
            pltpu.make_async_copy(downs[j], down_buf.at[j % 2], sems.at[1, j % 2]),
        )

    @pl.when(step == 0)
    def first():
        for copy in copies(0):
            copy.start()
        for n in range(sources):
            x_buf[n * capacity : (n + 1) * capacity, :] = xs[n][...]
            dy_buf[n * capacity : (n + 1) * capacity, :] = dys[n][...]
        out_acc[...] = jnp.zeros_like(out_acc)
        slot_acc[...] = jnp.zeros_like(slot_acc)

    for j in range(parts):

        @pl.when(step == j)
        def arrive(j=j):
            if j + 1 < parts:
                for copy in copies(j + 1):
                    copy.start()
            for copy in copies(j):
                copy.wait()

    which = lax.rem(step, 2)

    @pl.loop(0, x_buf.shape[0] // block)
    def rows_of(r):
        rows = pl.ds(pl.multiple_of(r * block, block), block)
        up, down = up_buf[which], down_buf[which]
        pre = mm(x_buf[rows, :], up)
        square = pre * pre
        tanh = jnp.tanh(GELU_SCALE * (pre * (1.0 + GELU_CUBE * square)))
        half = 0.5 * (1.0 + tanh)
        act = (pre * half).astype(bf16)
        act_ref[0, rows, :] = act
        out_acc[rows, :] += mm(act, down)
        slope = half + (0.5 * GELU_SCALE) * pre * (1.0 - tanh * tanh) * (
            1.0 + (3.0 * GELU_CUBE) * square
        )
        dpre = (mm(dy_buf[rows, :], down, NT) * slope).astype(bf16)
        dpre_ref[0, rows, :] = dpre
        slot_acc[rows, :] += mm(dpre, up, NT)

    @pl.when(step == parts - 1)
    def last():
        out = out_acc[...].astype(bf16)
        slot = slot_acc[...].astype(bf16)
        dgate = row_of(
            jnp.sum(dy_buf[...].astype(f32) * out.astype(f32), axis=1, keepdims=True)
        )
        dgate_ref[...] = dgate
        for n in range(sources):
            outs[n][...] = out[n * capacity : (n + 1) * capacity, :]
            slots[n][...] = slot[n * capacity : (n + 1) * capacity, :]


def row_block(rows, most=256):
    return max(b for b in range(16, most + 1, 16) if rows % b == 0)


def run_experts(xs, dys, ups, downs):
    sources = len(xs)
    capacity, width = xs[0].shape
    rows = sources * capacity
    units = ups[0].shape[1]
    parts = len(ups)

    def whole(shape):
        return pl.BlockSpec(shape, lambda g: (0, 0))

    hbm = pl.BlockSpec(memory_space=pl.ANY)
    piece = whole((capacity, width))
    shape = jax.ShapeDtypeStruct((capacity, width), bf16)
    kept = jax.ShapeDtypeStruct((parts, rows, units), bf16)
    kept_spec = pl.BlockSpec((1, rows, units), lambda g: (g, 0, 0))
    results = pl.pallas_call(
        functools.partial(expert_kernel, sources, row_block(rows)),
        out_shape=[shape] * (2 * sources) + [jax.ShapeDtypeStruct((1, rows), f32), kept, kept],
        grid=(parts,),
        in_specs=[piece] * (2 * sources) + [hbm] * (2 * parts),
        out_specs=[piece] * (2 * sources) + [whole((1, rows)), kept_spec, kept_spec],
        scratch_shapes=[
            pltpu.VMEM((rows, width), bf16),
            pltpu.VMEM((rows, width), bf16),
            pltpu.VMEM((2, width, units), bf16),
            pltpu.VMEM((2, units, width), bf16),
            pltpu.VMEM((rows, width), f32),
            pltpu.VMEM((rows, width), f32),
            pltpu.SemaphoreType.DMA((2, 2)),
        ],
        compiler_params=params(40),
        name="experts",
        cost_estimate=cost(16),
    )(*xs, *dys, *ups, *downs)
    return (
        results[:sources], results[sources : 2 * sources], results[2 * sources],
        results[2 * sources + 1], results[2 * sources + 2],
    )


def weight_kernel(experts, groups, gate_ref, *refs):
    xs, dys = refs[:experts], refs[experts : 2 * experts]
    acts, dpres = refs[2 * experts : 2 * experts + groups], refs[2 * experts + groups : 2 * experts + 2 * groups]
    refs = refs[2 * experts + 2 * groups :]
    ups, downs, (x_turn, dy_turn) = refs[:4], refs[4:8], refs[8:]
    step = pl.program_id(0)
    capacity = xs[0].shape[0]

    @pl.when(step == 0)
    def turn():
        for n in range(experts):
            cols = slice(n * capacity, (n + 1) * capacity)
            gate = gate_ref[0:1, cols]
            x_turn[:, cols] = (xs[n][...].astype(f32).T * gate).astype(bf16)
            dy_turn[:, cols] = (dys[n][...].astype(f32).T * gate).astype(bf16)

    act = jnp.concatenate([a[0] for a in acts], axis=0)
    dpre = jnp.concatenate([d[0] for d in dpres], axis=0)
    up = mm(x_turn[...], dpre)
    down = mm(dy_turn[...], act).T
    for j in range(4):

        @pl.when(step == j)
        def keep(j=j):
            ups[j][...] = up.astype(ups[j].dtype)
            downs[j][...] = down.astype(downs[j].dtype)


def weight_grads(gates, xs, dys, acts, dpres):
    experts, groups = len(xs), len(acts)
    capacity, width = xs[0].shape
    parts, rows, units = acts[0].shape

    def whole(shape):
        return pl.BlockSpec(shape, lambda g: (0, 0), pipeline_mode=pl.Buffered(1))

    kept = pl.BlockSpec((1, rows, units), lambda g: (g, 0, 0))
    types = (f32, bf16, f32, bf16)
    results = pl.pallas_call(
        functools.partial(weight_kernel, experts, groups),
        out_shape=[jax.ShapeDtypeStruct((width, units), t) for t in types]
        + [jax.ShapeDtypeStruct((units, width), t) for t in types],
        grid=(parts,),
        in_specs=[whole((1, experts * capacity))] + [whole((capacity, width))] * (2 * experts)
        + [kept] * (2 * groups),
        out_specs=[whole((width, units))] * parts + [whole((units, width))] * parts,
        scratch_shapes=[pltpu.VMEM((width, experts * capacity), bf16)] * 2,
        compiler_params=params(56),
        name="expert_weight_grads",
        cost_estimate=cost(30),
    )(gates, *xs, *dys, *acts, *dpres)
    return results[:parts], results[parts:]


def combine_back_kernel(
    own_ref, dgate_ref, hot_ref, pick0, pick1, residual_ref, dy_ref, gates_ref, routes_ref,
    router_ref, gain_ref, w_ref, t0, t1, t2, t3, *refs,
):
    experts = router_ref.shape[0]
    slots, (dres_ref, datt_ref, gout_ref, small_ref, slot_buf) = refs[:experts], refs[experts:]
    capacity = slots[0].shape[0]
    for n, slot in enumerate(slots):
        slot_buf[n * capacity : (n + 1) * capacity, :] = slot[...]
    residual = residual_ref[...]
    count = residual.shape[0]
    scale = lax.rsqrt(jnp.mean(residual * residual, axis=1, keepdims=True) + norm_eps)
    unit = residual * scale
    gain = gain_ref[...]
    row = dgate_ref[...]
    shape = (experts, row.shape[1])
    spread = jnp.where(iota(shape, 1) // capacity == iota(shape, 0), row, 0.0)
    table = sum(mm(piece, hot_ref[...]) for piece in split_three(spread))
    place_row = iota((experts, count), 0) ^ own_ref[1]
    routes = [routes_ref[k : k + 1, :] for k in range(2)]
    gates = [gates_ref[k : k + 1, :] for k in range(2)]
    dgates = [
        jnp.sum(jnp.where(place_row == r, table, 0.0), axis=0, keepdims=True) for r in routes
    ]
    mean = gates[0] * dgates[0] + gates[1] * dgates[1]
    expert_row = iota((experts, count), 0)
    dlogit = sum(
        jnp.where(expert_row == r, g * (d - mean), 0.0) for r, g, d in zip(routes, gates, dgates)
    )
    small_ref[...] = jnp.zeros_like(small_ref)
    small_ref[0:experts, :] = mm(dlogit, unit * gain, precision=precise)
    slot_rows = slot_buf[...]
    dnormed = mm(dlogit, router_ref[...], TN, precise)
    for gate, pick in zip(gates, (pick0, pick1)):
        dnormed = dnormed + column_of(gate) * mm(pick[...], slot_rows)
    small_ref[experts : experts + 1, :] = jnp.sum(dnormed * unit, axis=0, keepdims=True)
    scaled = dnormed * gain
    dres = dy_ref[...].astype(f32) + scale * (
        scaled - unit * jnp.mean(scaled * unit, axis=1, keepdims=True)
    )
    dres_ref[...] = dres
    branch = dres.astype(bf16)
    datt_ref[...] = mm(w_ref[...], branch, NT).astype(bf16)
    group = t0.shape[0]
    for j, part in enumerate((t0, t1, t2, t3)):
        rows = pl.ds(pl.multiple_of((own_ref[0] ^ j) * group, group), group)
        gout_ref[rows, :] = mm(part[...], branch)


def combine_back(own, slots, dgate, hot, picks, residual, dy, gates, routes_t, router_t, gain, w_out, parts):
    count, width = residual.shape
    experts = router_t.shape[0]
    shapes = [
        jax.ShapeDtypeStruct((count, width), f32),
        jax.ShapeDtypeStruct((width, count), bf16),
        jax.ShapeDtypeStruct((width, width), f32),
        jax.ShapeDtypeStruct((experts + 8, width), f32),
    ]
    return pl.pallas_call(
        combine_back_kernel,
        out_shape=shapes,
        in_specs=[smem_spec()] + [vmem_spec()] * (15 + experts),
        out_specs=[vmem_spec()] * len(shapes),
        scratch_shapes=[pltpu.VMEM((hot.shape[0], width), bf16)],
        compiler_params=params(56),
        name="combine_back",
        cost_estimate=cost(12),
    )(own, dgate, hot, *picks, residual, dy, gates, routes_t, router_t, gain, w_out, *parts, *slots)


def combine_kernel(pick0, pick1, residual_ref, gates_ref, *refs):
    outs, (y_ref, out_buf) = refs[:-2], refs[-2:]
    capacity = outs[0].shape[0]
    for n, out in enumerate(outs):
        out_buf[n * capacity : (n + 1) * capacity, :] = out[...]
    rows = out_buf[...]
    total = None
    for k, pick in enumerate((pick0, pick1)):
        term = column_of(gates_ref[k : k + 1, :]) * mm(pick[...], rows)
        total = term if total is None else total + term
    y_ref[...] = (residual_ref[...] + total).astype(bf16)


def combine(outs, picks, residual, gates):
    capacity, width = outs[0].shape
    return pl.pallas_call(
        combine_kernel,
        out_shape=jax.ShapeDtypeStruct(residual.shape, bf16),
        in_specs=[vmem_spec()] * (4 + len(outs)),
        out_specs=vmem_spec(),
        scratch_shapes=[pltpu.VMEM((len(outs) * capacity, width), bf16)],
        compiler_params=params(48),
        name="combine",
        cost_estimate=cost(5),
    )(*picks, residual, gates, *outs)


def lay_out_kernel(sizes, qkv_ref, out_ref, grad_qkv_ref, gain_ref, grad_out_ref, small_ref):
    exps, hids, rows, out_rows = sizes
    width = grad_out_ref.shape[1]
    bits = exps.bit_length() - 1

    def at(h, e):
        return (h & 1, h >> 1) + tuple((e >> b) & 1 for b in range(bits))

    third = exps * rows // 3
    gain = 0.0
    small_ref[...] = jnp.zeros_like(small_ref)
    for h in range(hids):
        block = jnp.concatenate([qkv_ref[at(h, e)][:rows] for e in range(exps)], axis=0)
        turned = block.astype(f32).T
        for t in range(3):
            start = t * width + h * third
            grad_qkv_ref[:, start : start + third] = turned[:, t * third : (t + 1) * third]
        gain = gain + qkv_ref[at(h, 0)][rows : rows + 1].astype(f32)
        for e in range(exps):
            n = h * exps + e
            piece = out_ref[at(h, e)].astype(f32)
            grad_out_ref[n * out_rows : (n + 1) * out_rows, :] = piece[:out_rows]
            if n < small_ref.shape[0]:
                small_ref[n : n + 1, :] = piece[out_rows : out_rows + 1]
    gain_ref[...] = gain


def lay_out(qkv, out, rows, out_rows, small_rows):
    hids, exps = 4, 1 << (qkv.ndim - 4)
    width = qkv.shape[-1]
    return pl.pallas_call(
        functools.partial(lay_out_kernel, (exps, hids, rows, out_rows)),
        out_shape=[
            jax.ShapeDtypeStruct((width, 3 * width), f32),
            jax.ShapeDtypeStruct((1, width), f32),
            jax.ShapeDtypeStruct((width, width), f32),
            jax.ShapeDtypeStruct((small_rows, width), f32),
        ],
        in_specs=[vmem_spec()] * 2,
        out_specs=[vmem_spec()] * 4,
        compiler_params=params(48),
        name="lay_out_sums",
        cost_estimate=cost(6),
    )(qkv, out)


def adam_update(weight, gradient, first_moment, second_moment, live_mask):
    first_next = beta_one * first_moment + (1.0 - beta_one) * gradient
    second_next = beta_two * second_moment + (1.0 - beta_two) * gradient * gradient
    first_hat = first_next / (1.0 - beta_one**adam_steps)
    second_hat = second_next / (1.0 - beta_two**adam_steps)
    weight_next = weight - learn_rate * first_hat / (jnp.sqrt(second_hat) + adam_eps)
    return (
        jnp.where(live_mask, weight_next, weight),
        jnp.where(live_mask, first_next, first_moment),
        jnp.where(live_mask, second_next, second_moment),
    )


def tie(value, other):
    return lax.optimization_barrier((value, other))[0]


def exchange(value, axis):
    return lax.all_to_all(value, axis, split_axis=0, concat_axis=0, tiled=True)


def send_all(pieces, axis):
    far_first = sorted(range(1, len(pieces)), reverse=True)
    order = [d for d in far_first if d * 2 >= len(pieces)][::-1]
    order += [d for d in far_first if d * 2 < len(pieces)]
    moved = {d: swap(pieces[d], axis, d) for d in order}
    return [pieces[0]] + [moved[d] for d in range(1, len(pieces))]


def reorder(value, index):
    count = value.shape[0]
    match = (jnp.arange(count) ^ index)[:, None] == jnp.arange(count)[None, :]
    return jnp.sum(jnp.where(match[:, :, None], value[None], 0.0), axis=1)


def split_sum(value, axis, distance):
    pairs = value.reshape((value.shape[0] // 2, 2) + value.shape[1:])
    low = (lax.axis_index(axis) & distance) == 0
    keep = jnp.where(low, pairs[:, 0], pairs[:, 1])
    give = jnp.where(low, pairs[:, 1], pairs[:, 0]).astype(bf16)
    return keep + swap(give, axis, distance).astype(f32)


def swap_stack(value, axis, distance):
    other = swap(value, axis, distance)
    low = (lax.axis_index(axis) & distance) == 0
    return jnp.stack([jnp.where(low, value, other), jnp.where(low, other, value)])


def gather_all(value, distances):
    for d in reversed(distances):
        value = swap_stack(value, "exp", d)
    for d in (2, 1):
        value = swap_stack(value, "hid", d)
    return value


def body(
    tokens, cotangent, routes, segments, lengths, gain_attn, gain_moe, w_qkv, w_out, router_w,
    router_first, router_second, up_w, down_w, up_first, up_second, down_first, down_second,
):
    exp_count = lax.axis_size("exp")
    hid_count = lax.axis_size("hid")
    hid = lax.axis_index("hid")
    exp_index = lax.axis_index("exp")
    own = jnp.stack([hid, exp_index]).astype(jnp.int32)
    x_own = tokens[0]
    dy = cotangent[0]
    count, width = x_own.shape
    experts = router_w.shape[1]
    frozen_count = experts // 2
    capacity = max(2, 3 * count // experts)
    group = width // hid_count
    is_new = exp_index >= frozen_count

    x_far = swap(x_own, "hid", 2)
    x_near = swap(x_own, "hid", 1)
    routes_t = routes[0].T
    hot, picks, dy_sends = make_tables(own, routes_t, dy, experts, capacity)
    seg_row = segments[0]
    info = jnp.stack(
        [
            jnp.sum((seg_row < 1).astype(jnp.int32)),
            jnp.sum((seg_row < 2).astype(jnp.int32)),
            lengths[0],
        ]
    )
    up_low = up_w[0].astype(bf16)
    down_low = down_w[0].astype(bf16)
    router_t = router_w.T
    x_far, (info, dy_sends, up_low, down_low, router_t, routes_t) = lax.optimization_barrier(
        (x_far, (info, dy_sends, up_low, down_low, router_t, routes_t))
    )
    x_last = swap(x_far, "hid", 1)
    blocks = (x_own, x_near, x_far, x_last)
    dy_rows = send_all(dy_sends, "exp")

    up_far, down_far = swap(up_low, "hid", 2), swap(down_low, "hid", 2)
    up_near, down_near = swap(up_low, "hid", 1), swap(down_low, "hid", 1)
    up_last, down_last = swap(up_far, "hid", 1), swap(down_far, "hid", 1)
    ups = (up_low, up_near, up_far, up_last)
    downs = (down_low, down_near, down_far, down_last)

    a_one, qkv_t, keys, values, w_heads = project_qkv(own, blocks, gain_attn[None], w_qkv)
    out_heads, out_low, logs = attend(info, keys, qkv_t)

    def piece_of(value, j):
        return lax.dynamic_slice_in_dim(value, (hid ^ j) * count, count, 1)

    att_parts = [piece_of(out_low, 0)] + [
        swap(piece_of(out_low, j), "hid", j) for j in range(1, hid_count)
    ]
    att_parts, dy_rows = lax.optimization_barrier((att_parts, dy_rows))

    residual, gates, slot_gates, sends = make_dispatch(
        own, att_parts, x_own, w_out, gain_moe[None], router_t, routes_t, hot, capacity
    )
    x_rows = send_all(sends, "exp")
    gate_rows = exchange(reorder(slot_gates.reshape(experts, capacity), exp_index), "exp")
    gate_rows = reorder(gate_rows, exp_index).reshape(1, experts * capacity)

    in_group = exp_count // 4
    groups = [range(g * in_group, (g + 1) * in_group) for g in (0, 2, 1, 3)]
    results = {}
    for members in groups:
        outs, slots, dgate, act, dpre = run_experts(
            [x_rows[d] for d in members], [dy_rows[d] for d in members], ups, downs
        )
        results[members[0] // in_group] = (outs, slots, dgate, act, dpre)
    results = [results[g] for g in range(4)]
    slot_back = send_all([s for r in results for s in r[1]], "exp")
    dgates = jnp.concatenate([r[2].reshape(in_group, capacity) for r in results], axis=0)
    dgates = reorder(exchange(reorder(dgates, exp_index), "exp"), exp_index)
    dgates = dgates.reshape(1, experts * capacity)

    part_ups, part_downs = weight_grads(
        gate_rows, x_rows, dy_rows, [r[3] for r in results], [r[4] for r in results]
    )
    near_up, near_down = swap(part_ups[1], "hid", 1), swap(part_downs[1], "hid", 1)
    last_up, last_down = swap(part_ups[3], "hid", 1), swap(part_downs[3], "hid", 1)
    far_up = (part_ups[2] + last_up.astype(f32)).astype(bf16)
    far_down = (part_downs[2] + last_down.astype(f32)).astype(bf16)
    far_up, far_down = swap(far_up, "hid", 2), swap(far_down, "hid", 2)
    grad_up = part_ups[0] + near_up.astype(f32) + far_up.astype(f32)
    grad_down = part_downs[0] + near_down.astype(f32) + far_down.astype(f32)
    grad_up = jnp.where(is_new, grad_up, 0.0)
    grad_down = jnp.where(is_new, grad_down, 0.0)

    dres, datt, gout, small = combine_back(
        own, slot_back, dgates, hot, picks, residual, dy, gates, routes_t, router_t,
        gain_moe[None], w_out, att_parts,
    )

    def heads_of(value, j):
        return lax.dynamic_slice_in_dim(value, (hid ^ j) * group, group, 0)

    datt_parts = [heads_of(datt, 0)] + [
        swap(heads_of(datt, j), "hid", j) for j in range(1, hid_count)
    ]

    out_back = send_all([o for r in results for o in r[0]], "exp")
    out_tokens = combine(out_back, picks, residual, gates)

    dqkv_t = jnp.concatenate(
        attend_back(info, own, keys, values, qkv_t, datt_parts, out_heads, logs), axis=0
    )
    grad_t = mm(dqkv_t, a_one)
    dnormed = mm(dqkv_t, w_heads, ((0,), (1,)))

    def rows_of(j):
        return lax.dynamic_slice_in_dim(dnormed, (hid ^ j) * count, count, 0)

    near = swap(rows_of(1).astype(bf16), "hid", 1)
    last = swap(rows_of(3).astype(bf16), "hid", 1)
    far = swap((rows_of(2) + last.astype(f32)).astype(bf16), "hid", 2)
    dnormed_own = rows_of(0) + near.astype(f32) + far.astype(f32)
    x = x_own.astype(f32)
    scale = lax.rsqrt(jnp.mean(x * x, axis=-1, keepdims=True) + norm_eps)
    unit = x * scale
    scaled = dnormed_own * gain_attn
    grad_tokens = (
        dres + scale * (scaled - unit * jnp.mean(scaled * unit, axis=-1, keepdims=True))
    ).astype(bf16)
    ggain_part = jnp.sum(dnormed * a_one.astype(f32), axis=0) / gain_attn

    rows = 3 * group // exp_count
    tail = -(rows + 1) % 8 + 1
    pad = jnp.broadcast_to(ggain_part, (exp_count, tail, width))
    piece = jnp.concatenate([grad_t.reshape(exp_count, rows, width), pad], axis=1)
    distances = [1 << b for b in range(exp_count.bit_length() - 1)]
    for d in distances:
        piece = split_sum(piece, "exp", d)
    whole = gather_all(piece[0].astype(bf16), distances)

    devices = exp_count * hid_count
    out_rows = width // devices
    extra = -(out_rows + 1) % 8 + 1
    small = jnp.pad(small[:devices], ((0, max(0, devices - small.shape[0])), (0, 0)))
    part = jnp.concatenate(
        [
            gout.reshape(devices, out_rows, width),
            small[:, None],
            jnp.zeros((devices, extra - 1, width), f32),
        ],
        axis=1,
    ).reshape(hid_count, exp_count * (out_rows + extra), width)
    for d in (1, 2):
        part = split_sum(part, "hid", d)
    part = part.reshape(exp_count, out_rows + extra, width)
    for d in distances:
        part = split_sum(part, "exp", d)
    out_whole = gather_all(part[0].astype(bf16), distances)

    grad_qkv, grad_gain_attn, grad_out_proj, small = lay_out(
        whole, out_whole, rows, out_rows, (experts + 8) // 8 * 8
    )
    grad_gain_attn = grad_gain_attn[0]
    grad_gain_moe = small[experts]
    live_columns = (jnp.arange(experts, dtype=jnp.int32) >= frozen_count)[None, :]
    grad_router = jnp.where(live_columns, small[:experts].T, 0.0)
    router_new, router_first_next, router_second_next = adam_update(
        router_w[:, frozen_count:], grad_router[:, frozen_count:], router_first, router_second, True
    )
    router_next = jnp.concatenate([router_w[:, :frozen_count], router_new], axis=1)
    up_next, up_first_next, up_second_next = adam_update(
        up_w[0], grad_up, up_first[0], up_second[0], is_new
    )
    down_next, down_first_next, down_second_next = adam_update(
        down_w[0], grad_down, down_first[0], down_second[0], is_new
    )
    return (
        out_tokens[None],
        grad_tokens[None],
        grad_qkv,
        grad_out_proj,
        grad_gain_attn,
        grad_gain_moe,
        grad_router,
        router_next,
        router_first_next,
        router_second_next,
        grad_up[None],
        grad_down[None],
        up_next[None],
        down_next[None],
        up_first_next[None],
        up_second_next[None],
        down_first_next[None],
        down_second_next[None],
    )


def solution(mesh):
    tok = P("exp", "hid", None)
    up = P("exp", None, "hid")
    return jax.shard_map(
        body,
        mesh=mesh,
        in_specs=(tok, tok, tok, P("exp", None), P("exp")) + (P(),) * 7
        + (up, tok, up, up, tok, tok),
        out_specs=(tok, tok) + (P(),) * 8 + (up, tok, up, tok, up, up, tok, tok),
        check_vma=False,
    )
```

```python
import functools

import jax
import jax.numpy as jnp
from jax import lax
from jax.experimental import pallas as pl
from jax.experimental.pallas import tpu as pltpu
from jax.sharding import PartitionSpec as P

HEADS = 12
HEAD_DIM = 64

precise = lax.Precision.HIGHEST
norm_eps = 1e-06
beta_one = 0.9
beta_two = 0.999
learn_rate = 0.01
adam_eps = 1e-08
adam_steps = 10.0
masked_score = -1e30

bf16 = jnp.bfloat16
f32 = jnp.float32
MIB = 1 << 20
COST_SCALE = 0.25


def mm(left, right, contract=((1,), (0,)), precision=None):
    return lax.dot_general(
        left, right, (contract, ((), ())), preferred_element_type=f32, precision=precision
    )


NT = ((1,), (1,))
TN = ((0,), (0,))


def swap(value, axis, distance):
    count = lax.axis_size(axis)
    return lax.ppermute(value, axis, [(i, i ^ distance) for i in range(count)])


def iota(shape, dim):
    return lax.broadcasted_iota(jnp.int32, shape, dim)


def split_three(value):
    high = value.astype(bf16)
    rest = value - high.astype(f32)
    mid = rest.astype(bf16)
    low = (rest - mid.astype(f32)).astype(bf16)
    return high, mid, low


EXTRA = 8


def three_rows(row):
    high, mid, low = (piece.astype(f32) for piece in split_three(row))
    return jnp.concatenate([high, mid, low, jnp.zeros((EXTRA - 3, row.shape[1]), f32)], axis=0).astype(bf16)


def vmem_spec():
    return pl.BlockSpec(memory_space=pltpu.VMEM)


def smem_spec():
    return pl.BlockSpec(memory_space=pltpu.SMEM)


def params(mib):
    return pltpu.CompilerParams(vmem_limit_bytes=mib * MIB)


def cost(micros):
    micros = micros * COST_SCALE
    return pl.CostEstimate(
        flops=int(micros * 1.1e9), bytes_accessed=int(micros * 3e6), transcendentals=0
    )


def halves_of(capacity):
    first = (capacity // 2 + 15) // 16 * 16
    return ((0, first), (first, capacity - first))


def tables_kernel(routes_ref, dy_ref, hot_a, hot_b, *outs):
    picks, send_ref = outs[:4], outs[4]
    experts, capacity, _ = send_ref.shape
    count = routes_ref.shape[1]
    expert_row = iota((experts, count), 0)
    route_rows = [routes_ref[k : k + 1, :] for k in range(2)]
    hits = [expert_row == row for row in route_rows]
    hit = hits[0] | hits[1]
    hit_low = jnp.where(hit, 1.0, 0.0).astype(bf16)
    upper = jnp.where(iota((count, count), 0) < iota((count, count), 1), 1.0, 0.0).astype(bf16)
    slot = mm(hit_low, upper)
    slot = jnp.where(hit & (slot < capacity), slot, -1.0)
    index_rows = []
    for (start, size), hot in zip(halves_of(capacity), (hot_a, hot_b)):
        row_id = iota((size, count), 0).astype(f32) + float(start)
        for e in range(experts):
            hot[e * size : (e + 1) * size, :] = jnp.where(
                row_id == slot[e : e + 1, :], 1.0, 0.0
            ).astype(bf16)
        rows = mm(hot[...], dy_ref[...]).astype(bf16)
        for e in range(experts):
            send_ref[e, start : start + size, :] = rows[e * size : (e + 1) * size, :]
        for k in range(2):
            own_slot = jnp.sum(jnp.where(hits[k], slot, 0.0), axis=0, keepdims=True)
            inside = (own_slot >= start) & (own_slot < start + size)
            place = route_rows[k].astype(f32) * size + own_slot - start
            index_rows.append(jnp.where(inside, place, -1.0))
    index_cols = jnp.concatenate(index_rows * 2, axis=0).T
    for n, pick in enumerate(picks):
        lane = iota(pick.shape, 1).astype(f32)
        pick[...] = jnp.where(lane == index_cols[:, n : n + 1], 1.0, 0.0).astype(bf16)


def make_tables(routes_t, dy, experts, capacity):
    count, width = dy.shape
    sizes = [experts * size for _, size in halves_of(capacity)]
    shapes = [jax.ShapeDtypeStruct((size, count), bf16) for size in sizes]
    shapes += [jax.ShapeDtypeStruct((count, size), bf16) for size in sizes for _ in range(2)]
    shapes += [jax.ShapeDtypeStruct((experts, capacity, width), bf16)]
    results = pl.pallas_call(
        tables_kernel,
        out_shape=shapes,
        in_specs=[vmem_spec()] * 2,
        out_specs=[vmem_spec()] * len(shapes),
        compiler_params=params(60),
        name="slot_tables",
        cost_estimate=cost(5),
    )(routes_t, dy)
    return results[0:2], results[2:6], results[6]


def qkv_kernel(
    own_ref, x0, x1, x2, x3, gain_ref, w_ref, a_ref, qkv_ref, k_ref, v_ref, w_buf, x_buf, heads_ref
):
    step = pl.program_id(0)
    width, cols = heads_ref.shape
    third = cols // 3

    @pl.when(step == 0)
    def turn():
        for h in range(width // third):

            @pl.when(own_ref[0] == h)
            def pick(h=h):
                for t in range(3):
                    start = t * width + h * third
                    heads_ref[:, t * third : (t + 1) * third] = w_ref[:, start : start + third]

        w_buf[...] = heads_ref[...].T

    for j, block in enumerate((x0, x1, x2, x3)):

        @pl.when(step == j)
        def take(block=block):
            x_buf[...] = block[...].astype(f32)

    x = x_buf[...]
    scale = lax.rsqrt(jnp.mean(x * x, axis=1, keepdims=True) + norm_eps)
    a = (x * scale * gain_ref[...]).astype(bf16)
    a_ref[...] = a
    qkv_t = mm(w_buf[...], a, NT).astype(bf16)
    qkv_ref[0:third, :] = qkv_t[0:third, :] * jnp.asarray(0.125, bf16)
    qkv_ref[third:, :] = qkv_t[third:, :]
    both = mm(a, heads_ref[:, third:]).astype(bf16)
    k_ref[...] = both[:, :third]
    v_ref[...] = both[:, third:]


def project_qkv(own, blocks, gain, w_qkv):
    count, width = blocks[0].shape
    parts = len(blocks)
    cols = w_qkv.shape[1] // parts
    third = cols // 3

    def whole(shape):
        return pl.BlockSpec(shape, lambda g, own_ref: (0, 0), pipeline_mode=pl.Buffered(1))

    return pl.pallas_call(
        qkv_kernel,
        out_shape=[
            jax.ShapeDtypeStruct((parts * count, width), bf16),
            jax.ShapeDtypeStruct((cols, parts * count), bf16),
            jax.ShapeDtypeStruct((parts * count, third), bf16),
            jax.ShapeDtypeStruct((parts * count, third), bf16),
            jax.ShapeDtypeStruct((cols, width), bf16),
        ],
        grid_spec=pltpu.PrefetchScalarGridSpec(
            num_scalar_prefetch=1,
            grid=(parts,),
            in_specs=[whole((count, width))] * parts
            + [whole((1, width)), whole((width, parts * cols))],
            out_specs=[
                pl.BlockSpec((count, width), lambda g, own_ref: (own_ref[0] ^ g, 0)),
                pl.BlockSpec((cols, count), lambda g, own_ref: (0, own_ref[0] ^ g)),
                pl.BlockSpec((count, third), lambda g, own_ref: (own_ref[0] ^ g, 0)),
                pl.BlockSpec((count, third), lambda g, own_ref: (own_ref[0] ^ g, 0)),
                whole((cols, width)),
            ],
            scratch_shapes=[pltpu.VMEM((count, width), f32), pltpu.VMEM((width, cols), bf16)],
        ),
        compiler_params=params(60),
        name="norm_qkv",
        cost_estimate=cost(11),
    )(own, *blocks, gain, w_qkv)


EDGE = 256


def query_rows(info_ref, query_start, size):
    query_row = query_start + iota((1, size), 1)
    first_cut, last_cut, length = info_ref[0], info_ref[1], info_ref[2]
    start_row = jnp.where(
        query_row >= last_cut, last_cut, jnp.where(query_row >= first_cut, first_cut, 0)
    )
    last_row = jnp.minimum(query_row, length - 1)
    return query_row, start_row, last_row


def score_parts(info_ref, keys_ref, queries, block, number, row_len):
    query_start = number * block
    query_row, start_row, last_row = query_rows(info_ref, query_start, block)
    free_from = query_start if query_start + block > row_len - EDGE else min(EDGE, query_start)
    parts = []
    for first, last in ((0, free_from), (free_from, query_start), (query_start, query_start + block)):
        if first == last:
            continue
        scores = mm(keys_ref[first:last, :], queries)
        key_col = first + iota(scores.shape, 0)
        if first == query_start:
            valid = (key_col >= start_row) & (key_col <= last_row) | (key_col == query_row)
            scores = jnp.where(valid, scores, masked_score)
        elif last == free_from:
            scores = jnp.where(key_col >= start_row, scores, masked_score)
        parts.append((first, last, scores))
    return parts


def attend_kernel(block, info_ref, k_ref, q_ref, v_ref, o_ref, low_ref, log_ref, q_pad):
    head = pl.program_id(0)
    row_len = k_ref.shape[0]
    q_pad[...] = jnp.zeros_like(q_pad)
    q_pad[pl.ds(pl.multiple_of(head * HEAD_DIM, HEAD_DIM), HEAD_DIM), :] = q_ref[...]
    for i in range(row_len // block):
        cols = slice(i * block, (i + 1) * block)
        parts = score_parts(info_ref, k_ref, q_pad[:, cols], block, i, row_len)
        top = functools.reduce(
            jnp.maximum, [jnp.max(s, axis=0, keepdims=True) for _, _, s in parts]
        )
        total, out = 0.0, 0.0
        for first, last, s in parts:
            p = jnp.exp(s - top)
            total = total + jnp.sum(p, axis=0, keepdims=True)
            out = out + mm(v_ref[:, first:last], p.astype(bf16))
        out = out / total
        o_ref[:, cols] = out
        low_ref[:, cols] = out.astype(bf16)
        log_ref[0, :, cols] = top + jnp.log(total)


def attend(info, keys, qkv_t, block=512):
    row_len, group = keys.shape
    heads = group // HEAD_DIM
    tile = pl.BlockSpec((HEAD_DIM, row_len), lambda h: (h, 0))
    return pl.pallas_call(
        functools.partial(attend_kernel, block),
        out_shape=[
            jax.ShapeDtypeStruct((group, row_len), f32),
            jax.ShapeDtypeStruct((group, row_len), bf16),
            jax.ShapeDtypeStruct((heads, 1, row_len), f32),
        ],
        grid=(heads,),
        in_specs=[
            smem_spec(),
            pl.BlockSpec((row_len, group), lambda h: (0, 0)),
            tile,
            pl.BlockSpec((HEAD_DIM, row_len), lambda h: (2 * heads + h, 0)),
        ],
        out_specs=[tile, tile, pl.BlockSpec((1, 1, row_len), lambda h: (h, 0, 0))],
        scratch_shapes=[pltpu.VMEM((group, row_len), bf16)],
        compiler_params=params(60),
        name="attend",
        cost_estimate=cost(17),
    )(info, keys, qkv_t, qkv_t)


def attend_back_kernel(
    block, head, info_ref, own_ref, k_ref, v_ref, q_ref, kt_ref, g0, g1, g2, g3, o_ref, log_ref,
    a_ref, dqkv_ref, grad_ref, q_pad, g_pad, dk_acc, dv_acc,
):
    row_len = k_ref.shape[0]
    own_rows = slice(head * HEAD_DIM, (head + 1) * HEAD_DIM)
    dk_acc[...] = jnp.zeros_like(dk_acc)
    dv_acc[...] = jnp.zeros_like(dv_acc)
    q_pad[...] = jnp.zeros_like(q_pad)
    g_pad[...] = jnp.zeros_like(g_pad)
    q_pad[own_rows, :] = q_ref[...]
    for j, part in enumerate((g0, g1, g2, g3)):
        size = part.shape[1]
        g_pad[own_rows, pl.ds(pl.multiple_of((own_ref[0] ^ j) * size, size), size)] = part[...]
    for i in range(row_len // block):
        cols = slice(i * block, (i + 1) * block)
        q, g = q_ref[:, cols], g_pad[own_rows, cols]
        g_wide = g_pad[:, cols]
        delta = jnp.sum(g.astype(f32) * o_ref[:, cols], axis=0, keepdims=True)
        log_total = log_ref[0, :, cols]
        dq = 0.0
        for first, last, s in score_parts(info_ref, k_ref, q_pad[:, cols], block, i, row_len):
            p = jnp.exp(s - log_total)
            dp = mm(v_ref[first:last, :], g_wide)
            ds = (p * (dp - delta)).astype(bf16)
            dv_acc[:, first:last] += mm(g, p.astype(bf16), NT)
            dk_acc[:, first:last] += mm(q, ds, NT)
            dq = dq + mm(kt_ref[:, first:last], ds)
        dqkv_ref[0:HEAD_DIM, cols] = (0.125 * dq).astype(bf16)
    dqkv_ref[HEAD_DIM : 2 * HEAD_DIM, :] = dk_acc[...].astype(bf16)
    dqkv_ref[2 * HEAD_DIM :, :] = dv_acc[...].astype(bf16)
    grad = mm(dqkv_ref[...], a_ref[...])
    rows = grad_ref.shape[1]
    for e in range(grad_ref.shape[0]):
        grad_ref[e] = grad[e * rows : (e + 1) * rows, :].astype(bf16)


def attend_back(head, pieces, info, own, keys, values, qkv_t, grads, out, logs, a_one, block=256):
    row_len, group = keys.shape
    heads = group // HEAD_DIM
    width = a_one.shape[1]
    whole = pl.BlockSpec((row_len, group), lambda g: (0, 0))
    piece = pl.BlockSpec((HEAD_DIM, grads[0].shape[1]), lambda g: (head, 0))
    tile = pl.BlockSpec((HEAD_DIM, row_len), lambda g: (head, 0))
    return pl.pallas_call(
        functools.partial(attend_back_kernel, block, head),
        out_shape=[
            jax.ShapeDtypeStruct((3 * HEAD_DIM, row_len), bf16),
            jax.ShapeDtypeStruct((pieces, 3 * HEAD_DIM // pieces, width), bf16),
        ],
        grid=(1,),
        in_specs=[
            smem_spec(),
            smem_spec(),
            whole,
            whole,
            tile,
            pl.BlockSpec((HEAD_DIM, row_len), lambda g: (heads + head, 0)),
            piece,
            piece,
            piece,
            piece,
            tile,
            pl.BlockSpec((1, 1, row_len), lambda g: (head, 0, 0)),
            pl.BlockSpec((row_len, width), lambda g: (0, 0)),
        ],
        out_specs=[
            pl.BlockSpec((3 * HEAD_DIM, row_len), lambda g: (0, 0)),
            pl.BlockSpec((pieces, 3 * HEAD_DIM // pieces, width), lambda g: (0, 0, 0)),
        ],
        scratch_shapes=[
            pltpu.VMEM((group, row_len), bf16),
            pltpu.VMEM((group, row_len), bf16),
            pltpu.VMEM((HEAD_DIM, row_len), f32),
            pltpu.VMEM((HEAD_DIM, row_len), f32),
        ],
        compiler_params=params(60),
        name="attend_back",
        cost_estimate=cost(11),
    )(info, own, keys, values, qkv_t, qkv_t, *grads, out, logs, a_one)


def gates_of(normed, router, route_rows):
    logits = mm(router, normed, NT, precise)
    expert_row = iota(logits.shape, 0)
    picked = [
        jnp.sum(jnp.where(expert_row == row, logits, 0.0), axis=0, keepdims=True)
        for row in route_rows
    ]
    top = jnp.maximum(picked[0], picked[1])
    raw = [jnp.exp(p - top) for p in picked]
    return [r / (raw[0] + raw[1]) for r in raw]


def dispatch_kernel(
    own_ref, t0, t1, t2, t3, x_ref, w_ref, gain_ref, router_ref, routes_ref, hot_a, hot_b,
    residual_ref, gates_ref, send_a, send_b,
):
    residual = x_ref[...].astype(f32)
    group = t0.shape[0]
    for j, part in enumerate((t0, t1, t2, t3)):
        rows = pl.ds(pl.multiple_of((own_ref[0] ^ j) * group, group), group)
        residual = residual + mm(part[...], w_ref[rows, :], TN)
    residual_ref[...] = residual
    scale = lax.rsqrt(jnp.mean(residual * residual, axis=1, keepdims=True) + norm_eps)
    normed = residual * scale * gain_ref[...]
    a_two = normed.astype(bf16)
    route_rows = [routes_ref[k : k + 1, :] for k in range(2)]
    gates = gates_of(normed, router_ref[...], route_rows)
    gates_ref[0:1, :] = gates[0]
    gates_ref[1:2, :] = gates[1]
    experts = router_ref.shape[0]
    expert_row = iota((experts, x_ref.shape[0]), 0)
    table = jnp.where(expert_row == route_rows[0], gates[0], 0.0) + jnp.where(
        expert_row == route_rows[1], gates[1], 0.0
    )
    stacked = jnp.concatenate([piece.astype(f32) for piece in split_three(table)], axis=0)
    stacked = stacked.astype(bf16)
    for hot, send in ((hot_a, send_a), (hot_b, send_b)):
        size = send.shape[1] - EXTRA
        rows = mm(hot[...], a_two).astype(bf16)
        for e in range(experts):
            own_rows = slice(e * size, (e + 1) * size)
            send[e, 0:size, :] = rows[own_rows, :]
            picked = mm(stacked, hot[own_rows, :], NT)
            three = [picked[k * experts + e : k * experts + e + 1, :] for k in range(3)]
            three = jnp.concatenate(three + [jnp.zeros((EXTRA - 3, size), f32)], axis=0)
            send[e, size:, :] = jnp.zeros((EXTRA, send.shape[2]), bf16)
            send[e, size:, 0:size] = three.astype(bf16)


def make_dispatch(own, parts, x, w_out, gain, router_t, routes_t, hots):
    count, width = x.shape
    experts = router_t.shape[0]
    shapes = [
        jax.ShapeDtypeStruct((count, width), f32),
        jax.ShapeDtypeStruct((2, count), f32),
    ]
    shapes += [
        jax.ShapeDtypeStruct((experts, hot.shape[0] // experts + EXTRA, width), bf16) for hot in hots
    ]
    return pl.pallas_call(
        dispatch_kernel,
        out_shape=shapes,
        in_specs=[smem_spec()] + [vmem_spec()] * 11,
        out_specs=[vmem_spec()] * len(shapes),
        compiler_params=params(60),
        name="project_dispatch",
        cost_estimate=cost(9),
    )(own, *parts, x, w_out, gain, router_t, routes_t, *hots)


def column_of(row):
    return jnp.broadcast_to(row, (128, row.shape[1])).T[:, 0:1]


def row_of(column):
    return jnp.broadcast_to(column, (column.shape[0], 128)).T[0:1, :]


GELU_SCALE = 0.7978845608028654
GELU_CUBE = 0.044715


def expert_kernel(start, x_ref, dy_ref, *refs):
    weights, refs = refs[:8], refs[8:]
    out_ref, slot_ref, act_ref, dpre_ref = refs[:4]
    x_buf, dy_buf, up_buf, down_buf, out_acc, slot_acc, sems = refs[4:]
    sources, size, width = out_ref.shape
    step = pl.program_id(0)
    parts = len(weights) // 2

    def copies(j):
        return (
            pltpu.make_async_copy(weights[2 * j], up_buf.at[j % 2], sems.at[0, j % 2]),
            pltpu.make_async_copy(weights[2 * j + 1], down_buf.at[j % 2], sems.at[1, j % 2]),
        )

    @pl.when(step == 0)
    def first():
        for copy in copies(0):
            copy.start()
        for n in range(sources):
            x_buf[n * size : (n + 1) * size, :] = x_ref[n, 0:size, :]
            dy_buf[n * size : (n + 1) * size, :] = dy_ref[n, start : start + size, :]
        out_acc[...] = jnp.zeros_like(out_acc)
        slot_acc[...] = jnp.zeros_like(slot_acc)

    for j in range(parts):

        @pl.when(step == j)
        def arrive(j=j):
            if j + 1 < parts:
                for copy in copies(j + 1):
                    copy.start()
            for copy in copies(j):
                copy.wait()

    which = lax.rem(step, 2)
    block = x_buf.shape[0] // 2

    @pl.loop(0, 2)
    def rows_of(r):
        rows = pl.ds(pl.multiple_of(r * block, block), block)
        up, down = up_buf[which], down_buf[which]
        pre = mm(x_buf[rows, :], up)
        square = pre * pre
        tanh = jnp.tanh(GELU_SCALE * (pre * (1.0 + GELU_CUBE * square)))
        half = 0.5 * (1.0 + tanh)
        act = (pre * half).astype(bf16)
        act_ref[0, rows, :] = act
        out_acc[rows, :] += mm(act, down)
        slope = half + (0.5 * GELU_SCALE) * pre * (1.0 - tanh * tanh) * (
            1.0 + (3.0 * GELU_CUBE) * square
        )
        dpre = (mm(dy_buf[rows, :], down, NT) * slope).astype(bf16)
        dpre_ref[0, rows, :] = dpre
        slot_acc[rows, :] += mm(dpre, up, NT)

    @pl.when(step == parts - 1)
    def last():
        for n in range(sources):
            rows = slice(n * size, (n + 1) * size)
            out = out_acc[rows, :].astype(bf16)
            out_ref[n] = out
            slot_ref[n, 0:size, :] = slot_acc[rows, :].astype(bf16)
            dgate = jnp.sum(
                dy_buf[rows, :].astype(f32) * out.astype(f32), axis=1, keepdims=True
            )
            slot_ref[n, size:, :] = jnp.zeros((EXTRA, width), bf16)
            slot_ref[n, size:, 0:size] = three_rows(row_of(dgate))


def run_experts(start, x, dy, weights):
    sources, size, width = x.shape
    size -= EXTRA
    rows = sources * size
    units = weights[0].shape[1]
    parts = len(weights) // 2

    def whole(shape):
        return pl.BlockSpec(shape, lambda g: (0,) * len(shape), pipeline_mode=pl.Buffered(1))

    kept = jax.ShapeDtypeStruct((parts, rows, units), bf16)
    kept_spec = pl.BlockSpec((1, rows, units), lambda g: (g, 0, 0))
    piece = (sources, size, width)
    return pl.pallas_call(
        functools.partial(expert_kernel, start),
        out_shape=[
            jax.ShapeDtypeStruct(piece, bf16), jax.ShapeDtypeStruct(x.shape, bf16), kept, kept
        ],
        grid=(parts,),
        in_specs=[whole(x.shape), whole(dy.shape)]
        + [pl.BlockSpec(memory_space=pl.ANY)] * (2 * parts),
        out_specs=[whole(piece), whole(x.shape), kept_spec, kept_spec],
        scratch_shapes=[
            pltpu.VMEM((rows, width), bf16),
            pltpu.VMEM((rows, width), bf16),
            pltpu.VMEM((2, width, units), bf16),
            pltpu.VMEM((2, units, width), bf16),
            pltpu.VMEM((rows, width), f32),
            pltpu.VMEM((rows, width), f32),
            pltpu.SemaphoreType.DMA((2, 2)),
        ],
        compiler_params=params(60),
        name="experts",
        cost_estimate=cost(27),
    )(x, dy, *weights)


def weight_kernel(dy_ref, x_a, x_b, act_a, act_b, dpre_a, dpre_b, own_out, near_out, far_out, x_turn, dy_turn, gate_buf):
    step = pl.program_id(0)
    experts, capacity, _ = dy_ref.shape

    @pl.when(step == 0)
    def turn():
        begin = 0
        for (start, size), x_ref in zip(halves_of(capacity), (x_a, x_b)):
            cols = slice(begin, begin + experts * size)
            for n in range(experts):
                three = x_ref[n, size:, 0:size].astype(f32)
                gate_buf[0:1, begin : begin + size] = three[0:1] + three[1:2] + three[2:3]
                begin += size
            gate = gate_buf[0:1, cols]
            shape = (experts * size, x_ref.shape[2])
            rows = x_ref[:, 0:size, :].reshape(shape).astype(f32)
            x_turn[:, cols] = (rows.T * gate).astype(bf16)
            rows = dy_ref[:, start : start + size, :].reshape(shape).astype(f32)
            dy_turn[:, cols] = (rows.T * gate).astype(bf16)

    cut = act_a.shape[1]
    up = mm(x_turn[:, :cut], dpre_a[0]) + mm(x_turn[:, cut:], dpre_b[0])
    down = (mm(dy_turn[:, :cut], act_a[0]) + mm(dy_turn[:, cut:], act_b[0])).T
    for j, (out, n) in enumerate(((own_out, 0), (near_out, 0), (far_out, 0), (near_out, 2))):

        @pl.when(step == j)
        def keep(out=out, n=n):
            out[n] = up.astype(out.dtype)
            out[n + 1] = down.astype(out.dtype)


def weight_grads(xs, dy, acts, dpres):
    experts, capacity, width = dy.shape
    parts, _, units = acts[0].shape
    assert units == width

    def whole(*shape):
        return pl.BlockSpec(shape, lambda g: (0,) * len(shape), pipeline_mode=pl.Buffered(1))

    kept = [pl.BlockSpec((1,) + a.shape[1:], lambda g: (g, 0, 0)) for a in (*acts, *dpres)]
    return pl.pallas_call(
        weight_kernel,
        out_shape=[
            jax.ShapeDtypeStruct((2, width, units), f32),
            jax.ShapeDtypeStruct((4, width, units), bf16),
            jax.ShapeDtypeStruct((2, width, units), f32),
        ],
        grid=(parts,),
        in_specs=[whole(*dy.shape)] + [whole(*x.shape) for x in xs] + kept,
        out_specs=[whole(2, width, units), whole(4, width, units), whole(2, width, units)],
        scratch_shapes=[pltpu.VMEM((width, experts * capacity), bf16)] * 2
        + [pltpu.VMEM((8, experts * capacity), f32)],
        compiler_params=params(60),
        name="expert_weight_grads",
        cost_estimate=cost(30),
    )(dy, *xs, *acts, *dpres)


def combine_back_kernel(
    own_ref, hot_a, hot_b, p0a, p1a, p0b, p1b, residual_ref, dy_ref, gates_ref, routes_ref,
    router_ref, gain_ref, w_ref, t0, t1, t2, t3, slot_a, slot_b,
    dres_ref, datt_ref, gout_ref, small_ref, buf_a, buf_b,
):
    experts = router_ref.shape[0]
    table = [0.0] * experts
    for slot, hot, buf in ((slot_a, hot_a, buf_a), (slot_b, hot_b, buf_b)):
        size = slot.shape[1] - EXTRA
        for e in range(experts):
            rows = slice(e * size, (e + 1) * size)
            buf[rows, :] = slot[e, 0:size, :]
            picked = mm(slot[e, size:, 0:size], hot[rows, :])
            table[e] = table[e] + (picked[0:1] + picked[1:2] + picked[2:3])
    table = jnp.concatenate(table, axis=0)
    residual = residual_ref[...]
    count = residual.shape[0]
    scale = lax.rsqrt(jnp.mean(residual * residual, axis=1, keepdims=True) + norm_eps)
    unit = residual * scale
    gain = gain_ref[...]
    expert_row = iota((experts, count), 0)
    routes = [routes_ref[k : k + 1, :] for k in range(2)]
    gates = [gates_ref[k : k + 1, :] for k in range(2)]
    dgates = [
        jnp.sum(jnp.where(expert_row == r, table, 0.0), axis=0, keepdims=True) for r in routes
    ]
    mean = gates[0] * dgates[0] + gates[1] * dgates[1]
    dlogit = sum(
        jnp.where(expert_row == r, g * (d - mean), 0.0) for r, g, d in zip(routes, gates, dgates)
    )
    small_ref[...] = jnp.zeros_like(small_ref)
    small_ref[0:experts, :] = mm(dlogit, unit * gain, precision=precise)
    dnormed = mm(dlogit, router_ref[...], TN, precise)
    for gate, pick_a, pick_b in ((gates[0], p0a, p0b), (gates[1], p1a, p1b)):
        rows = mm(pick_a[...], buf_a[...]) + mm(pick_b[...], buf_b[...])
        dnormed = dnormed + column_of(gate) * rows
    small_ref[experts : experts + 1, :] = jnp.sum(dnormed * unit, axis=0, keepdims=True)
    scaled = dnormed * gain
    dres = dy_ref[...].astype(f32) + scale * (
        scaled - unit * jnp.mean(scaled * unit, axis=1, keepdims=True)
    )
    dres_ref[...] = dres
    branch = dres.astype(bf16)
    datt_ref[...] = mm(w_ref[...], branch, NT).astype(bf16)
    group = t0.shape[0]
    for j, part in enumerate((t0, t1, t2, t3)):
        rows = pl.ds(pl.multiple_of((own_ref[0] ^ j) * group, group), group)
        gout_ref[rows, :] = mm(part[...], branch)


def combine_back(own, slots, hots, picks, residual, dy, gates, routes_t, router_t, gain, w_out, parts):
    count, width = residual.shape
    experts = router_t.shape[0]
    shapes = [
        jax.ShapeDtypeStruct((count, width), f32),
        jax.ShapeDtypeStruct((width, count), bf16),
        jax.ShapeDtypeStruct((width, width), f32),
        jax.ShapeDtypeStruct((experts + 8, width), f32),
    ]
    return pl.pallas_call(
        combine_back_kernel,
        out_shape=shapes,
        in_specs=[smem_spec()] + [vmem_spec()] * 19,
        out_specs=[vmem_spec()] * len(shapes),
        scratch_shapes=[pltpu.VMEM((hot.shape[0], width), bf16) for hot in hots],
        compiler_params=params(60),
        name="combine_back",
        cost_estimate=cost(13),
    )(own, *hots, *picks, residual, dy, gates, routes_t, router_t, gain, w_out, *parts, *slots)


def combine_kernel(p0a, p1a, p0b, p1b, residual_ref, gates_ref, out_a, out_b, y_ref, buf_a, buf_b):
    for out, buf in ((out_a, buf_a), (out_b, buf_b)):
        size = out.shape[1]
        for e in range(out.shape[0]):
            buf[e * size : (e + 1) * size, :] = out[e]
    total = residual_ref[...]
    for k, (pick_a, pick_b) in enumerate(((p0a, p0b), (p1a, p1b))):
        rows = mm(pick_a[...], buf_a[...]) + mm(pick_b[...], buf_b[...])
        total = total + column_of(gates_ref[k : k + 1, :]) * rows
    y_ref[...] = total.astype(bf16)


def combine(outs, picks, residual, gates):
    width = residual.shape[1]
    return pl.pallas_call(
        combine_kernel,
        out_shape=jax.ShapeDtypeStruct(residual.shape, bf16),
        in_specs=[vmem_spec()] * 8,
        out_specs=vmem_spec(),
        scratch_shapes=[pltpu.VMEM((out.shape[0] * out.shape[1], width), bf16) for out in outs],
        compiler_params=params(60),
        name="combine",
        cost_estimate=cost(6),
    )(*picks, residual, gates, *outs)


def spread_kernel(places_ref, d0, d1, d2, w_ref, near_out, last_out, far_out, own_out, d_buf):
    step = pl.program_id(0)
    heads = d_buf.shape[0] // (3 * HEAD_DIM)
    for c, part in enumerate((d0, d1, d2)):
        for t in range(3):
            start = (t * heads + c) * HEAD_DIM
            d_buf[start : start + HEAD_DIM, :] = part[t * HEAD_DIM : (t + 1) * HEAD_DIM, :]
    dn = mm(d_buf[...], w_ref[...], TN)
    for n, out in enumerate((near_out, last_out, far_out, own_out)):

        @pl.when(step == n)
        def keep(out=out):
            out[...] = dn.astype(out.dtype)


def spread(places, parts, w_t):
    rows, row_len = parts[0].shape
    cols, width = w_t.shape
    steps = places.shape[0]
    count = row_len // steps
    tile = pl.BlockSpec((rows, count), lambda g, places: (0, places[g]))

    def whole(shape):
        return pl.BlockSpec(shape, lambda g, places: (0, 0), pipeline_mode=pl.Buffered(1))

    return pl.pallas_call(
        spread_kernel,
        out_shape=[jax.ShapeDtypeStruct((count, width), t) for t in (bf16, bf16, f32, f32)],
        grid_spec=pltpu.PrefetchScalarGridSpec(
            num_scalar_prefetch=1,
            grid=(steps,),
            in_specs=[tile] * 3 + [whole((cols, width))],
            out_specs=[whole((count, width))] * 4,
            scratch_shapes=[pltpu.VMEM((cols, count), bf16)],
        ),
        compiler_params=params(40),
        name="spread_back",
        cost_estimate=cost(8),
    )(places, *parts, w_t)


def fold_kernel(special, taken, moved_ref, *refs):
    given, out_ref = refs[:-1], refs[-1]
    exps, rows, width = out_ref.shape
    sums = moved_ref[0, 0:taken].astype(f32)
    for e in range(1, exps):
        sums = sums + moved_ref[e, 0:taken].astype(f32)
    if special:
        body = taken - 2 * special
        high, mid, _ = split_three(
            sums[body : body + special] + sums[body + special : body + 2 * special]
        )
        sums = jnp.concatenate([sums[:body], high.astype(f32), mid.astype(f32)], axis=0)
    start = given[0].shape[1] if given else 0
    pad = rows - start - taken
    if pad:
        sums = jnp.concatenate([sums, jnp.zeros((pad, width), f32)], axis=0)
    sums = sums.astype(bf16)
    for e in range(exps):
        if given:
            out_ref[e, 0:start] = given[0][e]
        out_ref[e, start:] = sums


def fold(moved, taken, special, given=()):
    exps, _, width = moved.shape
    rows = taken + sum(g.shape[1] for g in given)
    return pl.pallas_call(
        functools.partial(fold_kernel, special, taken),
        out_shape=jax.ShapeDtypeStruct((exps, rows + -rows % 8, width), bf16),
        in_specs=[vmem_spec()] * (1 + len(given)),
        out_specs=vmem_spec(),
        compiler_params=params(40),
        name="fold_sums",
        cost_estimate=cost(2),
    )(moved, *given)


def lay_out_kernel(rows, own_ref, *refs):
    arrays, (w_ref, gain_ref, grad_ref, ggain_ref, b0, b1, b2, sems) = refs[:12], refs[12:]
    hids, exps = b0.shape[0], b0.shape[1]
    bufs = (b0, b1, b2)
    step = pl.program_id(0)
    block = grad_ref.shape[0]

    @pl.when(step == 0)
    def fetch():
        copies = [
            pltpu.make_async_copy(arrays[4 * c + j], bufs[c].at[own_ref[0] ^ j], sems.at[c, j])
            for c in range(3)
            for j in range(hids)
        ]
        for copy in copies:
            copy.start()
        for copy in copies:
            copy.wait()

    cols = pl.ds(pl.multiple_of(step * block, block), block)
    blocks = {}
    for h in range(hids):
        for c, buf in enumerate(bufs):
            pieces = [buf[h, e, 0:rows, cols].astype(f32) for e in range(exps)]
            blocks[h, c] = jnp.concatenate(pieces, axis=0)
    stacked = [
        blocks[h, c][t * HEAD_DIM : (t + 1) * HEAD_DIM]
        for t in range(3)
        for h in range(hids)
        for c in range(3)
    ]
    grad = jnp.concatenate(stacked, axis=0).T
    grad_ref[...] = grad
    total = jnp.sum(grad * w_ref[...].astype(f32), axis=1, keepdims=True)
    ggain_ref[...] = row_of(total) / gain_ref[...]


def lay_out(own, chunks, rows, w_qkv, gain, block=128):
    width, cols = w_qkv.shape
    arrays = [a for chunk in chunks for a in chunk]
    tile = pl.BlockSpec((block, cols), lambda g: (g, 0))
    row = pl.BlockSpec((1, block), lambda g: (0, g))
    return pl.pallas_call(
        functools.partial(lay_out_kernel, rows),
        out_shape=[
            jax.ShapeDtypeStruct((width, cols), f32),
            jax.ShapeDtypeStruct((1, width), f32),
        ],
        grid=(width // block,),
        in_specs=[smem_spec()] + [pl.BlockSpec(memory_space=pl.ANY)] * 12 + [tile, row],
        out_specs=[tile, row],
        scratch_shapes=[pltpu.VMEM((4,) + chunk[0].shape, bf16) for chunk in chunks]
        + [pltpu.SemaphoreType.DMA((3, 4))],
        compiler_params=params(50),
        name="lay_out_qkv",
        cost_estimate=cost(10),
    )(own, *arrays, w_qkv, gain)


def lay_out_rest_kernel(start, own_ref, *refs):
    arrays, (out_ref, buf, sems) = refs[:4], refs[4:]
    hids, exps = buf.shape[0], buf.shape[1]
    rows = out_ref.shape[0] // (hids * exps)
    copies = [
        pltpu.make_async_copy(arrays[j], buf.at[own_ref[0] ^ j], sems.at[j]) for j in range(hids)
    ]
    for copy in copies:
        copy.start()
    for copy in copies:
        copy.wait()
    for h in range(hids):
        for e in range(exps):
            n = h * exps + e
            out_ref[n * rows : (n + 1) * rows, :] = buf[h, e, start : start + rows].astype(f32)


def lay_out_rest(own, arrays, start, width):
    return pl.pallas_call(
        functools.partial(lay_out_rest_kernel, start),
        out_shape=jax.ShapeDtypeStruct((width, width), f32),
        in_specs=[smem_spec()] + [pl.BlockSpec(memory_space=pl.ANY)] * 4,
        out_specs=vmem_spec(),
        scratch_shapes=[pltpu.VMEM((4,) + arrays[0].shape, bf16), pltpu.SemaphoreType.DMA((4,))],
        compiler_params=params(50),
        name="lay_out_w_out",
        cost_estimate=cost(3),
    )(own, *arrays)


def adam_update(weight, gradient, first_moment, second_moment, live_mask):
    first_next = beta_one * first_moment + (1.0 - beta_one) * gradient
    second_next = beta_two * second_moment + (1.0 - beta_two) * gradient * gradient
    first_hat = first_next / (1.0 - beta_one**adam_steps)
    second_hat = second_next / (1.0 - beta_two**adam_steps)
    weight_next = weight - learn_rate * first_hat / (jnp.sqrt(second_hat) + adam_eps)
    return (
        jnp.where(live_mask, weight_next, weight),
        jnp.where(live_mask, first_next, first_moment),
        jnp.where(live_mask, second_next, second_moment),
    )


def tie(value, other):
    return lax.optimization_barrier((value, other))[0]


def exchange(value, axis):
    return lax.all_to_all(value, axis, split_axis=0, concat_axis=0, tiled=True)


def split_sum(value, axis, distance):
    pairs = value.reshape((value.shape[0] // 2, 2) + value.shape[1:])
    low = (lax.axis_index(axis) & distance) == 0
    keep = jnp.where(low, pairs[:, 0], pairs[:, 1])
    give = jnp.where(low, pairs[:, 1], pairs[:, 0]).astype(bf16)
    return keep + swap(give, axis, distance).astype(f32)


def halves(value):
    high = lax.reduce_precision(value, 8, 7)
    return high.astype(bf16), (value - high).astype(bf16)


def pad_rows(value):
    return jnp.pad(value, ((0, 0), (0, -value.shape[1] % 8), (0, 0)))


def gather_hid(value):
    far = swap(value, "hid", 2)
    near = swap(value, "hid", 1)
    return value, near, far, swap(far, "hid", 1)


def body(
    tokens, cotangent, routes, segments, lengths, gain_attn, gain_moe, w_qkv, w_out, router_w,
    router_first, router_second, up_w, down_w, up_first, up_second, down_first, down_second,
):
    exp_count = lax.axis_size("exp")
    hid_count = lax.axis_size("hid")
    hid = lax.axis_index("hid")
    exp_index = lax.axis_index("exp")
    own = jnp.stack([hid, exp_index]).astype(jnp.int32)
    x_own = tokens[0]
    dy = cotangent[0]
    count, width = x_own.shape
    experts = router_w.shape[1]
    frozen_count = experts // 2
    capacity = max(2, 3 * count // experts)
    group = width // hid_count
    heads = group // HEAD_DIM
    is_new = exp_index >= frozen_count

    x_far = swap(x_own, "hid", 2)
    x_near = swap(x_own, "hid", 1)
    routes_t = routes[0].T
    hots, picks, dy_send = make_tables(routes_t, dy, experts, capacity)
    seg_row = segments[0]
    info = jnp.stack(
        [
            jnp.sum((seg_row < 1).astype(jnp.int32)),
            jnp.sum((seg_row < 2).astype(jnp.int32)),
            lengths[0],
        ]
    )
    up_low = up_w[0].astype(bf16)
    down_low = down_w[0].astype(bf16)
    router_t = router_w.T
    x_far, (info, dy_send, up_low, down_low, router_t, routes_t) = lax.optimization_barrier(
        (x_far, (info, dy_send, up_low, down_low, router_t, routes_t))
    )
    x_last = swap(x_far, "hid", 1)
    blocks = (x_own, x_near, x_far, x_last)
    dy_all = exchange(dy_send, "exp")

    up_far = swap(up_low, "hid", 2)
    up_near, down_near = swap(up_low, "hid", 1), swap(down_low, "hid", 1)

    a_one, qkv_t, keys, values, w_t = project_qkv(own, blocks, gain_attn[None], w_qkv)
    out_heads, out_low, logs = attend(info, keys, qkv_t)
    out_low, (up_far, up_near, down_near) = lax.optimization_barrier(
        (out_low, (up_far, up_near, down_near))
    )

    def piece_of(value, j):
        return lax.dynamic_slice_in_dim(value, (hid ^ j) * count, count, 1)

    att_parts = [piece_of(out_low, 0)] + [
        swap(piece_of(out_low, j), "hid", j) for j in range(1, hid_count)
    ]
    att_parts, down_low = lax.optimization_barrier((att_parts, down_low))
    down_far = swap(down_low, "hid", 2)

    residual, gates, *sends = make_dispatch(
        own, att_parts, x_own, w_out, gain_moe[None], router_t, routes_t, hots
    )
    up_far, down_far = tie((up_far, down_far), residual)
    up_last, down_last = swap(up_far, "hid", 1), swap(down_far, "hid", 1)
    weights = (up_low, down_low, up_near, down_near, up_far, down_far, up_last, down_last)
    sends = tie(sends, dy_all)
    x_rows = [exchange(send, "exp") for send in sends]

    starts = [start for start, _ in halves_of(capacity)]
    results = [run_experts(start, x, dy_all, weights) for start, x in zip(starts, x_rows)]
    outs, slots, acts, dpres = zip(*results)
    slot_back = [exchange(slot, "exp") for slot in slots]

    own_part, near_part, far_part = weight_grads(x_rows, dy_all, acts, dpres)
    slot_back, near_part = lax.optimization_barrier((slot_back, near_part))
    near_part = swap(near_part, "hid", 1)

    dres, datt, gout, small = combine_back(
        own, slot_back, hots, picks, residual, dy, gates, routes_t, router_t,
        gain_moe[None], w_out, att_parts,
    )

    datt, near_part = lax.optimization_barrier((datt, near_part))

    def heads_of(value, j):
        return lax.dynamic_slice_in_dim(value, (hid ^ j) * group, group, 0)

    datt_parts = [heads_of(datt, 0)] + [
        swap(heads_of(datt, j), "hid", j) for j in range(1, hid_count)
    ]

    gout, small = tie((gout, small), datt_parts)

    gout = gout.reshape(hid_count, width // hid_count, width)
    for d in (1, 2):
        gout = split_sum(gout, "hid", d)
        small = small + swap(small, "hid", d)
    far_part, gout, small = lax.optimization_barrier((far_part, gout, small))
    far_part = swap((far_part + near_part[2:].astype(f32)).astype(bf16), "hid", 2)
    out_rows = width // (hid_count * exp_count)
    small_rows = -(-(experts + 1) // exp_count)
    missing = max(0, exp_count * small_rows - small.shape[0])
    small = jnp.pad(small, ((0, missing), (0, 0)))[: exp_count * small_rows]
    small = small.reshape(exp_count, small_rows, width)
    gout = gout.reshape(exp_count, out_rows, width).astype(bf16)

    rows = 3 * HEAD_DIM // exp_count
    chunks, dqkv = [], []
    for h in range(heads):
        if h == 1:
            out_first = exchange(tie(outs[0], slot_back), "exp")
            chunks[0] = jnp.concatenate([chunks[0], gout, *halves(small)], axis=1)
            chunks[0], out_first = lax.optimization_barrier((chunks[0], out_first))
            first = exchange(pad_rows(chunks[0]), "exp")
        if h == 2:
            datt_parts, first = lax.optimization_barrier((datt_parts, first))
        dqkv_h, grad_h = attend_back(
            h, exp_count, info, own, keys, values, qkv_t, datt_parts, out_heads, logs, a_one
        )
        dqkv.append(dqkv_h)
        chunks.append(grad_h)
    places = jnp.stack([hid ^ j for j in (1, 3, 2, 0)]).astype(jnp.int32)
    near_dn, last_dn, far_dn, own_dn = spread(places, dqkv, w_t)
    near_dn, last_dn = swap(near_dn, "hid", 1), swap(last_dn, "hid", 1)
    far_dn = swap((far_dn + last_dn.astype(f32)).astype(bf16), "hid", 2)
    dnormed = own_dn + near_dn.astype(f32) + far_dn.astype(f32)
    x = x_own.astype(f32)
    scale = lax.rsqrt(jnp.mean(x * x, axis=-1, keepdims=True) + norm_eps)
    unit = x * scale
    scaled = dnormed * gain_attn
    grad_tokens = (
        dres + scale * (scaled - unit * jnp.mean(scaled * unit, axis=-1, keepdims=True))
    ).astype(bf16)

    first_rows = rows + out_rows + 2 * small_rows
    second = exchange(fold(first, first_rows, small_rows, [chunks[1]]), "exp")
    third = exchange(fold(second, rows, 0, [chunks[2]]), "exp")
    fourth = exchange(fold(third, rows, 0), "exp")
    out_second = exchange(tie(outs[1], fourth), "exp")
    out_tokens = combine((out_first, out_second), picks, residual, gates)
    gathered = [
        gather_hid(value)
        for value in (second[:, rows : 2 * rows + out_rows], third[:, rows : 2 * rows], fourth)
    ]
    grad_qkv, grad_gain_attn = lay_out(own, gathered, rows, w_qkv, gain_attn[None])
    grad_out_proj = lay_out_rest(own, gathered[0], rows, width)
    start = 2 * rows + out_rows
    small = second[:, start : start + small_rows].astype(f32)
    small = small + second[:, start + small_rows : start + 2 * small_rows].astype(f32)
    small = small.reshape(exp_count * small_rows, width)
    far_part = [far_part[0], tie(far_part[1], fourth)]
    grad_up, grad_down = (
        jnp.where(is_new, own_part[n] + near_part[n].astype(f32) + far_part[n].astype(f32), 0.0)
        for n in range(2)
    )
    grad_gain_attn = grad_gain_attn[0]
    grad_gain_moe = small[experts]
    live_columns = (jnp.arange(experts, dtype=jnp.int32) >= frozen_count)[None, :]
    grad_router = jnp.where(live_columns, small[:experts].T, 0.0)
    router_new, router_first_next, router_second_next = adam_update(
        router_w[:, frozen_count:], grad_router[:, frozen_count:], router_first, router_second, True
    )
    router_next = jnp.concatenate([router_w[:, :frozen_count], router_new], axis=1)
    up_next, up_first_next, up_second_next = adam_update(
        up_w[0], grad_up, up_first[0], up_second[0], is_new
    )
    down_next, down_first_next, down_second_next = adam_update(
        down_w[0], grad_down, down_first[0], down_second[0], is_new
    )
    return (
        out_tokens[None],
        grad_tokens[None],
        grad_qkv,
        grad_out_proj,
        grad_gain_attn,
        grad_gain_moe,
        grad_router,
        router_next,
        router_first_next,
        router_second_next,
        grad_up[None],
        grad_down[None],
        up_next[None],
        down_next[None],
        up_first_next[None],
        up_second_next[None],
        down_first_next[None],
        down_second_next[None],
    )


def solution(mesh):
    tok = P("exp", "hid", None)
    up = P("exp", None, "hid")
    return jax.shard_map(
        body,
        mesh=mesh,
        in_specs=(tok, tok, tok, P("exp", None), P("exp")) + (P(),) * 7
        + (up, tok, up, up, tok, tok),
        out_specs=(tok, tok) + (P(),) * 8 + (up, tok, up, tok, up, up, tok, tok),
        check_vma=False,
    )
```

```python
import functools

import jax
import jax.numpy as jnp
from jax import lax
from jax.experimental import pallas as pl
from jax.experimental.pallas import tpu as pltpu
from jax.sharding import PartitionSpec as P

HEADS = 12
HEAD_DIM = 64

precise = lax.Precision.HIGHEST
norm_eps = 1e-06
beta_one = 0.9
beta_two = 0.999
learn_rate = 0.01
adam_eps = 1e-08
adam_steps = 10.0
masked_score = -1e30

bf16 = jnp.bfloat16
f32 = jnp.float32
MIB = 1 << 20
COST_SCALE = 0.1


def mm(left, right, contract=((1,), (0,)), precision=None):
    return lax.dot_general(
        left, right, (contract, ((), ())), preferred_element_type=f32, precision=precision
    )


NT = ((1,), (1,))
TN = ((0,), (0,))


def swap(value, axis, distance):
    count = lax.axis_size(axis)
    return lax.ppermute(value, axis, [(i, i ^ distance) for i in range(count)])


def iota(shape, dim):
    return lax.broadcasted_iota(jnp.int32, shape, dim)


def split_three(value):
    high = value.astype(bf16)
    rest = value - high.astype(f32)
    mid = rest.astype(bf16)
    low = (rest - mid.astype(f32)).astype(bf16)
    return high, mid, low


EXTRA = 8
LANE_B = 128


def three_rows(row):
    high, mid, low = (piece.astype(f32) for piece in split_three(row))
    return jnp.concatenate([high, mid, low, jnp.zeros((EXTRA - 3, row.shape[1]), f32)], axis=0).astype(bf16)


def vmem_spec():
    return pl.BlockSpec(memory_space=pltpu.VMEM)


def smem_spec():
    return pl.BlockSpec(memory_space=pltpu.SMEM)


def params(mib):
    return pltpu.CompilerParams(vmem_limit_bytes=mib * MIB)


def cost(micros):
    micros = micros * COST_SCALE
    return pl.CostEstimate(
        flops=int(micros * 1.1e9), bytes_accessed=int(micros * 3e6), transcendentals=0
    )


def halves_of(capacity):
    first = (capacity // 2 + 15) // 16 * 16
    return ((0, first), (first, capacity - first))


def tables_kernel(routes_ref, dy_ref, hot_a, hot_b, *outs):
    picks, send_ref = outs[:4], outs[4]
    experts, capacity, _ = send_ref.shape
    count = routes_ref.shape[1]
    expert_row = iota((experts, count), 0)
    route_rows = [routes_ref[k : k + 1, :] for k in range(2)]
    hits = [expert_row == row for row in route_rows]
    hit = hits[0] | hits[1]
    hit_low = jnp.where(hit, 1.0, 0.0).astype(bf16)
    upper = jnp.where(iota((count, count), 0) < iota((count, count), 1), 1.0, 0.0).astype(bf16)
    slot = mm(hit_low, upper)
    slot = jnp.where(hit & (slot < capacity), slot, -1.0)
    index_rows = []
    for (start, size), hot in zip(halves_of(capacity), (hot_a, hot_b)):
        row_id = iota((size, count), 0).astype(f32) + float(start)
        for e in range(experts):
            hot[e * size : (e + 1) * size, :] = jnp.where(
                row_id == slot[e : e + 1, :], 1.0, 0.0
            ).astype(bf16)
        rows = mm(hot[...], dy_ref[...]).astype(bf16)
        for e in range(experts):
            send_ref[e, start : start + size, :] = rows[e * size : (e + 1) * size, :]
        for k in range(2):
            own_slot = jnp.sum(jnp.where(hits[k], slot, 0.0), axis=0, keepdims=True)
            inside = (own_slot >= start) & (own_slot < start + size)
            place = route_rows[k].astype(f32) * size + own_slot - start
            index_rows.append(jnp.where(inside, place, -1.0))
    index_cols = jnp.concatenate(index_rows * 2, axis=0).T
    for n, pick in enumerate(picks):
        lane = iota(pick.shape, 1).astype(f32)
        pick[...] = jnp.where(lane == index_cols[:, n : n + 1], 1.0, 0.0).astype(bf16)


def make_tables(routes_t, dy, experts, capacity):
    count, width = dy.shape
    sizes = [experts * size for _, size in halves_of(capacity)]
    shapes = [jax.ShapeDtypeStruct((size, count), bf16) for size in sizes]
    shapes += [jax.ShapeDtypeStruct((count, size), bf16) for size in sizes for _ in range(2)]
    shapes += [jax.ShapeDtypeStruct((experts, capacity, width), bf16)]
    results = pl.pallas_call(
        tables_kernel,
        out_shape=shapes,
        in_specs=[vmem_spec()] * 2,
        out_specs=[vmem_spec()] * len(shapes),
        compiler_params=params(60),
        name="slot_tables",
        cost_estimate=cost(0.1),
    )(routes_t, dy)
    return results[0:2], results[2:6], results[6]


def qkv_kernel(
    pieces, own_ref, *refs
):
    blocks, refs = refs[: 2 * pieces], refs[2 * pieces :]
    gain_ref, w_ref, a0, a1, q0, q1, k0, k1, v0, v1, w_buf, heads_ref = refs
    width, cols = heads_ref.shape
    third = cols // 3
    for h in range(width // third):

        @pl.when(own_ref[0] == h)
        def pick(h=h):
            for t in range(3):
                start = t * width + h * third
                heads_ref[:, t * third : (t + 1) * third] = w_ref[:, start : start + third]

    w_buf[...] = heads_ref[...].T
    outs = ((a0, q0, k0, v0), (a1, q1, k1, v1))
    for n, (a_ref, qkv_ref, k_ref, v_ref) in enumerate(outs):
        x = [x_ref[...] for x_ref in blocks[n * pieces : (n + 1) * pieces]]
        x = jnp.concatenate(x, axis=0).astype(f32)
        scale = lax.rsqrt(jnp.mean(x * x, axis=1, keepdims=True) + norm_eps)
        a = (x * scale * gain_ref[...]).astype(bf16)
        a_ref[...] = a
        qkv_t = mm(w_buf[...], a, NT).astype(bf16)
        qkv_ref[0:third, :] = qkv_t[0:third, :] * jnp.asarray(0.125, bf16)
        qkv_ref[third:, :] = qkv_t[third:, :]
        both = mm(a, heads_ref[:, third:]).astype(bf16)
        k_ref[...] = both[:, :third]
        v_ref[...] = both[:, third:]


def project_qkv(own, blocks, gain, w_qkv):
    pieces = len(blocks) // 2
    count, width = pieces * blocks[0].shape[0], blocks[0].shape[1]
    cols = w_qkv.shape[1] // 4
    third = cols // 3
    shapes = [(count, width)] * 2 + [(cols, count)] * 2 + [(count, third)] * 4 + [(cols, width)]
    return pl.pallas_call(
        functools.partial(qkv_kernel, pieces),
        out_shape=[jax.ShapeDtypeStruct(shape, bf16) for shape in shapes],
        in_specs=[smem_spec()] + [vmem_spec()] * (2 * pieces + 2),
        out_specs=[vmem_spec()] * 9,
        scratch_shapes=[pltpu.VMEM((width, cols), bf16)],
        compiler_params=params(60),
        name="norm_qkv",
        cost_estimate=cost(0.1),
    )(own, *blocks, gain, w_qkv)


EDGE = 256


def query_rows(info_ref, query_start, size):
    query_row = query_start + iota((1, size), 1)
    first_cut, last_cut, length = info_ref[0], info_ref[1], info_ref[2]
    start_row = jnp.where(
        query_row >= last_cut, last_cut, jnp.where(query_row >= first_cut, first_cut, 0)
    )
    last_row = jnp.minimum(query_row, length - 1)
    return query_row, start_row, last_row


def score_parts(info_ref, keys_ref, queries, block, number, row_len):
    query_start = number * block
    query_row, start_row, last_row = query_rows(info_ref, query_start, block)
    free_from = query_start if query_start + block > row_len - EDGE else min(EDGE, query_start)
    parts = []
    for first, last in ((0, free_from), (free_from, query_start), (query_start, query_start + block)):
        if first == last:
            continue
        scores = mm(keys_ref[first:last, :], queries)
        key_col = first + iota(scores.shape, 0)
        if first == query_start:
            valid = (key_col >= start_row) & (key_col <= last_row) | (key_col == query_row)
            scores = jnp.where(valid, scores, masked_score)
        elif last == free_from:
            scores = jnp.where(key_col >= start_row, scores, masked_score)
        parts.append((first, last, scores))
    return parts


def gather_blocks(own_ref, buf, parts, axis):
    for j, part in enumerate(parts):
        size = part.shape[axis]
        where = pl.ds(pl.multiple_of((own_ref[0] ^ j) * size, size), size)
        if axis:
            buf[:, where] = part[...]
        else:
            buf[where, :] = part[...]


def attend_kernel(block, info_ref, own_ref, *refs):
    (k_parts, q_parts, v_parts), refs = (refs[0:4], refs[4:8], refs[8:12]), refs[12:]
    o_ref, log_ref, keys_ref = refs[:3]
    pieces, (q_pad, v_buf, low_buf) = refs[3:7], refs[7:]
    head = pl.program_id(0)
    row_len = keys_ref.shape[0]

    @pl.when(head == 0)
    def keys():
        gather_blocks(own_ref, keys_ref, k_parts, 0)

    q_pad[...] = jnp.zeros_like(q_pad)
    own_rows = pl.ds(pl.multiple_of(head * HEAD_DIM, HEAD_DIM), HEAD_DIM)
    gather_blocks(own_ref, q_pad.at[own_rows], q_parts, 1)
    gather_blocks(own_ref, v_buf, v_parts, 1)
    for i in range(row_len // block):
        cols = slice(i * block, (i + 1) * block)
        parts = score_parts(info_ref, keys_ref, q_pad[:, cols], block, i, row_len)
        top = functools.reduce(
            jnp.maximum, [jnp.max(s, axis=0, keepdims=True) for _, _, s in parts]
        )
        total, out = 0.0, 0.0
        for first, last, s in parts:
            p = jnp.exp(s - top)
            total = total + jnp.sum(p, axis=0, keepdims=True)
            out = out + mm(v_buf[:, first:last], p.astype(bf16))
        out = out / total
        o_ref[:, cols] = out
        low_buf[:, cols] = out.astype(bf16)
        log_ref[0, :, cols] = top + jnp.log(total)
    for j, piece in enumerate(pieces):
        size = piece.shape[1]
        where = pl.ds(pl.multiple_of((own_ref[0] ^ j) * size, size), size)
        piece[...] = low_buf[:, where]


def attend(info, own, k_parts, qkv_parts, block=512):
    count, group = k_parts[0].shape
    row_len = count * len(k_parts)
    heads = group // HEAD_DIM
    tile = pl.BlockSpec((HEAD_DIM, row_len), lambda h: (h, 0))
    whole = pl.BlockSpec((row_len, group), lambda h: (0, 0))
    keys = pl.BlockSpec((count, group), lambda h: (0, 0))
    query = pl.BlockSpec((HEAD_DIM, count), lambda h: (h, 0))
    value = pl.BlockSpec((HEAD_DIM, count), lambda h: (2 * heads + h, 0))
    results = pl.pallas_call(
        functools.partial(attend_kernel, block),
        out_shape=[
            jax.ShapeDtypeStruct((group, row_len), f32),
            jax.ShapeDtypeStruct((heads, 1, row_len), f32),
            jax.ShapeDtypeStruct((row_len, group), bf16),
        ]
        + [jax.ShapeDtypeStruct((group, count), bf16)] * 4,
        grid=(heads,),
        in_specs=[smem_spec()] * 2 + [keys] * 4 + [query] * 4 + [value] * 4,
        out_specs=[tile, pl.BlockSpec((1, 1, row_len), lambda h: (h, 0, 0)), whole] + [query] * 4,
        scratch_shapes=[
            pltpu.VMEM((group, row_len), bf16),
            pltpu.VMEM((HEAD_DIM, row_len), bf16),
            pltpu.VMEM((HEAD_DIM, row_len), bf16),
        ],
        compiler_params=params(60),
        name="attend",
        cost_estimate=cost(0.1),
    )(info, own, *k_parts, *qkv_parts, *qkv_parts)
    return results[0], results[1], results[2], results[3:]


def attend_back_kernel(block, first_head, info_ref, own_ref, k_ref, *refs):
    v_parts, q_parts, kt_parts, g_parts, a_parts = (refs[4 * n : 4 * n + 4] for n in range(5))
    o_ref, log_ref, dqkv_ref, grad_ref = refs[20:24]
    v_buf, q_pad, g_pad, kt_buf, a_buf, dk_acc, dv_acc = refs[24:]
    row_len = k_ref.shape[0]
    head = first_head + pl.program_id(0)
    own_rows = pl.ds(pl.multiple_of(head * HEAD_DIM, HEAD_DIM), HEAD_DIM)
    dk_acc[...] = jnp.zeros_like(dk_acc)
    dv_acc[...] = jnp.zeros_like(dv_acc)
    q_pad[...] = jnp.zeros_like(q_pad)
    g_pad[...] = jnp.zeros_like(g_pad)

    @pl.when(pl.program_id(0) == 0)
    def once():
        gather_blocks(own_ref, v_buf, v_parts, 0)
        gather_blocks(own_ref, a_buf, a_parts, 0)

    gather_blocks(own_ref, q_pad.at[own_rows], q_parts, 1)
    gather_blocks(own_ref, g_pad.at[own_rows], g_parts, 1)
    gather_blocks(own_ref, kt_buf, kt_parts, 1)
    for i in range(row_len // block):
        cols = slice(i * block, (i + 1) * block)
        q, g = q_pad[own_rows, cols], g_pad[own_rows, cols]
        g_wide = g_pad[:, cols]
        delta = jnp.sum(g.astype(f32) * o_ref[:, cols], axis=0, keepdims=True)
        log_total = log_ref[0, :, cols]
        dq = 0.0
        for first, last, s in score_parts(info_ref, k_ref, q_pad[:, cols], block, i, row_len):
            p = jnp.exp(s - log_total)
            dp = mm(v_buf[first:last, :], g_wide)
            ds = (p * (dp - delta)).astype(bf16)
            dv_acc[:, first:last] += mm(g, p.astype(bf16), NT)
            dk_acc[:, first:last] += mm(q, ds, NT)
            dq = dq + mm(kt_buf[:, first:last], ds)
        dqkv_ref[0:HEAD_DIM, cols] = (0.125 * dq).astype(bf16)
    dqkv_ref[HEAD_DIM : 2 * HEAD_DIM, :] = dk_acc[...].astype(bf16)
    dqkv_ref[2 * HEAD_DIM :, :] = dv_acc[...].astype(bf16)
    grad = mm(dqkv_ref[...], a_buf[...])
    rows = grad_ref.shape[2]
    for e in range(grad_ref.shape[1]):
        grad_ref[0, e] = grad[e * rows : (e + 1) * rows, :].astype(bf16)


def attend_back(first, number, pieces, info, own, keys, v_parts, qkv_parts, grads, out, logs, a_parts, block=256):
    row_len, group = keys.shape
    heads = group // HEAD_DIM
    count, width = a_parts[0].shape

    def whole(*shape):
        return pl.BlockSpec(shape, lambda g: (0,) * len(shape))

    def tile(n):
        return pl.BlockSpec((HEAD_DIM, count), lambda g: (n + g, 0))

    return pl.pallas_call(
        functools.partial(attend_back_kernel, block, first),
        out_shape=[
            jax.ShapeDtypeStruct((number * 3 * HEAD_DIM, row_len), bf16),
            jax.ShapeDtypeStruct((number, pieces, 3 * HEAD_DIM // pieces, width), bf16),
        ],
        grid=(number,),
        in_specs=[smem_spec()] * 2
        + [whole(row_len, group)]
        + [whole(count, group)] * 4
        + [tile(first)] * 4
        + [tile(heads + first)] * 4
        + [tile(first)] * 4
        + [whole(count, width)] * 4
        + [
            pl.BlockSpec((HEAD_DIM, row_len), lambda g: (first + g, 0)),
            pl.BlockSpec((1, 1, row_len), lambda g: (first + g, 0, 0)),
        ],
        out_specs=[
            pl.BlockSpec((3 * HEAD_DIM, row_len), lambda g: (g, 0)),
            pl.BlockSpec((1, pieces, 3 * HEAD_DIM // pieces, width), lambda g: (g, 0, 0, 0)),
        ],
        scratch_shapes=[
            pltpu.VMEM((row_len, group), bf16),
            pltpu.VMEM((group, row_len), bf16),
            pltpu.VMEM((group, row_len), bf16),
            pltpu.VMEM((HEAD_DIM, row_len), bf16),
            pltpu.VMEM((row_len, width), bf16),
            pltpu.VMEM((HEAD_DIM, row_len), f32),
            pltpu.VMEM((HEAD_DIM, row_len), f32),
        ],
        compiler_params=params(60),
        name="attend_back",
        cost_estimate=cost(11 * number),
    )(info, own, keys, *v_parts, *qkv_parts, *qkv_parts, *grads, *a_parts, out, logs)


def gates_of(normed, router, route_rows):
    logits = mm(router, normed, NT, precise)
    expert_row = iota(logits.shape, 0)
    picked = [
        jnp.sum(jnp.where(expert_row == row, logits, 0.0), axis=0, keepdims=True)
        for row in route_rows
    ]
    top = jnp.maximum(picked[0], picked[1])
    raw = [jnp.exp(p - top) for p in picked]
    return [r / (raw[0] + raw[1]) for r in raw]


def dispatch_kernel(
    own_ref, t0, t1, t2, t3, x_ref, w_ref, gain_ref, router_ref, routes_ref, hot_a, hot_b,
    residual_ref, gates_ref, send_a, send_b,
):
    residual = x_ref[...].astype(f32)
    group = t0.shape[0]
    for j, part in enumerate((t0, t1, t2, t3)):
        rows = pl.ds(pl.multiple_of((own_ref[0] ^ j) * group, group), group)
        residual = residual + mm(part[...], w_ref[rows, :], TN)
    residual_ref[...] = residual
    scale = lax.rsqrt(jnp.mean(residual * residual, axis=1, keepdims=True) + norm_eps)
    normed = residual * scale * gain_ref[...]
    a_two = normed.astype(bf16)
    route_rows = [routes_ref[k : k + 1, :] for k in range(2)]
    gates = gates_of(normed, router_ref[...], route_rows)
    gates_ref[0:1, :] = gates[0]
    gates_ref[1:2, :] = gates[1]
    experts = router_ref.shape[0]
    expert_row = iota((experts, x_ref.shape[0]), 0)
    table = jnp.where(expert_row == route_rows[0], gates[0], 0.0) + jnp.where(
        expert_row == route_rows[1], gates[1], 0.0
    )
    stacked = jnp.concatenate([piece.astype(f32) for piece in split_three(table)], axis=0)
    stacked = stacked.astype(bf16)
    last = send_b.shape[1] - EXTRA
    for e in range(experts):
        send_b[e, last:, :] = jnp.zeros((EXTRA, send_b.shape[2]), bf16)
    for hot, send, lane in ((hot_a, send_a, 0), (hot_b, send_b, LANE_B)):
        size = hot.shape[0] // experts
        rows = mm(hot[...], a_two).astype(bf16)
        for e in range(experts):
            own_rows = slice(e * size, (e + 1) * size)
            send[e, 0:size, :] = rows[own_rows, :]
            picked = mm(stacked, hot[own_rows, :], NT)
            three = [picked[k * experts + e : k * experts + e + 1, :] for k in range(3)]
            three = jnp.concatenate(three + [jnp.zeros((EXTRA - 3, size), f32)], axis=0)
            send_b[e, last:, lane : lane + size] = three.astype(bf16)


def make_dispatch(own, parts, x, w_out, gain, router_t, routes_t, hots):
    count, width = x.shape
    experts = router_t.shape[0]
    shapes = [
        jax.ShapeDtypeStruct((count, width), f32),
        jax.ShapeDtypeStruct((2, count), f32),
    ]
    sizes = [hot.shape[0] // experts for hot in hots]
    shapes += [
        jax.ShapeDtypeStruct((experts, sizes[0], width), bf16),
        jax.ShapeDtypeStruct((experts, sizes[1] + EXTRA, width), bf16),
    ]
    return pl.pallas_call(
        dispatch_kernel,
        out_shape=shapes,
        in_specs=[smem_spec()] + [vmem_spec()] * 11,
        out_specs=[vmem_spec()] * len(shapes),
        compiler_params=params(60),
        name="project_dispatch",
        cost_estimate=cost(0.1),
    )(own, *parts, x, w_out, gain, router_t, routes_t, *hots)


def column_of(row):
    return jnp.broadcast_to(row, (128, row.shape[1])).T[:, 0:1]


def row_of(column):
    return jnp.broadcast_to(column, (column.shape[0], 128)).T[0:1, :]


GELU_SCALE = 0.7978845608028654
GELU_CUBE = 0.044715


def expert_kernel(half, start, x_ref, dy_ref, *refs):
    weights, refs = refs[:8], refs[8:]
    if half:
        carried_ref, refs = refs[0], refs[2:]
        out_ref, slot_ref, act_ref, dpre_ref = refs[:4]
        refs = refs[4:]
    else:
        out_ref, slot_ref, act_ref, dpre_ref, carry_ref = refs[:5]
        refs = refs[5:]
    x_buf, dy_buf, up_buf, down_buf, out_acc, slot_acc, sems = refs
    sources, width = x_ref.shape[0], x_ref.shape[2]
    size = x_buf.shape[0] // sources
    step = pl.program_id(0)
    parts = len(weights) // 2

    def copies(j):
        return (
            pltpu.make_async_copy(weights[2 * j], up_buf.at[j % 2], sems.at[0, j % 2]),
            pltpu.make_async_copy(weights[2 * j + 1], down_buf.at[j % 2], sems.at[1, j % 2]),
        )

    @pl.when(step == 0)
    def first():
        for copy in copies(0):
            copy.start()
        for n in range(sources):
            x_buf[n * size : (n + 1) * size, :] = x_ref[n, 0:size, :]
            dy_buf[n * size : (n + 1) * size, :] = dy_ref[n, start : start + size, :]
        out_acc[...] = jnp.zeros_like(out_acc)
        slot_acc[...] = jnp.zeros_like(slot_acc)

    for j in range(parts):

        @pl.when(step == j)
        def arrive(j=j):
            if j + 1 < parts:
                for copy in copies(j + 1):
                    copy.start()
            for copy in copies(j):
                copy.wait()

    which = lax.rem(step, 2)
    block = x_buf.shape[0] // 2

    @pl.loop(0, 2)
    def rows_of(r):
        rows = pl.ds(pl.multiple_of(r * block, block), block)
        up, down = up_buf[which], down_buf[which]
        pre = mm(x_buf[rows, :], up)
        square = pre * pre
        tanh = jnp.tanh(GELU_SCALE * (pre * (1.0 + GELU_CUBE * square)))
        half = 0.5 * (1.0 + tanh)
        act = (pre * half).astype(bf16)
        act_ref[0, rows, :] = act
        out_acc[rows, :] += mm(act, down)
        slope = half + (0.5 * GELU_SCALE) * pre * (1.0 - tanh * tanh) * (
            1.0 + (3.0 * GELU_CUBE) * square
        )
        dpre = (mm(dy_buf[rows, :], down, NT) * slope).astype(bf16)
        dpre_ref[0, rows, :] = dpre
        slot_acc[rows, :] += mm(dpre, up, NT)

    @pl.when(step == parts - 1)
    def last():
        for n in range(sources):
            rows = slice(n * size, (n + 1) * size)
            out = out_acc[rows, :].astype(bf16)
            out_ref[n, start : start + size, :] = out
            slot_ref[n, 0:size, :] = slot_acc[rows, :].astype(bf16)
            dgate = jnp.sum(
                dy_buf[rows, :].astype(f32) * out.astype(f32), axis=1, keepdims=True
            )
            three = three_rows(row_of(dgate))
            if half:
                slot_ref[n, size:, :] = jnp.zeros((EXTRA, width), bf16)
                slot_ref[n, size:, 0:LANE_B] = carried_ref[n]
                slot_ref[n, size:, LANE_B : LANE_B + size] = three
            else:
                carry_ref[n] = jnp.zeros((EXTRA, LANE_B), bf16)
                carry_ref[n, :, 0:size] = three


def run_experts(half, start, size, x, dy, weights, before):
    sources, _, width = x.shape
    rows = sources * size
    units = weights[0].shape[1]
    parts = len(weights) // 2

    def whole(shape):
        return pl.BlockSpec(shape, lambda g: (0,) * len(shape), pipeline_mode=pl.Buffered(1))

    def shaped(*shape):
        return jax.ShapeDtypeStruct(shape, bf16)

    kept = shaped(parts, rows, units)
    kept_spec = pl.BlockSpec((1, rows, units), lambda g: (g, 0, 0))
    carry = shaped(sources, EXTRA, LANE_B)
    hbm = pl.BlockSpec(memory_space=pl.ANY)
    piece = pl.BlockSpec((sources, size, width), lambda g: (0, start // size, 0))
    return pl.pallas_call(
        functools.partial(expert_kernel, half, 0),
        out_shape=[shaped(*dy.shape), shaped(*x.shape), kept, kept] + ([] if half else [carry]),
        grid=(parts,),
        in_specs=[whole(x.shape), piece]
        + [hbm] * (2 * parts)
        + ([whole(carry.shape), hbm] if half else []),
        out_specs=[piece, whole(x.shape), kept_spec, kept_spec]
        + ([] if half else [whole(carry.shape)]),
        scratch_shapes=[
            pltpu.VMEM((rows, width), bf16),
            pltpu.VMEM((rows, width), bf16),
            pltpu.VMEM((2, width, units), bf16),
            pltpu.VMEM((2, units, width), bf16),
            pltpu.VMEM((rows, width), f32),
            pltpu.VMEM((rows, width), f32),
            pltpu.SemaphoreType.DMA((2, 2)),
        ],
        input_output_aliases={2 * parts + 3: 0} if half else {},
        compiler_params=params(60),
        name="experts",
        cost_estimate=cost(25),
    )(x, dy, *weights, *((before[4], before[0]) if half else ()))


def weight_kernel(dy_ref, x_a, x_b, act_a, act_b, dpre_a, dpre_b, own_out, near_out, far_up, far_down, x_buf, dy_buf):
    step = pl.program_id(0)
    experts, capacity, _ = dy_ref.shape

    @pl.when(step == 0)
    def gated():
        begin = 0
        halves = zip(halves_of(capacity), (x_a, x_b), (0, LANE_B))
        for (start, size), x_ref, lane in halves:
            for n in range(experts):
                rows = slice(begin, begin + size)
                begin += size
                three = x_b[n, x_b.shape[1] - EXTRA :, lane : lane + size].astype(f32)
                gate = column_of(three[0:1] + three[1:2] + three[2:3])
                x_buf[rows, :] = (x_ref[n, 0:size, :].astype(f32) * gate).astype(bf16)
                dy = dy_ref[n, start : start + size, :].astype(f32)
                dy_buf[rows, :] = (dy * gate).astype(bf16)

    cut = act_a.shape[1]
    up = mm(x_buf[:cut, :], dpre_a[0], TN) + mm(x_buf[cut:, :], dpre_b[0], TN)
    down = mm(act_a[0], dy_buf[:cut, :], TN) + mm(act_b[0], dy_buf[cut:, :], TN)
    for j, (out, n) in enumerate(((own_out, 0), (near_out, 0), (None, 0), (near_out, 2))):

        @pl.when(step == j)
        def keep(out=out, n=n):
            if out is None:
                far_up[...] = up
                far_down[...] = down
            else:
                out[n] = up.astype(out.dtype)
                out[n + 1] = down.astype(out.dtype)


def weight_grads(xs, dy, acts, dpres):
    experts, capacity, width = dy.shape
    parts, _, units = acts[0].shape
    assert units == width

    def whole(*shape):
        return pl.BlockSpec(shape, lambda g: (0,) * len(shape), pipeline_mode=pl.Buffered(1))

    kept = [pl.BlockSpec((1,) + a.shape[1:], lambda g: (g, 0, 0)) for a in (*acts, *dpres)]
    return pl.pallas_call(
        weight_kernel,
        out_shape=[
            jax.ShapeDtypeStruct((2, width, units), f32),
            jax.ShapeDtypeStruct((4, width, units), bf16),
            jax.ShapeDtypeStruct((width, units), f32),
            jax.ShapeDtypeStruct((units, width), f32),
        ],
        grid=(parts,),
        in_specs=[whole(*dy.shape)] + [whole(*x.shape) for x in xs] + kept,
        out_specs=[whole(2, width, units), whole(4, width, units)] + [whole(width, units)] * 2,
        scratch_shapes=[pltpu.VMEM((experts * capacity, width), bf16)] * 2,
        compiler_params=params(60),
        name="expert_weight_grads",
        cost_estimate=cost(25),
    )(dy, *xs, *acts, *dpres)


def combine_back_kernel(
    own_ref, hot_a, hot_b, p0a, p1a, p0b, p1b, residual_ref, dy_ref, gates_ref, routes_ref,
    router_ref, gain_ref, w_ref, slot_a, slot_b,
    dres_ref, branch_ref, small_ref, g0, g1, g2, g3, buf_a, buf_b, datt_buf,
):
    experts = router_ref.shape[0]
    table = [0.0] * experts
    last = slot_b.shape[1] - EXTRA
    for slot, hot, buf, lane in ((slot_a, hot_a, buf_a, 0), (slot_b, hot_b, buf_b, LANE_B)):
        size = hot.shape[0] // experts
        for e in range(experts):
            rows = slice(e * size, (e + 1) * size)
            buf[rows, :] = slot[e, 0:size, :]
            picked = mm(slot_b[e, last:, lane : lane + size], hot[rows, :])
            table[e] = table[e] + (picked[0:1] + picked[1:2] + picked[2:3])
    table = jnp.concatenate(table, axis=0)
    residual = residual_ref[...]
    count = residual.shape[0]
    scale = lax.rsqrt(jnp.mean(residual * residual, axis=1, keepdims=True) + norm_eps)
    unit = residual * scale
    gain = gain_ref[...]
    expert_row = iota((experts, count), 0)
    routes = [routes_ref[k : k + 1, :] for k in range(2)]
    gates = [gates_ref[k : k + 1, :] for k in range(2)]
    dgates = [
        jnp.sum(jnp.where(expert_row == r, table, 0.0), axis=0, keepdims=True) for r in routes
    ]
    mean = gates[0] * dgates[0] + gates[1] * dgates[1]
    dlogit = sum(
        jnp.where(expert_row == r, g * (d - mean), 0.0) for r, g, d in zip(routes, gates, dgates)
    )
    small_ref[...] = jnp.zeros_like(small_ref)
    small_ref[0:experts, :] = mm(dlogit, unit * gain, precision=precise)
    dnormed = mm(dlogit, router_ref[...], TN, precise)
    for gate, pick_a, pick_b in ((gates[0], p0a, p0b), (gates[1], p1a, p1b)):
        rows = mm(pick_a[...], buf_a[...]) + mm(pick_b[...], buf_b[...])
        dnormed = dnormed + column_of(gate) * rows
    small_ref[experts : experts + 1, :] = jnp.sum(dnormed * unit, axis=0, keepdims=True)
    scaled = dnormed * gain
    dres = dy_ref[...].astype(f32) + scale * (
        scaled - unit * jnp.mean(scaled * unit, axis=1, keepdims=True)
    )
    dres_ref[...] = dres
    branch = dres.astype(bf16)
    branch_ref[...] = branch
    datt_buf[...] = mm(w_ref[...], branch, NT).astype(bf16)
    for j, piece in enumerate((g0, g1, g2, g3)):
        size = piece.shape[0]
        piece[...] = datt_buf[pl.ds(pl.multiple_of((own_ref[0] ^ j) * size, size), size), :]


def combine_back(own, slots, hots, picks, residual, dy, gates, routes_t, router_t, gain, w_out):
    count, width = residual.shape
    experts = router_t.shape[0]
    shapes = [
        jax.ShapeDtypeStruct((count, width), f32),
        jax.ShapeDtypeStruct((count, width), bf16),
        jax.ShapeDtypeStruct((experts + 8, width), f32),
    ] + [jax.ShapeDtypeStruct((width // 4, count), bf16)] * 4
    results = pl.pallas_call(
        combine_back_kernel,
        out_shape=shapes,
        in_specs=[smem_spec()] + [vmem_spec()] * 15,
        out_specs=[vmem_spec()] * len(shapes),
        scratch_shapes=[pltpu.VMEM((hot.shape[0], width), bf16) for hot in hots]
        + [pltpu.VMEM((width, count), bf16)],
        compiler_params=params(60),
        name="combine_back",
        cost_estimate=cost(11),
    )(own, *hots, *picks, residual, dy, gates, routes_t, router_t, gain, w_out, *slots)
    return results[0], results[1], results[2], results[3:]


def out_grad_kernel(t0, t1, t2, t3, branch_ref, keep_ref, give_ref):
    branch = branch_ref[...]
    keep_ref[0] = mm(t0[...], branch)
    keep_ref[1] = mm(t2[...], branch)
    give_ref[0] = mm(t1[...], branch).astype(bf16)
    give_ref[1] = mm(t3[...], branch).astype(bf16)


def out_grads(parts, branch):
    shape = (2, parts[0].shape[0], branch.shape[1])
    return pl.pallas_call(
        out_grad_kernel,
        out_shape=[jax.ShapeDtypeStruct(shape, f32), jax.ShapeDtypeStruct(shape, bf16)],
        in_specs=[vmem_spec()] * 5,
        out_specs=[vmem_spec()] * 2,
        compiler_params=params(60),
        name="w_out_grads",
        cost_estimate=cost(3),
    )(*parts, branch)


def combine_kernel(p0a, p1a, p0b, p1b, residual_ref, gates_ref, out_ref, y_ref, buf_a, buf_b):
    experts, capacity, _ = out_ref.shape
    for (start, size), buf in zip(halves_of(capacity), (buf_a, buf_b)):
        for e in range(experts):
            buf[e * size : (e + 1) * size, :] = out_ref[e, start : start + size, :]
    total = residual_ref[...]
    for k, (pick_a, pick_b) in enumerate(((p0a, p0b), (p1a, p1b))):
        rows = mm(pick_a[...], buf_a[...]) + mm(pick_b[...], buf_b[...])
        total = total + column_of(gates_ref[k : k + 1, :]) * rows
    y_ref[...] = total.astype(bf16)


def combine(out, picks, residual, gates):
    experts, capacity, width = out.shape
    return pl.pallas_call(
        combine_kernel,
        out_shape=jax.ShapeDtypeStruct(residual.shape, bf16),
        in_specs=[vmem_spec()] * 7,
        out_specs=vmem_spec(),
        scratch_shapes=[
            pltpu.VMEM((experts * size, width), bf16) for _, size in halves_of(capacity)
        ],
        compiler_params=params(60),
        name="combine",
        cost_estimate=cost(6),
    )(*picks, residual, gates, out)


def spread_kernel(places_ref, d01, d2, w_ref, near_out, last_out, far_out, own_out, d_buf):
    step = pl.program_id(0)
    heads = d_buf.shape[0] // (3 * HEAD_DIM)
    for c, (part, n) in enumerate(((d01, 0), (d01, 3), (d2, 0))):
        for t in range(3):
            start = (t * heads + c) * HEAD_DIM
            d_buf[start : start + HEAD_DIM, :] = part[(n + t) * HEAD_DIM : (n + t + 1) * HEAD_DIM, :]
    dn = mm(d_buf[...], w_ref[...], TN)
    for n, out in enumerate((near_out, last_out, far_out, own_out)):

        @pl.when(step == n)
        def keep(out=out):
            out[...] = dn.astype(out.dtype)


def spread(places, parts, w_t):
    row_len = parts[0].shape[1]
    cols, width = w_t.shape
    steps = places.shape[0]
    count = row_len // steps
    tiles = [pl.BlockSpec((p.shape[0], count), lambda g, places: (0, places[g])) for p in parts]

    def whole(shape):
        return pl.BlockSpec(shape, lambda g, places: (0, 0), pipeline_mode=pl.Buffered(1))

    return pl.pallas_call(
        spread_kernel,
        out_shape=[jax.ShapeDtypeStruct((count, width), t) for t in (bf16, bf16, f32, f32)],
        grid_spec=pltpu.PrefetchScalarGridSpec(
            num_scalar_prefetch=1,
            grid=(steps,),
            in_specs=tiles + [whole((cols, width))],
            out_specs=[whole((count, width))] * 4,
            scratch_shapes=[pltpu.VMEM((cols, count), bf16)],
        ),
        compiler_params=params(40),
        name="spread_back",
        cost_estimate=cost(8),
    )(places, *parts, w_t)


def pack_kernel(special, g_ref, keep_ref, near_ref, far_ref, small_ref, out_ref):
    exps, _, width = out_ref.shape
    rows = g_ref.shape[2]
    gout = keep_ref[0] + near_ref[0].astype(f32) + far_ref[...].astype(f32)
    out_rows = gout.shape[0] // exps
    begin = 2 * rows + out_rows
    pad = out_ref.shape[1] - begin - 2 * special
    for e in range(exps):
        out_ref[e, 0:rows] = g_ref[0, e]
        out_ref[e, rows : 2 * rows] = g_ref[1, e]
        high, mid, _ = split_three(small_ref[e * special : (e + 1) * special, :])
        parts = [gout[e * out_rows : (e + 1) * out_rows], high.astype(f32), mid.astype(f32)]
        if pad:
            parts.append(jnp.zeros((pad, width), f32))
        out_ref[e, 2 * rows :] = jnp.concatenate(parts, axis=0).astype(bf16)


def pack(grads, keep, near, far, small, special):
    _, exps, rows, width = grads.shape
    total = 2 * rows + keep.shape[1] // exps + 2 * special
    return pl.pallas_call(
        functools.partial(pack_kernel, special),
        out_shape=jax.ShapeDtypeStruct((exps, total + -total % 8, width), bf16),
        in_specs=[vmem_spec()] * 5,
        out_specs=vmem_spec(),
        compiler_params=params(50),
        name="pack_sums",
        cost_estimate=cost(2),
    )(grads, keep, near, far, small)


def fold_kernel(special, taken, moved_ref, *refs):
    given, out_ref = refs[:-1], refs[-1]
    exps, rows, width = out_ref.shape
    sums = moved_ref[0, 0:taken].astype(f32)
    for e in range(1, exps):
        sums = sums + moved_ref[e, 0:taken].astype(f32)
    if special:
        body = taken - 2 * special
        high, mid, _ = split_three(
            sums[body : body + special] + sums[body + special : body + 2 * special]
        )
        sums = jnp.concatenate([sums[:body], high.astype(f32), mid.astype(f32)], axis=0)
    start = given[0].shape[1] if given else 0
    pad = rows - start - taken
    if pad:
        sums = jnp.concatenate([sums, jnp.zeros((pad, width), f32)], axis=0)
    sums = sums.astype(bf16)
    for e in range(exps):
        if given:
            out_ref[e, 0:start] = given[0][e]
        out_ref[e, start:] = sums


def fold(moved, taken, special, given=()):
    exps, _, width = moved.shape
    rows = taken + sum(g.shape[1] for g in given)
    return pl.pallas_call(
        functools.partial(fold_kernel, special, taken),
        out_shape=jax.ShapeDtypeStruct((exps, rows + -rows % 8, width), bf16),
        in_specs=[vmem_spec()] * (1 + len(given)),
        out_specs=vmem_spec(),
        compiler_params=params(40),
        name="fold_sums",
        cost_estimate=cost(2),
    )(moved, *given)


def lay_out_kernel(rows, own_ref, *refs):
    arrays, (w_ref, gain_ref, grad_ref, ggain_ref, b0, b1, sems) = refs[:8], refs[8:]
    hids, exps = b0.shape[0], b0.shape[1]
    step = pl.program_id(0)
    block = grad_ref.shape[0]

    @pl.when(step == 0)
    def fetch():
        copies = [
            pltpu.make_async_copy(arrays[4 * c + j], buf.at[own_ref[0] ^ j], sems.at[c, j])
            for c, buf in enumerate((b0, b1))
            for j in range(hids)
        ]
        for copy in copies:
            copy.start()
        for copy in copies:
            copy.wait()

    cols = pl.ds(pl.multiple_of(step * block, block), block)
    blocks = {}
    for h in range(hids):
        for c, (buf, start) in enumerate(((b0, 0), (b0, rows), (b1, 0))):
            pieces = [buf[h, e, start : start + rows, cols].astype(f32) for e in range(exps)]
            blocks[h, c] = jnp.concatenate(pieces, axis=0)
    stacked = [
        blocks[h, c][t * HEAD_DIM : (t + 1) * HEAD_DIM]
        for t in range(3)
        for h in range(hids)
        for c in range(3)
    ]
    grad = jnp.concatenate(stacked, axis=0).T
    grad_ref[...] = grad
    total = jnp.sum(grad * w_ref[...].astype(f32), axis=1, keepdims=True)
    ggain_ref[...] = row_of(total) / gain_ref[...]


def lay_out(own, chunks, rows, w_qkv, gain, block=128):
    width, cols = w_qkv.shape
    arrays = [a for chunk in chunks for a in chunk]
    tile = pl.BlockSpec((block, cols), lambda g: (g, 0))
    row = pl.BlockSpec((1, block), lambda g: (0, g))
    return pl.pallas_call(
        functools.partial(lay_out_kernel, rows),
        out_shape=[
            jax.ShapeDtypeStruct((width, cols), f32),
            jax.ShapeDtypeStruct((1, width), f32),
        ],
        grid=(width // block,),
        in_specs=[smem_spec()] + [pl.BlockSpec(memory_space=pl.ANY)] * 8 + [tile, row],
        out_specs=[tile, row],
        scratch_shapes=[pltpu.VMEM((4,) + chunk[0].shape, bf16) for chunk in chunks]
        + [pltpu.SemaphoreType.DMA((2, 4))],
        compiler_params=params(50),
        name="lay_out_qkv",
        cost_estimate=cost(10),
    )(own, *arrays, w_qkv, gain)


def lay_out_rest_kernel(start, own_ref, *refs):
    arrays, (out_ref, buf, sems) = refs[:4], refs[4:]
    hids, exps = buf.shape[0], buf.shape[1]
    rows = out_ref.shape[0] // (hids * exps)
    copies = [
        pltpu.make_async_copy(arrays[j], buf.at[own_ref[0] ^ j], sems.at[j]) for j in range(hids)
    ]
    for copy in copies:
        copy.start()
    for copy in copies:
        copy.wait()
    for h in range(hids):
        for e in range(exps):
            n = h * exps + e
            out_ref[n * rows : (n + 1) * rows, :] = buf[h, e, start : start + rows].astype(f32)


def lay_out_rest(own, arrays, start, width):
    return pl.pallas_call(
        functools.partial(lay_out_rest_kernel, start),
        out_shape=jax.ShapeDtypeStruct((width, width), f32),
        in_specs=[smem_spec()] + [pl.BlockSpec(memory_space=pl.ANY)] * 4,
        out_specs=vmem_spec(),
        scratch_shapes=[pltpu.VMEM((4,) + arrays[0].shape, bf16), pltpu.SemaphoreType.DMA((4,))],
        compiler_params=params(50),
        name="lay_out_w_out",
        cost_estimate=cost(3),
    )(own, *arrays)


def adam_update(weight, gradient, first_moment, second_moment, live_mask):
    first_next = beta_one * first_moment + (1.0 - beta_one) * gradient
    second_next = beta_two * second_moment + (1.0 - beta_two) * gradient * gradient
    first_hat = first_next / (1.0 - beta_one**adam_steps)
    second_hat = second_next / (1.0 - beta_two**adam_steps)
    weight_next = weight - learn_rate * first_hat / (jnp.sqrt(second_hat) + adam_eps)
    return (
        jnp.where(live_mask, weight_next, weight),
        jnp.where(live_mask, first_next, first_moment),
        jnp.where(live_mask, second_next, second_moment),
    )


def expert_update_kernel(live_ref, own_ref, near_ref, far_ref, weight_ref, first_ref, second_ref, *outs):
    live = live_ref[0] > 0
    grad = own_ref[0] + near_ref[0].astype(f32) + far_ref[...].astype(f32)
    grad = jnp.where(live, grad, 0.0)
    outs[0][...] = grad
    updated = adam_update(weight_ref[...], grad, first_ref[...], second_ref[...], live)
    for out, value in zip(outs[1:], updated):
        out[...] = value


def expert_update(live, own, near, number, far, weight, first_moment, second_moment, block=128):
    tile = pl.BlockSpec((block, weight.shape[1]), lambda g: (g, 0))
    stacked = pl.BlockSpec((1, block, weight.shape[1]), lambda g: (number, g, 0))
    return pl.pallas_call(
        expert_update_kernel,
        out_shape=[jax.ShapeDtypeStruct(weight.shape, f32)] * 4,
        grid=(weight.shape[0] // block,),
        in_specs=[smem_spec(), stacked, stacked] + [tile] * 4,
        out_specs=[tile] * 4,
        compiler_params=params(60),
        name="expert_update",
        cost_estimate=cost(8),
    )(live, own, near, far, weight, first_moment, second_moment)


def tie(value, other):
    return lax.optimization_barrier((value, other))[0]


def exchange(value, axis):
    return lax.all_to_all(value, axis, split_axis=0, concat_axis=0, tiled=True)


def split_sum(value, axis, distance):
    pairs = value.reshape((value.shape[0] // 2, 2) + value.shape[1:])
    low = (lax.axis_index(axis) & distance) == 0
    keep = jnp.where(low, pairs[:, 0], pairs[:, 1])
    give = jnp.where(low, pairs[:, 1], pairs[:, 0]).astype(bf16)
    return keep + swap(give, axis, distance).astype(f32)


def halves(value):
    high = lax.reduce_precision(value, 8, 7)
    return high.astype(bf16), (value - high).astype(bf16)


def pad_rows(value):
    return jnp.pad(value, ((0, 0), (0, -value.shape[1] % 8), (0, 0)))


def gather_hid(value):
    far = swap(value, "hid", 2)
    near = swap(value, "hid", 1)
    return value, near, far, swap(far, "hid", 1)


def body(
    tokens, cotangent, routes, segments, lengths, gain_attn, gain_moe, w_qkv, w_out, router_w,
    router_first, router_second, up_w, down_w, up_first, up_second, down_first, down_second,
):
    exp_count = lax.axis_size("exp")
    hid_count = lax.axis_size("hid")
    hid = lax.axis_index("hid")
    exp_index = lax.axis_index("exp")
    own = jnp.stack([hid, exp_index]).astype(jnp.int32)
    x_own = tokens[0]
    dy = cotangent[0]
    count, width = x_own.shape
    experts = router_w.shape[1]
    frozen_count = experts // 2
    capacity = max(2, 3 * count // experts)
    group = width // hid_count
    heads = group // HEAD_DIM
    is_new = exp_index >= frozen_count

    x_halves = [x_own[: count // 2], x_own[count // 2 :]]
    x_far = [swap(half, "hid", 2) for half in x_halves]
    x_near = swap(x_own, "hid", 1)
    routes_t = routes[0].T
    hots, picks, dy_send = make_tables(routes_t, dy, experts, capacity)
    seg_row = segments[0]
    info = jnp.stack(
        [
            jnp.sum((seg_row < 1).astype(jnp.int32)),
            jnp.sum((seg_row < 2).astype(jnp.int32)),
            lengths[0],
        ]
    )
    up_low = up_w[0].astype(bf16)
    down_low = down_w[0].astype(bf16)
    router_t = router_w.T
    first = project_qkv(own, (x_own, x_near), gain_attn[None], w_qkv)
    x_far, (info, dy_send, up_low, down_low, router_t, routes_t) = lax.optimization_barrier(
        (x_far, (info, dy_send, up_low, down_low, router_t, routes_t))
    )
    x_last = [swap(half, "hid", 1) for half in x_far]
    dy_all = exchange(dy_send, "exp")

    up_far = swap(up_low, "hid", 2)
    up_near, down_near = (swap(tie(low, x_last), "hid", 1) for low in (up_low, down_low))

    second = project_qkv(own, (*x_far, *x_last), gain_attn[None], w_qkv)
    w_t = first[8]
    a_parts, qkv_parts, k_parts, v_parts = (
        (*first[n : n + 2], *second[n : n + 2]) for n in (0, 2, 4, 6)
    )
    out_heads, logs, keys, pieces = attend(info, own, k_parts, qkv_parts)
    pieces, (up_far, up_near, down_near) = lax.optimization_barrier(
        (pieces, (up_far, up_near, down_near))
    )
    att_parts = [pieces[0]] + [swap(pieces[j], "hid", j) for j in range(1, hid_count)]
    att_parts, down_low = lax.optimization_barrier((att_parts, down_low))
    down_far = swap(down_low, "hid", 2)

    residual, gates, *sends = make_dispatch(
        own, att_parts, x_own, w_out, gain_moe[None], router_t, routes_t, hots
    )
    up_far, down_far = tie((up_far, down_far), residual)
    up_last, down_last = swap(up_far, "hid", 1), swap(down_far, "hid", 1)
    weights = (up_low, down_low, up_near, down_near, up_far, down_far, up_last, down_last)
    sends = tie(sends, dy_all)
    x_rows = [exchange(send, "exp") for send in sends]

    results = [None]
    for half, ((start, size), x) in enumerate(zip(halves_of(capacity), x_rows)):
        results.append(run_experts(half, start, size, x, dy_all, weights, results[-1]))
    outs = results[2][0]
    slots, acts, dpres = ([r[n] for r in results[1:]] for n in (1, 2, 3))
    slot_back = [exchange(slot, "exp") for slot in slots]

    own_part, near_part, far_up, far_down = weight_grads(x_rows, dy_all, acts, dpres)
    slot_back, near_part = lax.optimization_barrier((slot_back, near_part))
    near_part = swap(near_part, "hid", 1)

    dres, branch, small, datt_parts = combine_back(
        own, slot_back, hots, picks, residual, dy, gates, routes_t, router_t, gain_moe[None], w_out
    )
    out_back = exchange(tie(outs, slot_back), "exp")
    datt_parts, near_part = lax.optimization_barrier((datt_parts, near_part))
    datt_parts = [datt_parts[0]] + [swap(datt_parts[j], "hid", j) for j in range(1, hid_count)]
    gout, gout_near = out_grads(att_parts, branch)

    out_rows = width // (hid_count * exp_count)
    small_rows = -(-(experts + 1) // exp_count)
    missing = max(0, exp_count * small_rows - small.shape[0])
    small = jnp.pad(small, ((0, missing), (0, 0)))
    gout_near = swap(gout_near, "hid", 1)
    small = small + swap(small, "hid", 1)
    far_up = (far_up + near_part[2].astype(f32)).astype(bf16)
    far_down = (far_down + near_part[3].astype(f32)).astype(bf16)
    far_up, far_down = tie((far_up, far_down), datt_parts)
    far_up = swap(far_up, "hid", 2)
    rows = 3 * HEAD_DIM // exp_count
    given = (info, own, keys, v_parts, qkv_parts, datt_parts, out_heads, logs, a_parts)
    dqkv_first, grads_first = attend_back(0, heads - 1, exp_count, *given)
    gout_near, small = tie((gout_near, small), dqkv_first)
    small = small + swap(small, "hid", 2)
    gout_far = swap((gout[1] + gout_near[1].astype(f32)).astype(bf16), "hid", 2)
    packed = pack(grads_first, gout, gout_near, gout_far, small, small_rows)
    packed, out_back, far_up = lax.optimization_barrier((packed, out_back, far_up))
    far_down = swap(tie(far_down, (gout_far, small)), "hid", 2)
    first = exchange(packed, "exp")
    dqkv_last, grads_last = attend_back(heads - 1, 1, exp_count, *given)
    dqkv = [dqkv_first, dqkv_last]
    first_rows = 2 * rows + out_rows + 2 * small_rows

    first_sums = fold(first, first_rows, small_rows, [grads_last[0]])
    second = exchange(first_sums, "exp")

    dqkv, far_down = tie((dqkv, far_down), first_sums)
    places = jnp.stack([hid ^ j for j in (1, 3, 2, 0)]).astype(jnp.int32)
    near_dn, last_dn, far_dn, own_dn = spread(places, dqkv, w_t)
    near_dn, last_dn = swap(near_dn, "hid", 1), swap(last_dn, "hid", 1)
    far_dn = (far_dn + last_dn.astype(f32)).astype(bf16)
    out_back, far_up = tie((out_back, far_up), far_dn)
    far_dn = swap(far_dn, "hid", 2)
    start = 3 * rows + out_rows
    small = second[:, start : start + small_rows].astype(f32)
    small = small + second[:, start + small_rows : start + 2 * small_rows].astype(f32)
    small = small.reshape(exp_count * small_rows, width)

    out_tokens = combine(out_back, picks, residual, gates)
    live = is_new.astype(jnp.int32).reshape(1)
    grad_up, up_next, up_first_next, up_second_next = expert_update(
        live, own_part, near_part, 0, far_up, up_w[0], up_first[0], up_second[0]
    )
    second, out_tokens, up_next = lax.optimization_barrier((second, out_tokens, up_next))
    last_sums = fold(second, rows, 0)
    far_dn, far_down = tie((far_dn, far_down), last_sums)
    dnormed = own_dn + near_dn.astype(f32) + far_dn.astype(f32)
    x = x_own.astype(f32)
    scale = lax.rsqrt(jnp.mean(x * x, axis=-1, keepdims=True) + norm_eps)
    unit = x * scale
    scaled = dnormed * gain_attn
    grad_tokens = (
        dres + scale * (scaled - unit * jnp.mean(scaled * unit, axis=-1, keepdims=True))
    ).astype(bf16)
    third = exchange(last_sums, "exp")
    gathered = gather_hid(second[:, rows:start])
    grad_down = own_part[1] + near_part[1].astype(f32) + far_down.astype(f32)
    grad_down = jnp.where(is_new, grad_down, 0.0)
    down_next, down_first_next, down_second_next = adam_update(
        down_w[0], grad_down, down_first[0], down_second[0], is_new
    )
    grad_out_proj = lay_out_rest(own, gathered, 2 * rows, width)
    grad_gain_moe = small[experts]
    live_columns = (jnp.arange(experts, dtype=jnp.int32) >= frozen_count)[None, :]
    grad_router = jnp.where(live_columns, small[:experts].T, 0.0)
    router_new, router_first_next, router_second_next = adam_update(
        router_w[:, frozen_count:], grad_router[:, frozen_count:], router_first, router_second, True
    )
    router_next = jnp.concatenate([router_w[:, :frozen_count], router_new], axis=1)
    near, far = swap(third, "hid", 1), swap(third, "hid", 2)
    ready = (grad_out_proj, grad_router, router_next, router_first_next, router_second_next)
    far, ready = lax.optimization_barrier((far, ready))
    grad_out_proj, grad_router, router_next, router_first_next, router_second_next = ready
    gathered = (gathered, (third, near, far, swap(far, "hid", 1)))
    grad_qkv, grad_gain_attn = lay_out(own, gathered, rows, w_qkv, gain_attn[None])
    grad_gain_attn = grad_gain_attn[0]
    return (
        out_tokens[None],
        grad_tokens[None],
        grad_qkv,
        grad_out_proj,
        grad_gain_attn,
        grad_gain_moe,
        grad_router,
        router_next,
        router_first_next,
        router_second_next,
        grad_up[None],
        grad_down[None],
        up_next[None],
        down_next[None],
        up_first_next[None],
        up_second_next[None],
        down_first_next[None],
        down_second_next[None],
    )


def solution(mesh):
    tok = P("exp", "hid", None)
    up = P("exp", None, "hid")
    return jax.shard_map(
        body,
        mesh=mesh,
        in_specs=(tok, tok, tok, P("exp", None), P("exp")) + (P(),) * 7
        + (up, tok, up, up, tok, tok),
        out_specs=(tok, tok) + (P(),) * 8 + (up, tok, up, tok, up, up, tok, tok),
        check_vma=False,
    )
```

```python
import functools

import jax
import jax.numpy as jnp
from jax import lax
from jax.experimental import pallas as pl
from jax.experimental.pallas import tpu as pltpu
from jax.sharding import PartitionSpec as P

HEADS = 12
HEAD_DIM = 64

precise = lax.Precision.HIGHEST
norm_eps = 1e-06
beta_one = 0.9
beta_two = 0.999
learn_rate = 0.01
adam_eps = 1e-08
adam_steps = 10.0
masked_score = -1e30

bf16 = jnp.bfloat16
f32 = jnp.float32
MIB = 1 << 20
COST_SCALE = 0.1


def mm(left, right, contract=((1,), (0,)), precision=None):
    return lax.dot_general(
        left, right, (contract, ((), ())), preferred_element_type=f32, precision=precision
    )


NT = ((1,), (1,))
TN = ((0,), (0,))


def swap(value, axis, distance):
    count = lax.axis_size(axis)
    return lax.ppermute(value, axis, [(i, i ^ distance) for i in range(count)])


def iota(shape, dim):
    return lax.broadcasted_iota(jnp.int32, shape, dim)


def split_three(value):
    high = value.astype(bf16)
    rest = value - high.astype(f32)
    mid = rest.astype(bf16)
    low = (rest - mid.astype(f32)).astype(bf16)
    return high, mid, low


EXTRA = 8
LANE_B = 128


def three_rows(row):
    high, mid, low = (piece.astype(f32) for piece in split_three(row))
    return jnp.concatenate([high, mid, low, jnp.zeros((EXTRA - 3, row.shape[1]), f32)], axis=0).astype(bf16)


def vmem_spec():
    return pl.BlockSpec(memory_space=pltpu.VMEM)


def smem_spec():
    return pl.BlockSpec(memory_space=pltpu.SMEM)


def params(mib):
    return pltpu.CompilerParams(vmem_limit_bytes=mib * MIB)


def cost(micros):
    micros = micros * COST_SCALE
    return pl.CostEstimate(
        flops=int(micros * 1.1e9), bytes_accessed=int(micros * 3e6), transcendentals=0
    )


def halves_of(capacity):
    first = (capacity // 2 + 15) // 16 * 16
    return ((0, first), (first, capacity - first))


def tables_kernel(routes_ref, dy_ref, hot_a, hot_b, *outs):
    picks, send_ref = outs[:4], outs[4]
    experts, capacity, _ = send_ref.shape
    count = routes_ref.shape[1]
    expert_row = iota((experts, count), 0)
    route_rows = [routes_ref[k : k + 1, :] for k in range(2)]
    hits = [expert_row == row for row in route_rows]
    hit = hits[0] | hits[1]
    hit_low = jnp.where(hit, 1.0, 0.0).astype(bf16)
    upper = jnp.where(iota((count, count), 0) < iota((count, count), 1), 1.0, 0.0).astype(bf16)
    slot = mm(hit_low, upper)
    slot = jnp.where(hit & (slot < capacity), slot, -1.0)
    index_rows = []
    for (start, size), hot in zip(halves_of(capacity), (hot_a, hot_b)):
        row_id = iota((size, count), 0).astype(f32) + float(start)
        for e in range(experts):
            hot[e * size : (e + 1) * size, :] = jnp.where(
                row_id == slot[e : e + 1, :], 1.0, 0.0
            ).astype(bf16)
        rows = mm(hot[...], dy_ref[...]).astype(bf16)
        for e in range(experts):
            send_ref[e, start : start + size, :] = rows[e * size : (e + 1) * size, :]
        for k in range(2):
            own_slot = jnp.sum(jnp.where(hits[k], slot, 0.0), axis=0, keepdims=True)
            inside = (own_slot >= start) & (own_slot < start + size)
            place = route_rows[k].astype(f32) * size + own_slot - start
            index_rows.append(jnp.where(inside, place, -1.0))
    index_cols = jnp.concatenate(index_rows * 2, axis=0).T
    for n, pick in enumerate(picks):
        lane = iota(pick.shape, 1).astype(f32)
        pick[...] = jnp.where(lane == index_cols[:, n : n + 1], 1.0, 0.0).astype(bf16)


def make_tables(routes_t, dy, experts, capacity):
    count, width = dy.shape
    sizes = [experts * size for _, size in halves_of(capacity)]
    shapes = [jax.ShapeDtypeStruct((size, count), bf16) for size in sizes]
    shapes += [jax.ShapeDtypeStruct((count, size), bf16) for size in sizes for _ in range(2)]
    shapes += [jax.ShapeDtypeStruct((experts, capacity, width), bf16)]
    results = pl.pallas_call(
        tables_kernel,
        out_shape=shapes,
        in_specs=[vmem_spec()] * 2,
        out_specs=[vmem_spec()] * len(shapes),
        compiler_params=params(60),
        name="slot_tables",
        cost_estimate=cost(0.1),
    )(routes_t, dy)
    return results[0:2], results[2:6], results[6]


def qkv_kernel(
    pieces, own_ref, *refs
):
    blocks, refs = refs[: 2 * pieces], refs[2 * pieces :]
    gain_ref, w_ref, a0, a1, q0, q1, k0, k1, v0, v1, w_buf, heads_ref = refs
    width, cols = heads_ref.shape
    third = cols // 3
    for h in range(width // third):

        @pl.when(own_ref[0] == h)
        def pick(h=h):
            for t in range(3):
                start = t * width + h * third
                heads_ref[:, t * third : (t + 1) * third] = w_ref[:, start : start + third]

    w_buf[...] = heads_ref[...].T
    outs = ((a0, q0, k0, v0), (a1, q1, k1, v1))
    for n, (a_ref, qkv_ref, k_ref, v_ref) in enumerate(outs):
        x = [x_ref[...] for x_ref in blocks[n * pieces : (n + 1) * pieces]]
        x = jnp.concatenate(x, axis=0).astype(f32)
        scale = lax.rsqrt(jnp.mean(x * x, axis=1, keepdims=True) + norm_eps)
        a = (x * scale * gain_ref[...]).astype(bf16)
        a_ref[...] = a
        qkv_t = mm(w_buf[...], a, NT).astype(bf16)
        qkv_ref[0:third, :] = qkv_t[0:third, :] * jnp.asarray(0.125, bf16)
        qkv_ref[third:, :] = qkv_t[third:, :]
        both = mm(a, heads_ref[:, third:]).astype(bf16)
        k_ref[...] = both[:, :third]
        v_ref[...] = both[:, third:]


def project_qkv(own, blocks, gain, w_qkv):
    pieces = len(blocks) // 2
    count, width = pieces * blocks[0].shape[0], blocks[0].shape[1]
    cols = w_qkv.shape[1] // 4
    third = cols // 3
    shapes = [(count, width)] * 2 + [(cols, count)] * 2 + [(count, third)] * 4 + [(cols, width)]
    return pl.pallas_call(
        functools.partial(qkv_kernel, pieces),
        out_shape=[jax.ShapeDtypeStruct(shape, bf16) for shape in shapes],
        in_specs=[smem_spec()] + [vmem_spec()] * (2 * pieces + 2),
        out_specs=[vmem_spec()] * 9,
        scratch_shapes=[pltpu.VMEM((width, cols), bf16)],
        compiler_params=params(60),
        name="norm_qkv",
        cost_estimate=cost(0.1),
    )(own, *blocks, gain, w_qkv)


EDGE = 256


def query_rows(info_ref, query_start, size):
    query_row = query_start + iota((1, size), 1)
    first_cut, last_cut, length = info_ref[0], info_ref[1], info_ref[2]
    start_row = jnp.where(
        query_row >= last_cut, last_cut, jnp.where(query_row >= first_cut, first_cut, 0)
    )
    last_row = jnp.minimum(query_row, length - 1)
    return query_row, start_row, last_row


def score_parts(info_ref, keys_ref, queries, block, number, row_len):
    query_start = number * block
    query_row, start_row, last_row = query_rows(info_ref, query_start, block)
    free_from = query_start if query_start + block > row_len - EDGE else min(EDGE, query_start)
    parts = []
    for first, last in ((0, free_from), (free_from, query_start), (query_start, query_start + block)):
        if first == last:
            continue
        scores = mm(keys_ref[first:last, :], queries)
        key_col = first + iota(scores.shape, 0)
        if first == query_start:
            valid = (key_col >= start_row) & (key_col <= last_row) | (key_col == query_row)
            scores = jnp.where(valid, scores, masked_score)
        elif last == free_from:
            scores = jnp.where(key_col >= start_row, scores, masked_score)
        parts.append((first, last, scores))
    return parts


def gather_blocks(own_ref, buf, parts, axis):
    for j, part in enumerate(parts):
        size = part.shape[axis]
        where = pl.ds(pl.multiple_of((own_ref[0] ^ j) * size, size), size)
        if axis:
            buf[:, where] = part[...]
        else:
            buf[where, :] = part[...]


def attend_kernel(block, info_ref, own_ref, *refs):
    (k_parts, q_parts, v_parts), refs = (refs[0:4], refs[4:8], refs[8:12]), refs[12:]
    o_ref, log_ref, keys_ref = refs[:3]
    pieces, (q_pad, v_buf, low_buf) = refs[3:7], refs[7:]
    head = pl.program_id(0)
    row_len = keys_ref.shape[0]

    @pl.when(head == 0)
    def keys():
        gather_blocks(own_ref, keys_ref, k_parts, 0)

    q_pad[...] = jnp.zeros_like(q_pad)
    own_rows = pl.ds(pl.multiple_of(head * HEAD_DIM, HEAD_DIM), HEAD_DIM)
    gather_blocks(own_ref, q_pad.at[own_rows], q_parts, 1)
    gather_blocks(own_ref, v_buf, v_parts, 1)
    for i in range(row_len // block):
        cols = slice(i * block, (i + 1) * block)
        parts = score_parts(info_ref, keys_ref, q_pad[:, cols], block, i, row_len)
        top = functools.reduce(
            jnp.maximum, [jnp.max(s, axis=0, keepdims=True) for _, _, s in parts]
        )
        total, out = 0.0, 0.0
        for first, last, s in parts:
            p = jnp.exp(s - top)
            total = total + jnp.sum(p, axis=0, keepdims=True)
            out = out + mm(v_buf[:, first:last], p.astype(bf16))
        out = out / total
        o_ref[:, cols] = out
        low_buf[:, cols] = out.astype(bf16)
        log_ref[0, :, cols] = top + jnp.log(total)
    for j, piece in enumerate(pieces):
        size = piece.shape[1]
        where = pl.ds(pl.multiple_of((own_ref[0] ^ j) * size, size), size)
        piece[...] = low_buf[:, where]


def attend(info, own, k_parts, qkv_parts, block=512):
    count, group = k_parts[0].shape
    row_len = count * len(k_parts)
    heads = group // HEAD_DIM
    tile = pl.BlockSpec((HEAD_DIM, row_len), lambda h: (h, 0))
    whole = pl.BlockSpec((row_len, group), lambda h: (0, 0))
    keys = pl.BlockSpec((count, group), lambda h: (0, 0))
    query = pl.BlockSpec((HEAD_DIM, count), lambda h: (h, 0))
    value = pl.BlockSpec((HEAD_DIM, count), lambda h: (2 * heads + h, 0))
    results = pl.pallas_call(
        functools.partial(attend_kernel, block),
        out_shape=[
            jax.ShapeDtypeStruct((group, row_len), f32),
            jax.ShapeDtypeStruct((heads, 1, row_len), f32),
            jax.ShapeDtypeStruct((row_len, group), bf16),
        ]
        + [jax.ShapeDtypeStruct((group, count), bf16)] * 4,
        grid=(heads,),
        in_specs=[smem_spec()] * 2 + [keys] * 4 + [query] * 4 + [value] * 4,
        out_specs=[tile, pl.BlockSpec((1, 1, row_len), lambda h: (h, 0, 0)), whole] + [query] * 4,
        scratch_shapes=[
            pltpu.VMEM((group, row_len), bf16),
            pltpu.VMEM((HEAD_DIM, row_len), bf16),
            pltpu.VMEM((HEAD_DIM, row_len), bf16),
        ],
        compiler_params=params(60),
        name="attend",
        cost_estimate=cost(0.1),
    )(info, own, *k_parts, *qkv_parts, *qkv_parts)
    return results[0], results[1], results[2], results[3:]


def attend_back_kernel(block, first_head, info_ref, own_ref, k_ref, *refs):
    v_parts, q_parts, kt_parts, g_parts, a_parts = (refs[4 * n : 4 * n + 4] for n in range(5))
    o_ref, log_ref, dqkv_ref, grad_ref = refs[20:24]
    v_buf, q_pad, g_pad, kt_buf, a_buf, dk_acc, dv_acc = refs[24:]
    row_len = k_ref.shape[0]
    head = first_head + pl.program_id(0)
    own_rows = pl.ds(pl.multiple_of(head * HEAD_DIM, HEAD_DIM), HEAD_DIM)
    dk_acc[...] = jnp.zeros_like(dk_acc)
    dv_acc[...] = jnp.zeros_like(dv_acc)
    q_pad[...] = jnp.zeros_like(q_pad)
    g_pad[...] = jnp.zeros_like(g_pad)

    @pl.when(pl.program_id(0) == 0)
    def once():
        gather_blocks(own_ref, v_buf, v_parts, 0)
        gather_blocks(own_ref, a_buf, a_parts, 0)

    gather_blocks(own_ref, q_pad.at[own_rows], q_parts, 1)
    gather_blocks(own_ref, g_pad.at[own_rows], g_parts, 1)
    gather_blocks(own_ref, kt_buf, kt_parts, 1)
    for i in range(row_len // block):
        cols = slice(i * block, (i + 1) * block)
        q, g = q_pad[own_rows, cols], g_pad[own_rows, cols]
        g_wide = g_pad[:, cols]
        delta = jnp.sum(g.astype(f32) * o_ref[:, cols], axis=0, keepdims=True)
        log_total = log_ref[0, :, cols]
        dq = 0.0
        for first, last, s in score_parts(info_ref, k_ref, q_pad[:, cols], block, i, row_len):
            p = jnp.exp(s - log_total)
            dp = mm(v_buf[first:last, :], g_wide)
            ds = (p * (dp - delta)).astype(bf16)
            dv_acc[:, first:last] += mm(g, p.astype(bf16), NT)
            dk_acc[:, first:last] += mm(q, ds, NT)
            dq = dq + mm(kt_buf[:, first:last], ds)
        dqkv_ref[0:HEAD_DIM, cols] = (0.125 * dq).astype(bf16)
    dqkv_ref[HEAD_DIM : 2 * HEAD_DIM, :] = dk_acc[...].astype(bf16)
    dqkv_ref[2 * HEAD_DIM :, :] = dv_acc[...].astype(bf16)
    grad = mm(dqkv_ref[...], a_buf[...])
    rows = grad_ref.shape[2]
    for e in range(grad_ref.shape[0]):
        grad_ref[e, 0] = grad[e * rows : (e + 1) * rows, :].astype(bf16)


def attend_back(first, number, pieces, info, own, keys, v_parts, qkv_parts, grads, out, logs, a_parts, block=256):
    row_len, group = keys.shape
    heads = group // HEAD_DIM
    count, width = a_parts[0].shape

    def whole(*shape):
        return pl.BlockSpec(shape, lambda g: (0,) * len(shape))

    def tile(n):
        return pl.BlockSpec((HEAD_DIM, count), lambda g: (n + g, 0))

    return pl.pallas_call(
        functools.partial(attend_back_kernel, block, first),
        out_shape=[
            jax.ShapeDtypeStruct((number * 3 * HEAD_DIM, row_len), bf16),
            jax.ShapeDtypeStruct((pieces, number, 3 * HEAD_DIM // pieces, width), bf16),
        ],
        grid=(number,),
        in_specs=[smem_spec()] * 2
        + [whole(row_len, group)]
        + [whole(count, group)] * 4
        + [tile(first)] * 4
        + [tile(heads + first)] * 4
        + [tile(first)] * 4
        + [whole(count, width)] * 4
        + [
            pl.BlockSpec((HEAD_DIM, row_len), lambda g: (first + g, 0)),
            pl.BlockSpec((1, 1, row_len), lambda g: (first + g, 0, 0)),
        ],
        out_specs=[
            pl.BlockSpec((3 * HEAD_DIM, row_len), lambda g: (g, 0)),
            pl.BlockSpec((pieces, 1, 3 * HEAD_DIM // pieces, width), lambda g: (0, g, 0, 0)),
        ],
        scratch_shapes=[
            pltpu.VMEM((row_len, group), bf16),
            pltpu.VMEM((group, row_len), bf16),
            pltpu.VMEM((group, row_len), bf16),
            pltpu.VMEM((HEAD_DIM, row_len), bf16),
            pltpu.VMEM((row_len, width), bf16),
            pltpu.VMEM((HEAD_DIM, row_len), f32),
            pltpu.VMEM((HEAD_DIM, row_len), f32),
        ],
        compiler_params=params(60),
        name="attend_back",
        cost_estimate=cost(11 * number),
    )(info, own, keys, *v_parts, *qkv_parts, *qkv_parts, *grads, *a_parts, out, logs)


def gates_of(normed, router, route_rows):
    logits = mm(router, normed, NT, precise)
    expert_row = iota(logits.shape, 0)
    picked = [
        jnp.sum(jnp.where(expert_row == row, logits, 0.0), axis=0, keepdims=True)
        for row in route_rows
    ]
    top = jnp.maximum(picked[0], picked[1])
    raw = [jnp.exp(p - top) for p in picked]
    return [r / (raw[0] + raw[1]) for r in raw]


def dispatch_kernel(
    own_ref, t0, t1, t2, t3, x_ref, w_ref, gain_ref, router_ref, routes_ref, hot_a, hot_b,
    residual_ref, gates_ref, send_a, send_b,
):
    residual = x_ref[...].astype(f32)
    group = t0.shape[0]
    for j, part in enumerate((t0, t1, t2, t3)):
        rows = pl.ds(pl.multiple_of((own_ref[0] ^ j) * group, group), group)
        residual = residual + mm(part[...], w_ref[rows, :], TN)
    residual_ref[...] = residual
    scale = lax.rsqrt(jnp.mean(residual * residual, axis=1, keepdims=True) + norm_eps)
    normed = residual * scale * gain_ref[...]
    a_two = normed.astype(bf16)
    route_rows = [routes_ref[k : k + 1, :] for k in range(2)]
    gates = gates_of(normed, router_ref[...], route_rows)
    gates_ref[0:1, :] = gates[0]
    gates_ref[1:2, :] = gates[1]
    experts = router_ref.shape[0]
    expert_row = iota((experts, x_ref.shape[0]), 0)
    table = jnp.where(expert_row == route_rows[0], gates[0], 0.0) + jnp.where(
        expert_row == route_rows[1], gates[1], 0.0
    )
    stacked = jnp.concatenate([piece.astype(f32) for piece in split_three(table)], axis=0)
    stacked = stacked.astype(bf16)
    last = send_b.shape[1] - EXTRA
    for e in range(experts):
        send_b[e, last:, :] = jnp.zeros((EXTRA, send_b.shape[2]), bf16)
    for hot, send, lane in ((hot_a, send_a, 0), (hot_b, send_b, LANE_B)):
        size = hot.shape[0] // experts
        rows = mm(hot[...], a_two).astype(bf16)
        for e in range(experts):
            own_rows = slice(e * size, (e + 1) * size)
            send[e, 0:size, :] = rows[own_rows, :]
            picked = mm(stacked, hot[own_rows, :], NT)
            three = [picked[k * experts + e : k * experts + e + 1, :] for k in range(3)]
            three = jnp.concatenate(three + [jnp.zeros((EXTRA - 3, size), f32)], axis=0)
            send_b[e, last:, lane : lane + size] = three.astype(bf16)


def make_dispatch(own, parts, x, w_out, gain, router_t, routes_t, hots):
    count, width = x.shape
    experts = router_t.shape[0]
    shapes = [
        jax.ShapeDtypeStruct((count, width), f32),
        jax.ShapeDtypeStruct((2, count), f32),
    ]
    sizes = [hot.shape[0] // experts for hot in hots]
    shapes += [
        jax.ShapeDtypeStruct((experts, sizes[0], width), bf16),
        jax.ShapeDtypeStruct((experts, sizes[1] + EXTRA, width), bf16),
    ]
    return pl.pallas_call(
        dispatch_kernel,
        out_shape=shapes,
        in_specs=[smem_spec()] + [vmem_spec()] * 11,
        out_specs=[vmem_spec()] * len(shapes),
        compiler_params=params(60),
        name="project_dispatch",
        cost_estimate=cost(0.1),
    )(own, *parts, x, w_out, gain, router_t, routes_t, *hots)


def column_of(row):
    return jnp.broadcast_to(row, (128, row.shape[1])).T[:, 0:1]


def row_of(column):
    return jnp.broadcast_to(column, (column.shape[0], 128)).T[0:1, :]


GELU_SCALE = 0.7978845608028654
GELU_CUBE = 0.044715


def expert_kernel(half, start, x_ref, dy_ref, *refs):
    weights, refs = refs[:8], refs[8:]
    if half:
        carried_ref, refs = refs[0], refs[2:]
        out_ref, slot_ref, act_ref, dpre_ref = refs[:4]
        refs = refs[4:]
    else:
        out_ref, slot_ref, act_ref, dpre_ref, carry_ref = refs[:5]
        refs = refs[5:]
    x_buf, dy_buf, up_buf, down_buf, out_acc, slot_acc, sems = refs
    sources, width = x_ref.shape[0], x_ref.shape[2]
    size = x_buf.shape[0] // sources
    step = pl.program_id(0)
    parts = len(weights) // 2

    def copies(j):
        return (
            pltpu.make_async_copy(weights[2 * j], up_buf.at[j % 2], sems.at[0, j % 2]),
            pltpu.make_async_copy(weights[2 * j + 1], down_buf.at[j % 2], sems.at[1, j % 2]),
        )

    @pl.when(step == 0)
    def first():
        for copy in copies(0):
            copy.start()
        for n in range(sources):
            x_buf[n * size : (n + 1) * size, :] = x_ref[n, 0:size, :]
            dy_buf[n * size : (n + 1) * size, :] = dy_ref[n, start : start + size, :]
        out_acc[...] = jnp.zeros_like(out_acc)
        slot_acc[...] = jnp.zeros_like(slot_acc)

    for j in range(parts):

        @pl.when(step == j)
        def arrive(j=j):
            if j + 1 < parts:
                for copy in copies(j + 1):
                    copy.start()
            for copy in copies(j):
                copy.wait()

    which = lax.rem(step, 2)
    block = x_buf.shape[0] // 2

    @pl.loop(0, 2)
    def rows_of(r):
        rows = pl.ds(pl.multiple_of(r * block, block), block)
        up, down = up_buf[which], down_buf[which]
        pre = mm(x_buf[rows, :], up)
        square = pre * pre
        tanh = jnp.tanh(GELU_SCALE * (pre * (1.0 + GELU_CUBE * square)))
        half = 0.5 * (1.0 + tanh)
        act = (pre * half).astype(bf16)
        act_ref[0, rows, :] = act
        out_acc[rows, :] += mm(act, down)
        slope = half + (0.5 * GELU_SCALE) * pre * (1.0 - tanh * tanh) * (
            1.0 + (3.0 * GELU_CUBE) * square
        )
        dpre = (mm(dy_buf[rows, :], down, NT) * slope).astype(bf16)
        dpre_ref[0, rows, :] = dpre
        slot_acc[rows, :] += mm(dpre, up, NT)

    @pl.when(step == parts - 1)
    def last():
        for n in range(sources):
            rows = slice(n * size, (n + 1) * size)
            out = out_acc[rows, :].astype(bf16)
            out_ref[n, start : start + size, :] = out
            slot_ref[n, 0:size, :] = slot_acc[rows, :].astype(bf16)
            dgate = jnp.sum(
                dy_buf[rows, :].astype(f32) * out.astype(f32), axis=1, keepdims=True
            )
            three = three_rows(row_of(dgate))
            if half:
                slot_ref[n, size:, :] = jnp.zeros((EXTRA, width), bf16)
                slot_ref[n, size:, 0:LANE_B] = carried_ref[n]
                slot_ref[n, size:, LANE_B : LANE_B + size] = three
            else:
                carry_ref[n] = jnp.zeros((EXTRA, LANE_B), bf16)
                carry_ref[n, :, 0:size] = three


def run_experts(half, start, size, x, dy, weights, before):
    sources, _, width = x.shape
    rows = sources * size
    units = weights[0].shape[1]
    parts = len(weights) // 2

    def whole(shape):
        return pl.BlockSpec(shape, lambda g: (0,) * len(shape), pipeline_mode=pl.Buffered(1))

    def shaped(*shape):
        return jax.ShapeDtypeStruct(shape, bf16)

    kept = shaped(parts, rows, units)
    kept_spec = pl.BlockSpec((1, rows, units), lambda g: (g, 0, 0))
    carry = shaped(sources, EXTRA, LANE_B)
    hbm = pl.BlockSpec(memory_space=pl.ANY)
    piece = pl.BlockSpec((sources, size, width), lambda g: (0, start // size, 0))
    return pl.pallas_call(
        functools.partial(expert_kernel, half, 0),
        out_shape=[shaped(*dy.shape), shaped(*x.shape), kept, kept] + ([] if half else [carry]),
        grid=(parts,),
        in_specs=[whole(x.shape), piece]
        + [hbm] * (2 * parts)
        + ([whole(carry.shape), hbm] if half else []),
        out_specs=[piece, whole(x.shape), kept_spec, kept_spec]
        + ([] if half else [whole(carry.shape)]),
        scratch_shapes=[
            pltpu.VMEM((rows, width), bf16),
            pltpu.VMEM((rows, width), bf16),
            pltpu.VMEM((2, width, units), bf16),
            pltpu.VMEM((2, units, width), bf16),
            pltpu.VMEM((rows, width), f32),
            pltpu.VMEM((rows, width), f32),
            pltpu.SemaphoreType.DMA((2, 2)),
        ],
        input_output_aliases={2 * parts + 3: 0} if half else {},
        compiler_params=params(60),
        name="experts",
        cost_estimate=cost(25),
    )(x, dy, *weights, *((before[4], before[0]) if half else ()))


def weight_kernel(dy_ref, x_a, x_b, act_a, act_b, dpre_a, dpre_b, own_out, near_out, far_up, far_down, x_buf, dy_buf):
    step = pl.program_id(0)
    experts, capacity, _ = dy_ref.shape

    @pl.when(step == 0)
    def gated():
        begin = 0
        halves = zip(halves_of(capacity), (x_a, x_b), (0, LANE_B))
        for (start, size), x_ref, lane in halves:
            for n in range(experts):
                rows = slice(begin, begin + size)
                begin += size
                three = x_b[n, x_b.shape[1] - EXTRA :, lane : lane + size].astype(f32)
                gate = column_of(three[0:1] + three[1:2] + three[2:3])
                x_buf[rows, :] = (x_ref[n, 0:size, :].astype(f32) * gate).astype(bf16)
                dy = dy_ref[n, start : start + size, :].astype(f32)
                dy_buf[rows, :] = (dy * gate).astype(bf16)

    cut = act_a.shape[1]
    up = mm(x_buf[:cut, :], dpre_a[0], TN) + mm(x_buf[cut:, :], dpre_b[0], TN)
    down = mm(act_a[0], dy_buf[:cut, :], TN) + mm(act_b[0], dy_buf[cut:, :], TN)
    for j, (out, n) in enumerate(((own_out, 0), (near_out, 0), (None, 0), (near_out, 2))):

        @pl.when(step == j)
        def keep(out=out, n=n):
            if out is None:
                far_up[...] = up
                far_down[...] = down
            else:
                out[n] = up.astype(out.dtype)
                out[n + 1] = down.astype(out.dtype)


def weight_grads(xs, dy, acts, dpres):
    experts, capacity, width = dy.shape
    parts, _, units = acts[0].shape
    assert units == width

    def whole(*shape):
        return pl.BlockSpec(shape, lambda g: (0,) * len(shape), pipeline_mode=pl.Buffered(1))

    kept = [pl.BlockSpec((1,) + a.shape[1:], lambda g: (g, 0, 0)) for a in (*acts, *dpres)]
    return pl.pallas_call(
        weight_kernel,
        out_shape=[
            jax.ShapeDtypeStruct((2, width, units), f32),
            jax.ShapeDtypeStruct((4, width, units), bf16),
            jax.ShapeDtypeStruct((width, units), f32),
            jax.ShapeDtypeStruct((units, width), f32),
        ],
        grid=(parts,),
        in_specs=[whole(*dy.shape)] + [whole(*x.shape) for x in xs] + kept,
        out_specs=[whole(2, width, units), whole(4, width, units)] + [whole(width, units)] * 2,
        scratch_shapes=[pltpu.VMEM((experts * capacity, width), bf16)] * 2,
        compiler_params=params(60),
        name="expert_weight_grads",
        cost_estimate=cost(25),
    )(dy, *xs, *acts, *dpres)


def combine_back_kernel(
    own_ref, hot_a, hot_b, p0a, p1a, p0b, p1b, residual_ref, dy_ref, gates_ref, routes_ref,
    router_ref, gain_ref, w_ref, slot_a, slot_b,
    dres_ref, branch_ref, small_ref, g0, g1, g2, g3, buf_a, buf_b, datt_buf,
):
    experts = router_ref.shape[0]
    table = [0.0] * experts
    last = slot_b.shape[1] - EXTRA
    for slot, hot, buf, lane in ((slot_a, hot_a, buf_a, 0), (slot_b, hot_b, buf_b, LANE_B)):
        size = hot.shape[0] // experts
        for e in range(experts):
            rows = slice(e * size, (e + 1) * size)
            buf[rows, :] = slot[e, 0:size, :]
            picked = mm(slot_b[e, last:, lane : lane + size], hot[rows, :])
            table[e] = table[e] + (picked[0:1] + picked[1:2] + picked[2:3])
    table = jnp.concatenate(table, axis=0)
    residual = residual_ref[...]
    count = residual.shape[0]
    scale = lax.rsqrt(jnp.mean(residual * residual, axis=1, keepdims=True) + norm_eps)
    unit = residual * scale
    gain = gain_ref[...]
    expert_row = iota((experts, count), 0)
    routes = [routes_ref[k : k + 1, :] for k in range(2)]
    gates = [gates_ref[k : k + 1, :] for k in range(2)]
    dgates = [
        jnp.sum(jnp.where(expert_row == r, table, 0.0), axis=0, keepdims=True) for r in routes
    ]
    mean = gates[0] * dgates[0] + gates[1] * dgates[1]
    dlogit = sum(
        jnp.where(expert_row == r, g * (d - mean), 0.0) for r, g, d in zip(routes, gates, dgates)
    )
    small_ref[...] = jnp.zeros_like(small_ref)
    small_ref[0:experts, :] = mm(dlogit, unit * gain, precision=precise)
    dnormed = mm(dlogit, router_ref[...], TN, precise)
    for gate, pick_a, pick_b in ((gates[0], p0a, p0b), (gates[1], p1a, p1b)):
        rows = mm(pick_a[...], buf_a[...]) + mm(pick_b[...], buf_b[...])
        dnormed = dnormed + column_of(gate) * rows
    small_ref[experts : experts + 1, :] = jnp.sum(dnormed * unit, axis=0, keepdims=True)
    scaled = dnormed * gain
    dres = dy_ref[...].astype(f32) + scale * (
        scaled - unit * jnp.mean(scaled * unit, axis=1, keepdims=True)
    )
    dres_ref[...] = dres
    branch = dres.astype(bf16)
    branch_ref[...] = branch
    datt_buf[...] = mm(w_ref[...], branch, NT).astype(bf16)
    for j, piece in enumerate((g0, g1, g2, g3)):
        size = piece.shape[0]
        piece[...] = datt_buf[pl.ds(pl.multiple_of((own_ref[0] ^ j) * size, size), size), :]


def combine_back(own, slots, hots, picks, residual, dy, gates, routes_t, router_t, gain, w_out):
    count, width = residual.shape
    experts = router_t.shape[0]
    shapes = [
        jax.ShapeDtypeStruct((count, width), f32),
        jax.ShapeDtypeStruct((count, width), bf16),
        jax.ShapeDtypeStruct((experts + 8, width), f32),
    ] + [jax.ShapeDtypeStruct((width // 4, count), bf16)] * 4
    results = pl.pallas_call(
        combine_back_kernel,
        out_shape=shapes,
        in_specs=[smem_spec()] + [vmem_spec()] * 15,
        out_specs=[vmem_spec()] * len(shapes),
        scratch_shapes=[pltpu.VMEM((hot.shape[0], width), bf16) for hot in hots]
        + [pltpu.VMEM((width, count), bf16)],
        compiler_params=params(60),
        name="combine_back",
        cost_estimate=cost(11),
    )(own, *hots, *picks, residual, dy, gates, routes_t, router_t, gain, w_out, *slots)
    return results[0], results[1], results[2], results[3:]


def out_grad_kernel(t0, t1, t2, t3, branch_ref, keep_ref, give_ref):
    branch = branch_ref[...]
    keep_ref[0] = mm(t0[...], branch)
    keep_ref[1] = mm(t2[...], branch)
    give_ref[0] = mm(t1[...], branch).astype(bf16)
    give_ref[1] = mm(t3[...], branch).astype(bf16)


def out_grads(parts, branch):
    shape = (2, parts[0].shape[0], branch.shape[1])
    return pl.pallas_call(
        out_grad_kernel,
        out_shape=[jax.ShapeDtypeStruct(shape, f32), jax.ShapeDtypeStruct(shape, bf16)],
        in_specs=[vmem_spec()] * 5,
        out_specs=[vmem_spec()] * 2,
        compiler_params=params(60),
        name="w_out_grads",
        cost_estimate=cost(3),
    )(*parts, branch)


def combine_kernel(p0a, p1a, p0b, p1b, residual_ref, gates_ref, out_ref, y_ref, buf_a, buf_b):
    experts, capacity, _ = out_ref.shape
    for (start, size), buf in zip(halves_of(capacity), (buf_a, buf_b)):
        for e in range(experts):
            buf[e * size : (e + 1) * size, :] = out_ref[e, start : start + size, :]
    total = residual_ref[...]
    for k, (pick_a, pick_b) in enumerate(((p0a, p0b), (p1a, p1b))):
        rows = mm(pick_a[...], buf_a[...]) + mm(pick_b[...], buf_b[...])
        total = total + column_of(gates_ref[k : k + 1, :]) * rows
    y_ref[...] = total.astype(bf16)


def combine(out, picks, residual, gates):
    experts, capacity, width = out.shape
    return pl.pallas_call(
        combine_kernel,
        out_shape=jax.ShapeDtypeStruct(residual.shape, bf16),
        in_specs=[vmem_spec()] * 7,
        out_specs=vmem_spec(),
        scratch_shapes=[
            pltpu.VMEM((experts * size, width), bf16) for _, size in halves_of(capacity)
        ],
        compiler_params=params(60),
        name="combine",
        cost_estimate=cost(6),
    )(*picks, residual, gates, out)


def spread_kernel(places_ref, d01, d2, w_ref, near_out, last_out, far_out, own_out, d_buf):
    step = pl.program_id(0)
    heads = d_buf.shape[0] // (3 * HEAD_DIM)
    for c, (part, n) in enumerate(((d01, 0), (d01, 3), (d2, 0))):
        for t in range(3):
            start = (t * heads + c) * HEAD_DIM
            d_buf[start : start + HEAD_DIM, :] = part[(n + t) * HEAD_DIM : (n + t + 1) * HEAD_DIM, :]
    dn = mm(d_buf[...], w_ref[...], TN)
    for n, out in enumerate((near_out, last_out, far_out, own_out)):

        @pl.when(step == n)
        def keep(out=out):
            out[...] = dn.astype(out.dtype)


def spread(places, parts, w_t):
    row_len = parts[0].shape[1]
    cols, width = w_t.shape
    steps = places.shape[0]
    count = row_len // steps
    tiles = [pl.BlockSpec((p.shape[0], count), lambda g, places: (0, places[g])) for p in parts]

    def whole(shape):
        return pl.BlockSpec(shape, lambda g, places: (0, 0), pipeline_mode=pl.Buffered(1))

    return pl.pallas_call(
        spread_kernel,
        out_shape=[jax.ShapeDtypeStruct((count, width), t) for t in (bf16, bf16, f32, f32)],
        grid_spec=pltpu.PrefetchScalarGridSpec(
            num_scalar_prefetch=1,
            grid=(steps,),
            in_specs=tiles + [whole((cols, width))],
            out_specs=[whole((count, width))] * 4,
            scratch_shapes=[pltpu.VMEM((cols, count), bf16)],
        ),
        compiler_params=params(40),
        name="spread_back",
        cost_estimate=cost(8),
    )(places, *parts, w_t)


def mix_kernel(taken, special, moved_ref, grad_ref, keep_ref, near_ref, far_ref, small_ref, out_ref):
    exps, rows, width = out_ref.shape
    sums = moved_ref[0, 0:taken].astype(f32)
    for e in range(1, exps):
        sums = sums + moved_ref[e, 0:taken].astype(f32)
    gout = keep_ref[0] + near_ref[0].astype(f32) + far_ref[...].astype(f32)
    out_rows = gout.shape[0] // exps
    pad = rows - taken - grad_ref.shape[2] - out_rows - 2 * special
    for e in range(exps):
        high, mid, _ = split_three(small_ref[e * special : (e + 1) * special, :])
        parts = [sums, grad_ref[e, 0].astype(f32), gout[e * out_rows : (e + 1) * out_rows]]
        parts += [high.astype(f32), mid.astype(f32)]
        if pad:
            parts.append(jnp.zeros((pad, width), f32))
        out_ref[e] = jnp.concatenate(parts, axis=0).astype(bf16)


def mix(moved, taken, grad, keep, near, far, small, special):
    exps, _, rows, width = grad.shape
    total = taken + rows + keep.shape[1] // exps + 2 * special
    return pl.pallas_call(
        functools.partial(mix_kernel, taken, special),
        out_shape=jax.ShapeDtypeStruct((exps, total + -total % 8, width), bf16),
        in_specs=[vmem_spec()] * 6,
        out_specs=vmem_spec(),
        compiler_params=params(50),
        name="mix_sums",
        cost_estimate=cost(2),
    )(moved, grad, keep, near, far, small)


def fold_kernel(start, taken, special, moved_ref, out_ref):
    exps, rows, width = out_ref.shape
    sums = moved_ref[0, start : start + taken].astype(f32)
    for e in range(1, exps):
        sums = sums + moved_ref[e, start : start + taken].astype(f32)
    body = taken - 2 * special
    high, mid, _ = split_three(
        sums[body : body + special] + sums[body + special : body + 2 * special]
    )
    parts = [sums[:body], high.astype(f32), mid.astype(f32)]
    if rows > taken:
        parts.append(jnp.zeros((rows - taken, width), f32))
    sums = jnp.concatenate(parts, axis=0).astype(bf16)
    for e in range(exps):
        out_ref[e] = sums


def fold(moved, start, taken, special):
    exps, _, width = moved.shape
    return pl.pallas_call(
        functools.partial(fold_kernel, start, taken, special),
        out_shape=jax.ShapeDtypeStruct((exps, taken + -taken % 8, width), bf16),
        in_specs=[vmem_spec()],
        out_specs=vmem_spec(),
        compiler_params=params(40),
        name="fold_sums",
        cost_estimate=cost(2),
    )(moved)


def lay_out_kernel(rows, out_rows, small_rows, own_ref, *refs):
    arrays, refs = refs[:8], refs[8:]
    w_ref, gain_ref, grad_ref, ggain_ref, gout_ref, small_ref, b0, b1, sems = refs
    hids, exps = b0.shape[0], b0.shape[1]
    step = pl.program_id(0)
    block = grad_ref.shape[0]

    @pl.when(step == 0)
    def fetch():
        copies = [
            pltpu.make_async_copy(arrays[4 * c + j], buf.at[own_ref[0] ^ j], sems.at[c, j])
            for c, buf in enumerate((b0, b1))
            for j in range(hids)
        ]
        for copy in copies:
            copy.start()
        for copy in copies:
            copy.wait()

    cols = pl.ds(pl.multiple_of(step * block, block), block)
    blocks = {}
    for h in range(hids):
        for c, (buf, start) in enumerate(((b0, 0), (b0, rows), (b1, 0))):
            pieces = [buf[h, e, start : start + rows, cols].astype(f32) for e in range(exps)]
            blocks[h, c] = jnp.concatenate(pieces, axis=0)
    stacked = [
        blocks[h, c][t * HEAD_DIM : (t + 1) * HEAD_DIM]
        for t in range(3)
        for h in range(hids)
        for c in range(3)
    ]
    grad = jnp.concatenate(stacked, axis=0).T
    grad_ref[...] = grad
    total = jnp.sum(grad * w_ref[...].astype(f32), axis=1, keepdims=True)
    ggain_ref[...] = row_of(total) / gain_ref[...]
    for h in range(hids):
        for e in range(exps):
            n = h * exps + e
            piece = b1[h, e, rows : rows + out_rows, cols]
            gout_ref[n * out_rows : (n + 1) * out_rows, :] = piece.astype(f32)
    start = rows + out_rows
    for e in range(exps):
        total = 0.0
        for h in range(hids):
            high = b1[h, e, start : start + small_rows, cols].astype(f32)
            low = b1[h, e, start + small_rows : start + 2 * small_rows, cols].astype(f32)
            total = total + (high + low)
        small_ref[e * small_rows : (e + 1) * small_rows, :] = total


def lay_out(own, chunks, rows, out_rows, small_rows, w_qkv, gain, block=256):
    width, cols = w_qkv.shape
    smalls = chunks[0][0].shape[0] * small_rows
    arrays = [a for chunk in chunks for a in chunk]
    tile = pl.BlockSpec((block, cols), lambda g: (g, 0))
    row = pl.BlockSpec((1, block), lambda g: (0, g))
    return pl.pallas_call(
        functools.partial(lay_out_kernel, rows, out_rows, small_rows),
        out_shape=[
            jax.ShapeDtypeStruct((width, cols), f32),
            jax.ShapeDtypeStruct((1, width), f32),
            jax.ShapeDtypeStruct((width, width), f32),
            jax.ShapeDtypeStruct((smalls, width), f32),
        ],
        grid=(width // block,),
        in_specs=[smem_spec()] + [pl.BlockSpec(memory_space=pl.ANY)] * 8 + [tile, row],
        out_specs=[
            tile, row, pl.BlockSpec((width, block), lambda g: (0, g)),
            pl.BlockSpec((smalls, block), lambda g: (0, g)),
        ],
        scratch_shapes=[pltpu.VMEM((4,) + chunk[0].shape, bf16) for chunk in chunks]
        + [pltpu.SemaphoreType.DMA((2, 4))],
        compiler_params=params(50),
        name="lay_out_sums",
        cost_estimate=cost(10),
    )(own, *arrays, w_qkv, gain)


def adam_update(weight, gradient, first_moment, second_moment, live_mask):
    first_next = beta_one * first_moment + (1.0 - beta_one) * gradient
    second_next = beta_two * second_moment + (1.0 - beta_two) * gradient * gradient
    first_hat = first_next / (1.0 - beta_one**adam_steps)
    second_hat = second_next / (1.0 - beta_two**adam_steps)
    weight_next = weight - learn_rate * first_hat / (jnp.sqrt(second_hat) + adam_eps)
    return (
        jnp.where(live_mask, weight_next, weight),
        jnp.where(live_mask, first_next, first_moment),
        jnp.where(live_mask, second_next, second_moment),
    )


def expert_update_kernel(live_ref, own_ref, near_ref, far_ref, weight_ref, first_ref, second_ref, *outs):
    live = live_ref[0] > 0
    grad = own_ref[0] + near_ref[0].astype(f32) + far_ref[...].astype(f32)
    grad = jnp.where(live, grad, 0.0)
    outs[0][...] = grad
    updated = adam_update(weight_ref[...], grad, first_ref[...], second_ref[...], live)
    for out, value in zip(outs[1:], updated):
        out[...] = value


def expert_update(live, own, near, number, far, weight, first_moment, second_moment, block=128):
    tile = pl.BlockSpec((block, weight.shape[1]), lambda g: (g, 0))
    stacked = pl.BlockSpec((1, block, weight.shape[1]), lambda g: (number, g, 0))
    return pl.pallas_call(
        expert_update_kernel,
        out_shape=[jax.ShapeDtypeStruct(weight.shape, f32)] * 4,
        grid=(weight.shape[0] // block,),
        in_specs=[smem_spec(), stacked, stacked] + [tile] * 4,
        out_specs=[tile] * 4,
        compiler_params=params(60),
        name="expert_update",
        cost_estimate=cost(8),
    )(live, own, near, far, weight, first_moment, second_moment)


def tie(value, other):
    return lax.optimization_barrier((value, other))[0]


def exchange(value, axis):
    return lax.all_to_all(value, axis, split_axis=0, concat_axis=0, tiled=True)


def split_sum(value, axis, distance):
    pairs = value.reshape((value.shape[0] // 2, 2) + value.shape[1:])
    low = (lax.axis_index(axis) & distance) == 0
    keep = jnp.where(low, pairs[:, 0], pairs[:, 1])
    give = jnp.where(low, pairs[:, 1], pairs[:, 0]).astype(bf16)
    return keep + swap(give, axis, distance).astype(f32)


def halves(value):
    high = lax.reduce_precision(value, 8, 7)
    return high.astype(bf16), (value - high).astype(bf16)


def pad_rows(value):
    return jnp.pad(value, ((0, 0), (0, -value.shape[1] % 8), (0, 0)))


def gather_hid(value):
    far = swap(value, "hid", 2)
    near = swap(value, "hid", 1)
    return value, near, far, swap(far, "hid", 1)


def body(
    tokens, cotangent, routes, segments, lengths, gain_attn, gain_moe, w_qkv, w_out, router_w,
    router_first, router_second, up_w, down_w, up_first, up_second, down_first, down_second,
):
    exp_count = lax.axis_size("exp")
    hid_count = lax.axis_size("hid")
    hid = lax.axis_index("hid")
    exp_index = lax.axis_index("exp")
    own = jnp.stack([hid, exp_index]).astype(jnp.int32)
    x_own = tokens[0]
    dy = cotangent[0]
    count, width = x_own.shape
    experts = router_w.shape[1]
    frozen_count = experts // 2
    capacity = max(2, 3 * count // experts)
    group = width // hid_count
    heads = group // HEAD_DIM
    is_new = exp_index >= frozen_count

    x_halves = [x_own[: count // 2], x_own[count // 2 :]]
    x_far = [swap(half, "hid", 2) for half in x_halves]
    x_near = swap(x_own, "hid", 1)
    routes_t = routes[0].T
    hots, picks, dy_send = make_tables(routes_t, dy, experts, capacity)
    seg_row = segments[0]
    info = jnp.stack(
        [
            jnp.sum((seg_row < 1).astype(jnp.int32)),
            jnp.sum((seg_row < 2).astype(jnp.int32)),
            lengths[0],
        ]
    )
    up_low = up_w[0].astype(bf16)
    down_low = down_w[0].astype(bf16)
    router_t = router_w.T
    first = project_qkv(own, (x_own, x_near), gain_attn[None], w_qkv)
    x_far, (info, dy_send, up_low, down_low, router_t, routes_t) = lax.optimization_barrier(
        (x_far, (info, dy_send, up_low, down_low, router_t, routes_t))
    )
    x_last = [swap(half, "hid", 1) for half in x_far]
    dy_all = exchange(dy_send, "exp")

    up_far = swap(up_low, "hid", 2)
    up_near, down_near = (swap(tie(low, x_last), "hid", 1) for low in (up_low, down_low))

    second = project_qkv(own, (*x_far, *x_last), gain_attn[None], w_qkv)
    w_t = first[8]
    a_parts, qkv_parts, k_parts, v_parts = (
        (*first[n : n + 2], *second[n : n + 2]) for n in (0, 2, 4, 6)
    )
    out_heads, logs, keys, pieces = attend(info, own, k_parts, qkv_parts)
    pieces, (up_far, up_near, down_near) = lax.optimization_barrier(
        (pieces, (up_far, up_near, down_near))
    )
    att_parts = [pieces[0]] + [swap(pieces[j], "hid", j) for j in range(1, hid_count)]
    att_parts, down_low = lax.optimization_barrier((att_parts, down_low))
    down_far = swap(down_low, "hid", 2)

    residual, gates, *sends = make_dispatch(
        own, att_parts, x_own, w_out, gain_moe[None], router_t, routes_t, hots
    )
    up_far, down_far = tie((up_far, down_far), residual)
    up_last, down_last = swap(up_far, "hid", 1), swap(down_far, "hid", 1)
    weights = (up_low, down_low, up_near, down_near, up_far, down_far, up_last, down_last)
    sends = tie(sends, dy_all)
    x_rows = [exchange(send, "exp") for send in sends]

    results = [None]
    for half, ((start, size), x) in enumerate(zip(halves_of(capacity), x_rows)):
        results.append(run_experts(half, start, size, x, dy_all, weights, results[-1]))
    outs = results[2][0]
    slots, acts, dpres = ([r[n] for r in results[1:]] for n in (1, 2, 3))
    slot_back = [exchange(slot, "exp") for slot in slots]

    own_part, near_part, far_up, far_down = weight_grads(x_rows, dy_all, acts, dpres)
    slot_back, near_part = lax.optimization_barrier((slot_back, near_part))
    near_part = swap(near_part, "hid", 1)

    dres, branch, small, datt_parts = combine_back(
        own, slot_back, hots, picks, residual, dy, gates, routes_t, router_t, gain_moe[None], w_out
    )
    out_back = exchange(tie(outs, slot_back), "exp")
    datt_parts, near_part = lax.optimization_barrier((datt_parts, near_part))
    datt_parts = [datt_parts[0]] + [swap(datt_parts[j], "hid", j) for j in range(1, hid_count)]
    gout, gout_near = out_grads(att_parts, branch)

    out_rows = width // (hid_count * exp_count)
    small_rows = -(-(experts + 1) // exp_count)
    missing = max(0, exp_count * small_rows - small.shape[0])
    small = jnp.pad(small, ((0, missing), (0, 0)))
    gout_near = swap(gout_near, "hid", 1)
    far_up = (far_up + near_part[2].astype(f32)).astype(bf16)
    far_down = (far_down + near_part[3].astype(f32)).astype(bf16)
    far_up, far_down = tie((far_up, far_down), datt_parts)
    far_up = swap(far_up, "hid", 2)
    rows = 3 * HEAD_DIM // exp_count
    given = (info, own, keys, v_parts, qkv_parts, datt_parts, out_heads, logs, a_parts)
    dqkv_first, grads_first = attend_back(0, heads - 1, exp_count, *given)
    gout_near = tie(gout_near, dqkv_first)
    gout_far = swap((gout[1] + gout_near[1].astype(f32)).astype(bf16), "hid", 2)
    grads_first, out_back, far_up, gout_far = lax.optimization_barrier(
        (grads_first, out_back, far_up, gout_far)
    )
    far_down = swap(tie(far_down, gout_far), "hid", 2)
    first = exchange(pad_rows(grads_first.reshape(exp_count, -1, width)), "exp")
    dqkv_last, grads_last = attend_back(heads - 1, 1, exp_count, *given)
    dqkv = [dqkv_first, dqkv_last]
    known = (heads - 1) * rows
    first_sums = mix(first, known, grads_last, gout, gout_near, gout_far, small, small_rows)
    second = exchange(first_sums, "exp")

    dqkv, far_down = tie((dqkv, far_down), first_sums)
    places = jnp.stack([hid ^ j for j in (1, 3, 2, 0)]).astype(jnp.int32)
    near_dn, last_dn, far_dn, own_dn = spread(places, dqkv, w_t)
    near_dn, last_dn = swap(near_dn, "hid", 1), swap(last_dn, "hid", 1)
    far_dn = (far_dn + last_dn.astype(f32)).astype(bf16)
    out_back = tie(out_back, far_dn)
    far_dn = swap(far_dn, "hid", 2)

    out_tokens = combine(out_back, picks, residual, gates)
    second, out_tokens = lax.optimization_barrier((second, out_tokens))
    last_sums = fold(second, known, rows + out_rows + 2 * small_rows, small_rows)
    far_dn, far_up = tie((far_dn, far_up), last_sums)
    live = is_new.astype(jnp.int32).reshape(1)
    grad_up, up_next, up_first_next, up_second_next = expert_update(
        live, own_part, near_part, 0, far_up, up_w[0], up_first[0], up_second[0]
    )
    dnormed = own_dn + near_dn.astype(f32) + far_dn.astype(f32)
    x = x_own.astype(f32)
    scale = lax.rsqrt(jnp.mean(x * x, axis=-1, keepdims=True) + norm_eps)
    unit = x * scale
    scaled = dnormed * gain_attn
    grad_tokens = (
        dres + scale * (scaled - unit * jnp.mean(scaled * unit, axis=-1, keepdims=True))
    ).astype(bf16)
    third = exchange(last_sums, "exp")
    third, grad_tokens, up_next = lax.optimization_barrier((third, grad_tokens, up_next))
    far_down = tie(far_down, third)
    gathered = gather_hid(second[:, :known])
    grad_down = own_part[1] + near_part[1].astype(f32) + far_down.astype(f32)
    grad_down = jnp.where(is_new, grad_down, 0.0)
    down_next, down_first_next, down_second_next = adam_update(
        down_w[0], grad_down, down_first[0], down_second[0], is_new
    )
    gathered = (gathered, gather_hid(third))
    grad_qkv, grad_gain_attn, grad_out_proj, small = lay_out(
        own, gathered, rows, out_rows, small_rows, w_qkv, gain_attn[None]
    )
    grad_gain_moe = small[experts]
    live_columns = (jnp.arange(experts, dtype=jnp.int32) >= frozen_count)[None, :]
    grad_router = jnp.where(live_columns, small[:experts].T, 0.0)
    router_new, router_first_next, router_second_next = adam_update(
        router_w[:, frozen_count:], grad_router[:, frozen_count:], router_first, router_second, True
    )
    router_next = jnp.concatenate([router_w[:, :frozen_count], router_new], axis=1)
    grad_gain_attn = grad_gain_attn[0]
    return (
        out_tokens[None],
        grad_tokens[None],
        grad_qkv,
        grad_out_proj,
        grad_gain_attn,
        grad_gain_moe,
        grad_router,
        router_next,
        router_first_next,
        router_second_next,
        grad_up[None],
        grad_down[None],
        up_next[None],
        down_next[None],
        up_first_next[None],
        up_second_next[None],
        down_first_next[None],
        down_second_next[None],
    )


def solution(mesh):
    tok = P("exp", "hid", None)
    up = P("exp", None, "hid")
    return jax.shard_map(
        body,
        mesh=mesh,
        in_specs=(tok, tok, tok, P("exp", None), P("exp")) + (P(),) * 7
        + (up, tok, up, up, tok, tok),
        out_specs=(tok, tok) + (P(),) * 8 + (up, tok, up, tok, up, up, tok, tok),
        check_vma=False,
    )
```

```python
import functools

import jax
import jax.numpy as jnp
from jax import lax
from jax.experimental import pallas as pl
from jax.experimental.pallas import tpu as pltpu
from jax.sharding import PartitionSpec as P

HEADS = 12
HEAD_DIM = 64

precise = lax.Precision.HIGHEST
norm_eps = 1e-06
beta_one = 0.9
beta_two = 0.999
learn_rate = 0.01
adam_eps = 1e-08
adam_steps = 10.0
masked_score = -1e30

bf16 = jnp.bfloat16
f32 = jnp.float32
MIB = 1 << 20
COST_SCALE = 0.1


def mm(left, right, contract=((1,), (0,)), precision=None):
    return lax.dot_general(
        left, right, (contract, ((), ())), preferred_element_type=f32, precision=precision
    )


NT = ((1,), (1,))
TN = ((0,), (0,))


def swap(value, axis, distance):
    count = lax.axis_size(axis)
    return lax.ppermute(value, axis, [(i, i ^ distance) for i in range(count)])


def iota(shape, dim):
    return lax.broadcasted_iota(jnp.int32, shape, dim)


def split_three(value):
    high = value.astype(bf16)
    rest = value - high.astype(f32)
    mid = rest.astype(bf16)
    low = (rest - mid.astype(f32)).astype(bf16)
    return high, mid, low


EXTRA = 8
LANE_B = 128


def three_rows(row):
    high, mid, low = (piece.astype(f32) for piece in split_three(row))
    return jnp.concatenate([high, mid, low, jnp.zeros((EXTRA - 3, row.shape[1]), f32)], axis=0).astype(bf16)


def vmem_spec():
    return pl.BlockSpec(memory_space=pltpu.VMEM)


def smem_spec():
    return pl.BlockSpec(memory_space=pltpu.SMEM)


def params(mib):
    return pltpu.CompilerParams(vmem_limit_bytes=mib * MIB)


def cost(micros):
    micros = micros * COST_SCALE
    return pl.CostEstimate(
        flops=int(micros * 1.1e9), bytes_accessed=int(micros * 3e6), transcendentals=0
    )


def halves_of(capacity):
    first = (capacity // 2 + 15) // 16 * 16
    return ((0, first), (first, capacity - first))


def tables_kernel(routes_ref, dy_ref, hot_a, hot_b, *outs):
    picks, send_ref = outs[:4], outs[4]
    experts, capacity, _ = send_ref.shape
    count = routes_ref.shape[1]
    expert_row = iota((experts, count), 0)
    route_rows = [routes_ref[k : k + 1, :] for k in range(2)]
    hits = [expert_row == row for row in route_rows]
    hit = hits[0] | hits[1]
    hit_low = jnp.where(hit, 1.0, 0.0).astype(bf16)
    upper = jnp.where(iota((count, count), 0) < iota((count, count), 1), 1.0, 0.0).astype(bf16)
    slot = mm(hit_low, upper)
    slot = jnp.where(hit & (slot < capacity), slot, -1.0)
    index_rows = []
    for (start, size), hot in zip(halves_of(capacity), (hot_a, hot_b)):
        row_id = iota((size, count), 0).astype(f32) + float(start)
        for e in range(experts):
            hot[e * size : (e + 1) * size, :] = jnp.where(
                row_id == slot[e : e + 1, :], 1.0, 0.0
            ).astype(bf16)
        rows = mm(hot[...], dy_ref[...]).astype(bf16)
        for e in range(experts):
            send_ref[e, start : start + size, :] = rows[e * size : (e + 1) * size, :]
        for k in range(2):
            own_slot = jnp.sum(jnp.where(hits[k], slot, 0.0), axis=0, keepdims=True)
            inside = (own_slot >= start) & (own_slot < start + size)
            place = route_rows[k].astype(f32) * size + own_slot - start
            index_rows.append(jnp.where(inside, place, -1.0))
    index_cols = jnp.concatenate(index_rows * 2, axis=0).T
    for n, pick in enumerate(picks):
        lane = iota(pick.shape, 1).astype(f32)
        pick[...] = jnp.where(lane == index_cols[:, n : n + 1], 1.0, 0.0).astype(bf16)


def make_tables(routes_t, dy, experts, capacity):
    count, width = dy.shape
    sizes = [experts * size for _, size in halves_of(capacity)]
    shapes = [jax.ShapeDtypeStruct((size, count), bf16) for size in sizes]
    shapes += [jax.ShapeDtypeStruct((count, size), bf16) for size in sizes for _ in range(2)]
    shapes += [jax.ShapeDtypeStruct((experts, capacity, width), bf16)]
    results = pl.pallas_call(
        tables_kernel,
        out_shape=shapes,
        in_specs=[vmem_spec()] * 2,
        out_specs=[vmem_spec()] * len(shapes),
        compiler_params=params(60),
        name="slot_tables",
        cost_estimate=cost(0.1),
    )(routes_t, dy)
    return results[0:2], results[2:6], results[6]


def qkv_kernel(
    pieces, turned, own_ref, *refs
):
    blocks, refs = refs[: 2 * pieces], refs[2 * pieces :]
    gain_ref, w_ref, a0, a1, q0, q1, k0, k1, v0, v1 = refs[:10]
    if turned:
        w_buf = w_ref
    else:
        w_buf, heads_ref = refs[10:]
        width, cols = heads_ref.shape
        part = cols // 3
        for h in range(width // part):

            @pl.when(own_ref[0] == h)
            def pick(h=h):
                for t in range(3):
                    start = t * width + h * part
                    heads_ref[:, t * part : (t + 1) * part] = w_ref[:, start : start + part]

        w_buf[...] = heads_ref[...].T
    third = w_buf.shape[0] // 3
    outs = ((a0, q0, k0, v0), (a1, q1, k1, v1))
    for n, (a_ref, qkv_ref, k_ref, v_ref) in enumerate(outs):
        x = [x_ref[...] for x_ref in blocks[n * pieces : (n + 1) * pieces]]
        x = jnp.concatenate(x, axis=0).astype(f32)
        scale = lax.rsqrt(jnp.mean(x * x, axis=1, keepdims=True) + norm_eps)
        a = (x * scale * gain_ref[...]).astype(bf16)
        a_ref[...] = a
        qkv_t = mm(w_buf[...], a, NT).astype(bf16)
        qkv_ref[0:third, :] = qkv_t[0:third, :] * jnp.asarray(0.125, bf16)
        qkv_ref[third:, :] = qkv_t[third:, :]
        both = mm(a, w_buf[third:, :], NT).astype(bf16)
        k_ref[...] = both[:, :third]
        v_ref[...] = both[:, third:]


def project_qkv(own, blocks, gain, w_qkv, turned=False):
    pieces = len(blocks) // 2
    count, width = pieces * blocks[0].shape[0], blocks[0].shape[1]
    cols = w_qkv.shape[0] if turned else w_qkv.shape[1] // 4
    third = cols // 3
    shapes = [(count, width)] * 2 + [(cols, count)] * 2 + [(count, third)] * 4
    shapes += [] if turned else [(cols, width)]
    return pl.pallas_call(
        functools.partial(qkv_kernel, pieces, turned),
        out_shape=[jax.ShapeDtypeStruct(shape, bf16) for shape in shapes],
        in_specs=[smem_spec()] + [vmem_spec()] * (2 * pieces + 2),
        out_specs=[vmem_spec()] * len(shapes),
        scratch_shapes=[] if turned else [pltpu.VMEM((width, cols), bf16)],
        compiler_params=params(60),
        name="norm_qkv",
        cost_estimate=cost(0.1),
    )(own, *blocks, gain, w_qkv)


EDGE = 256


def query_rows(info_ref, query_start, size):
    query_row = query_start + iota((1, size), 1)
    first_cut, last_cut, length = info_ref[0], info_ref[1], info_ref[2]
    start_row = jnp.where(
        query_row >= last_cut, last_cut, jnp.where(query_row >= first_cut, first_cut, 0)
    )
    last_row = jnp.minimum(query_row, length - 1)
    return query_row, start_row, last_row


def score_parts(info_ref, keys_ref, queries, block, number, row_len):
    query_start = number * block
    query_row, start_row, last_row = query_rows(info_ref, query_start, block)
    free_from = query_start if query_start + block > row_len - EDGE else min(EDGE, query_start)
    parts = []
    for first, last in ((0, free_from), (free_from, query_start), (query_start, query_start + block)):
        if first == last:
            continue
        scores = mm(keys_ref[first:last, :], queries)
        key_col = first + iota(scores.shape, 0)
        if first == query_start:
            valid = (key_col >= start_row) & (key_col <= last_row) | (key_col == query_row)
            scores = jnp.where(valid, scores, masked_score)
        elif last == free_from:
            scores = jnp.where(key_col >= start_row, scores, masked_score)
        parts.append((first, last, scores))
    return parts


def gather_blocks(own_ref, buf, parts, axis):
    for j, part in enumerate(parts):
        size = part.shape[axis]
        where = pl.ds(pl.multiple_of((own_ref[0] ^ j) * size, size), size)
        if axis:
            buf[:, where] = part[...]
        else:
            buf[where, :] = part[...]


def attend_kernel(block, info_ref, own_ref, *refs):
    (k_parts, q_parts, v_parts), refs = (refs[0:4], refs[4:8], refs[8:12]), refs[12:]
    o_ref, log_ref, keys_ref = refs[:3]
    pieces, (q_pad, v_buf, low_buf) = refs[3:7], refs[7:]
    head = pl.program_id(0)
    row_len = keys_ref.shape[0]

    @pl.when(head == 0)
    def keys():
        gather_blocks(own_ref, keys_ref, k_parts, 0)

    q_pad[...] = jnp.zeros_like(q_pad)
    own_rows = pl.ds(pl.multiple_of(head * HEAD_DIM, HEAD_DIM), HEAD_DIM)
    gather_blocks(own_ref, q_pad.at[own_rows], q_parts, 1)
    gather_blocks(own_ref, v_buf, v_parts, 1)
    for i in range(row_len // block):
        cols = slice(i * block, (i + 1) * block)
        parts = score_parts(info_ref, keys_ref, q_pad[:, cols], block, i, row_len)
        top = functools.reduce(
            jnp.maximum, [jnp.max(s, axis=0, keepdims=True) for _, _, s in parts]
        )
        total, out = 0.0, 0.0
        for first, last, s in parts:
            p = jnp.exp(s - top)
            total = total + jnp.sum(p, axis=0, keepdims=True)
            out = out + mm(v_buf[:, first:last], p.astype(bf16))
        out = out / total
        o_ref[:, cols] = out
        low_buf[:, cols] = out.astype(bf16)
        log_ref[0, :, cols] = top + jnp.log(total)
    for j, piece in enumerate(pieces):
        size = piece.shape[1]
        where = pl.ds(pl.multiple_of((own_ref[0] ^ j) * size, size), size)
        piece[...] = low_buf[:, where]


def attend(info, own, k_parts, qkv_parts, block=512):
    count, group = k_parts[0].shape
    row_len = count * len(k_parts)
    heads = group // HEAD_DIM
    tile = pl.BlockSpec((HEAD_DIM, row_len), lambda h: (h, 0))
    whole = pl.BlockSpec((row_len, group), lambda h: (0, 0))
    keys = pl.BlockSpec((count, group), lambda h: (0, 0))
    query = pl.BlockSpec((HEAD_DIM, count), lambda h: (h, 0))
    value = pl.BlockSpec((HEAD_DIM, count), lambda h: (2 * heads + h, 0))
    results = pl.pallas_call(
        functools.partial(attend_kernel, block),
        out_shape=[
            jax.ShapeDtypeStruct((group, row_len), f32),
            jax.ShapeDtypeStruct((heads, 1, row_len), f32),
            jax.ShapeDtypeStruct((row_len, group), bf16),
        ]
        + [jax.ShapeDtypeStruct((group, count), bf16)] * 4,
        grid=(heads,),
        in_specs=[smem_spec()] * 2 + [keys] * 4 + [query] * 4 + [value] * 4,
        out_specs=[tile, pl.BlockSpec((1, 1, row_len), lambda h: (h, 0, 0)), whole] + [query] * 4,
        scratch_shapes=[
            pltpu.VMEM((group, row_len), bf16),
            pltpu.VMEM((HEAD_DIM, row_len), bf16),
            pltpu.VMEM((HEAD_DIM, row_len), bf16),
        ],
        compiler_params=params(60),
        name="attend",
        cost_estimate=cost(0.1),
    )(info, own, *k_parts, *qkv_parts, *qkv_parts)
    return results[0], results[1], results[2], results[3:]


def attend_back_kernel(block, first_head, info_ref, own_ref, k_ref, *refs):
    v_parts, q_parts, kt_parts, g_parts, a_parts = (refs[4 * n : 4 * n + 4] for n in range(5))
    o_ref, log_ref, dqkv_ref, grad_ref = refs[20:24]
    v_buf, q_pad, g_pad, kt_buf, a_buf, dk_acc, dv_acc = refs[24:]
    row_len = k_ref.shape[0]
    head = first_head + pl.program_id(0)
    own_rows = pl.ds(pl.multiple_of(head * HEAD_DIM, HEAD_DIM), HEAD_DIM)
    dk_acc[...] = jnp.zeros_like(dk_acc)
    dv_acc[...] = jnp.zeros_like(dv_acc)
    q_pad[...] = jnp.zeros_like(q_pad)
    g_pad[...] = jnp.zeros_like(g_pad)

    @pl.when(pl.program_id(0) == 0)
    def once():
        gather_blocks(own_ref, v_buf, v_parts, 0)
        gather_blocks(own_ref, a_buf, a_parts, 0)

    gather_blocks(own_ref, q_pad.at[own_rows], q_parts, 1)
    gather_blocks(own_ref, g_pad.at[own_rows], g_parts, 1)
    gather_blocks(own_ref, kt_buf, kt_parts, 1)
    for i in range(row_len // block):
        cols = slice(i * block, (i + 1) * block)
        q, g = q_pad[own_rows, cols], g_pad[own_rows, cols]
        g_wide = g_pad[:, cols]
        delta = jnp.sum(g.astype(f32) * o_ref[:, cols], axis=0, keepdims=True)
        log_total = log_ref[0, :, cols]
        dq = 0.0
        for first, last, s in score_parts(info_ref, k_ref, q_pad[:, cols], block, i, row_len):
            p = jnp.exp(s - log_total)
            dp = mm(v_buf[first:last, :], g_wide)
            ds = (p * (dp - delta)).astype(bf16)
            dv_acc[:, first:last] += mm(g, p.astype(bf16), NT)
            dk_acc[:, first:last] += mm(q, ds, NT)
            dq = dq + mm(kt_buf[:, first:last], ds)
        dqkv_ref[0:HEAD_DIM, cols] = (0.125 * dq).astype(bf16)
    dqkv_ref[HEAD_DIM : 2 * HEAD_DIM, :] = dk_acc[...].astype(bf16)
    dqkv_ref[2 * HEAD_DIM :, :] = dv_acc[...].astype(bf16)
    grad = mm(dqkv_ref[...], a_buf[...])
    rows = grad_ref.shape[2]
    for e in range(grad_ref.shape[0]):
        grad_ref[e, 0] = grad[e * rows : (e + 1) * rows, :].astype(bf16)


def attend_back(first, number, pieces, info, own, keys, v_parts, qkv_parts, grads, out, logs, a_parts, block=256):
    row_len, group = keys.shape
    heads = group // HEAD_DIM
    count, width = a_parts[0].shape

    def whole(*shape):
        return pl.BlockSpec(shape, lambda g: (0,) * len(shape))

    def tile(n):
        return pl.BlockSpec((HEAD_DIM, count), lambda g: (n + g, 0))

    return pl.pallas_call(
        functools.partial(attend_back_kernel, block, first),
        out_shape=[
            jax.ShapeDtypeStruct((number * 3 * HEAD_DIM, row_len), bf16),
            jax.ShapeDtypeStruct((pieces, number, 3 * HEAD_DIM // pieces, width), bf16),
        ],
        grid=(number,),
        in_specs=[smem_spec()] * 2
        + [whole(row_len, group)]
        + [whole(count, group)] * 4
        + [tile(first)] * 4
        + [tile(heads + first)] * 4
        + [tile(first)] * 4
        + [whole(count, width)] * 4
        + [
            pl.BlockSpec((HEAD_DIM, row_len), lambda g: (first + g, 0)),
            pl.BlockSpec((1, 1, row_len), lambda g: (first + g, 0, 0)),
        ],
        out_specs=[
            pl.BlockSpec((3 * HEAD_DIM, row_len), lambda g: (g, 0)),
            pl.BlockSpec((pieces, 1, 3 * HEAD_DIM // pieces, width), lambda g: (0, g, 0, 0)),
        ],
        scratch_shapes=[
            pltpu.VMEM((row_len, group), bf16),
            pltpu.VMEM((group, row_len), bf16),
            pltpu.VMEM((group, row_len), bf16),
            pltpu.VMEM((HEAD_DIM, row_len), bf16),
            pltpu.VMEM((row_len, width), bf16),
            pltpu.VMEM((HEAD_DIM, row_len), f32),
            pltpu.VMEM((HEAD_DIM, row_len), f32),
        ],
        compiler_params=params(60),
        name="attend_back",
        cost_estimate=cost(11 * number),
    )(info, own, keys, *v_parts, *qkv_parts, *qkv_parts, *grads, *a_parts, out, logs)


def gates_of(normed, router, route_rows):
    logits = mm(router, normed, NT, precise)
    expert_row = iota(logits.shape, 0)
    picked = [
        jnp.sum(jnp.where(expert_row == row, logits, 0.0), axis=0, keepdims=True)
        for row in route_rows
    ]
    top = jnp.maximum(picked[0], picked[1])
    raw = [jnp.exp(p - top) for p in picked]
    return [r / (raw[0] + raw[1]) for r in raw]


def dispatch_kernel(
    own_ref, t0, t1, t2, t3, x_ref, w_ref, gain_ref, router_ref, routes_ref, hot_a, hot_b,
    residual_ref, gates_ref, send_a, send_b,
):
    residual = x_ref[...].astype(f32)
    group = t0.shape[0]
    for j, part in enumerate((t0, t1, t2, t3)):
        rows = pl.ds(pl.multiple_of((own_ref[0] ^ j) * group, group), group)
        residual = residual + mm(part[...], w_ref[rows, :], TN)
    residual_ref[...] = residual
    scale = lax.rsqrt(jnp.mean(residual * residual, axis=1, keepdims=True) + norm_eps)
    normed = residual * scale * gain_ref[...]
    a_two = normed.astype(bf16)
    route_rows = [routes_ref[k : k + 1, :] for k in range(2)]
    gates = gates_of(normed, router_ref[...], route_rows)
    gates_ref[0:1, :] = gates[0]
    gates_ref[1:2, :] = gates[1]
    experts = router_ref.shape[0]
    expert_row = iota((experts, x_ref.shape[0]), 0)
    table = jnp.where(expert_row == route_rows[0], gates[0], 0.0) + jnp.where(
        expert_row == route_rows[1], gates[1], 0.0
    )
    stacked = jnp.concatenate([piece.astype(f32) for piece in split_three(table)], axis=0)
    stacked = stacked.astype(bf16)
    last = send_b.shape[1] - EXTRA
    for e in range(experts):
        send_b[e, last:, :] = jnp.zeros((EXTRA, send_b.shape[2]), bf16)
    for hot, send, lane in ((hot_a, send_a, 0), (hot_b, send_b, LANE_B)):
        size = hot.shape[0] // experts
        rows = mm(hot[...], a_two).astype(bf16)
        for e in range(experts):
            own_rows = slice(e * size, (e + 1) * size)
            send[e, 0:size, :] = rows[own_rows, :]
            picked = mm(stacked, hot[own_rows, :], NT)
            three = [picked[k * experts + e : k * experts + e + 1, :] for k in range(3)]
            three = jnp.concatenate(three + [jnp.zeros((EXTRA - 3, size), f32)], axis=0)
            send_b[e, last:, lane : lane + size] = three.astype(bf16)


def make_dispatch(own, parts, x, w_out, gain, router_t, routes_t, hots):
    count, width = x.shape
    experts = router_t.shape[0]
    shapes = [
        jax.ShapeDtypeStruct((count, width), f32),
        jax.ShapeDtypeStruct((2, count), f32),
    ]
    sizes = [hot.shape[0] // experts for hot in hots]
    shapes += [
        jax.ShapeDtypeStruct((experts, sizes[0], width), bf16),
        jax.ShapeDtypeStruct((experts, sizes[1] + EXTRA, width), bf16),
    ]
    return pl.pallas_call(
        dispatch_kernel,
        out_shape=shapes,
        in_specs=[smem_spec()] + [vmem_spec()] * 11,
        out_specs=[vmem_spec()] * len(shapes),
        compiler_params=params(60),
        name="project_dispatch",
        cost_estimate=cost(0.1),
    )(own, *parts, x, w_out, gain, router_t, routes_t, *hots)


def column_of(row):
    return jnp.broadcast_to(row, (128, row.shape[1])).T[:, 0:1]


def row_of(column):
    return jnp.broadcast_to(column, (column.shape[0], 128)).T[0:1, :]


GELU_SCALE = 0.7978845608028654
GELU_CUBE = 0.044715


def expert_kernel(half, start, x_ref, dy_ref, *refs):
    weights, refs = refs[:8], refs[8:]
    if half:
        carried_ref, refs = refs[0], refs[2:]
        out_ref, slot_ref, act_ref, dpre_ref = refs[:4]
        refs = refs[4:]
    else:
        out_ref, slot_ref, act_ref, dpre_ref, carry_ref = refs[:5]
        refs = refs[5:]
    x_buf, dy_buf, up_buf, down_buf, out_acc, slot_acc, sems = refs
    sources, width = x_ref.shape[0], x_ref.shape[2]
    size = x_buf.shape[0] // sources
    step = pl.program_id(0)
    parts = len(weights) // 2

    def copies(j):
        return (
            pltpu.make_async_copy(weights[2 * j], up_buf.at[j % 2], sems.at[0, j % 2]),
            pltpu.make_async_copy(weights[2 * j + 1], down_buf.at[j % 2], sems.at[1, j % 2]),
        )

    @pl.when(step == 0)
    def first():
        for copy in copies(0):
            copy.start()
        for n in range(sources):
            x_buf[n * size : (n + 1) * size, :] = x_ref[n, 0:size, :]
            dy_buf[n * size : (n + 1) * size, :] = dy_ref[n, start : start + size, :]
        out_acc[...] = jnp.zeros_like(out_acc)
        slot_acc[...] = jnp.zeros_like(slot_acc)

    for j in range(parts):

        @pl.when(step == j)
        def arrive(j=j):
            if j + 1 < parts:
                for copy in copies(j + 1):
                    copy.start()
            for copy in copies(j):
                copy.wait()

    which = lax.rem(step, 2)
    block = x_buf.shape[0] // 2

    @pl.loop(0, 2)
    def rows_of(r):
        rows = pl.ds(pl.multiple_of(r * block, block), block)
        up, down = up_buf[which], down_buf[which]
        pre = mm(x_buf[rows, :], up)
        square = pre * pre
        tanh = jnp.tanh(GELU_SCALE * (pre * (1.0 + GELU_CUBE * square)))
        half = 0.5 * (1.0 + tanh)
        act = (pre * half).astype(bf16)
        act_ref[0, rows, :] = act
        out_acc[rows, :] += mm(act, down)
        slope = half + (0.5 * GELU_SCALE) * pre * (1.0 - tanh * tanh) * (
            1.0 + (3.0 * GELU_CUBE) * square
        )
        dpre = (mm(dy_buf[rows, :], down, NT) * slope).astype(bf16)
        dpre_ref[0, rows, :] = dpre
        slot_acc[rows, :] += mm(dpre, up, NT)

    @pl.when(step == parts - 1)
    def last():
        for n in range(sources):
            rows = slice(n * size, (n + 1) * size)
            out = out_acc[rows, :].astype(bf16)
            out_ref[n, start : start + size, :] = out
            slot_ref[n, 0:size, :] = slot_acc[rows, :].astype(bf16)
            dgate = jnp.sum(
                dy_buf[rows, :].astype(f32) * out.astype(f32), axis=1, keepdims=True
            )
            three = three_rows(row_of(dgate))
            if half:
                slot_ref[n, size:, :] = jnp.zeros((EXTRA, width), bf16)
                slot_ref[n, size:, 0:LANE_B] = carried_ref[n]
                slot_ref[n, size:, LANE_B : LANE_B + size] = three
            else:
                carry_ref[n] = jnp.zeros((EXTRA, LANE_B), bf16)
                carry_ref[n, :, 0:size] = three


def run_experts(half, start, size, x, dy, weights, before):
    sources, _, width = x.shape
    rows = sources * size
    units = weights[0].shape[1]
    parts = len(weights) // 2

    def whole(shape):
        return pl.BlockSpec(shape, lambda g: (0,) * len(shape), pipeline_mode=pl.Buffered(1))

    def shaped(*shape):
        return jax.ShapeDtypeStruct(shape, bf16)

    kept = shaped(parts, rows, units)
    kept_spec = pl.BlockSpec((1, rows, units), lambda g: (g, 0, 0))
    carry = shaped(sources, EXTRA, LANE_B)
    hbm = pl.BlockSpec(memory_space=pl.ANY)
    piece = pl.BlockSpec((sources, size, width), lambda g: (0, start // size, 0))
    return pl.pallas_call(
        functools.partial(expert_kernel, half, 0),
        out_shape=[shaped(*dy.shape), shaped(*x.shape), kept, kept] + ([] if half else [carry]),
        grid=(parts,),
        in_specs=[whole(x.shape), piece]
        + [hbm] * (2 * parts)
        + ([whole(carry.shape), hbm] if half else []),
        out_specs=[piece, whole(x.shape), kept_spec, kept_spec]
        + ([] if half else [whole(carry.shape)]),
        scratch_shapes=[
            pltpu.VMEM((rows, width), bf16),
            pltpu.VMEM((rows, width), bf16),
            pltpu.VMEM((2, width, units), bf16),
            pltpu.VMEM((2, units, width), bf16),
            pltpu.VMEM((rows, width), f32),
            pltpu.VMEM((rows, width), f32),
            pltpu.SemaphoreType.DMA((2, 2)),
        ],
        input_output_aliases={2 * parts + 3: 0} if half else {},
        compiler_params=params(60),
        name="experts",
        cost_estimate=cost(25),
    )(x, dy, *weights, *((before[4], before[0]) if half else ()))


def weight_kernel(dy_ref, x_a, x_b, act_a, act_b, dpre_a, dpre_b, own_out, near_out, far_up, far_down, x_buf, dy_buf):
    step = pl.program_id(0)
    experts, capacity, _ = dy_ref.shape

    @pl.when(step == 0)
    def gated():
        begin = 0
        halves = zip(halves_of(capacity), (x_a, x_b), (0, LANE_B))
        for (start, size), x_ref, lane in halves:
            for n in range(experts):
                rows = slice(begin, begin + size)
                begin += size
                three = x_b[n, x_b.shape[1] - EXTRA :, lane : lane + size].astype(f32)
                gate = column_of(three[0:1] + three[1:2] + three[2:3])
                x_buf[rows, :] = (x_ref[n, 0:size, :].astype(f32) * gate).astype(bf16)
                dy = dy_ref[n, start : start + size, :].astype(f32)
                dy_buf[rows, :] = (dy * gate).astype(bf16)

    cut = act_a.shape[1]
    up = mm(x_buf[:cut, :], dpre_a[0], TN) + mm(x_buf[cut:, :], dpre_b[0], TN)
    down = mm(act_a[0], dy_buf[:cut, :], TN) + mm(act_b[0], dy_buf[cut:, :], TN)
    for j, (out, n) in enumerate(((own_out, 0), (near_out, 0), (None, 0), (near_out, 2))):

        @pl.when(step == j)
        def keep(out=out, n=n):
            if out is None:
                far_up[...] = up
                far_down[...] = down
            else:
                out[n] = up.astype(out.dtype)
                out[n + 1] = down.astype(out.dtype)


def weight_grads(xs, dy, acts, dpres):
    experts, capacity, width = dy.shape
    parts, _, units = acts[0].shape
    assert units == width

    def whole(*shape):
        return pl.BlockSpec(shape, lambda g: (0,) * len(shape), pipeline_mode=pl.Buffered(1))

    kept = [pl.BlockSpec((1,) + a.shape[1:], lambda g: (g, 0, 0)) for a in (*acts, *dpres)]
    return pl.pallas_call(
        weight_kernel,
        out_shape=[
            jax.ShapeDtypeStruct((2, width, units), f32),
            jax.ShapeDtypeStruct((4, width, units), bf16),
            jax.ShapeDtypeStruct((width, units), f32),
            jax.ShapeDtypeStruct((units, width), f32),
        ],
        grid=(parts,),
        in_specs=[whole(*dy.shape)] + [whole(*x.shape) for x in xs] + kept,
        out_specs=[whole(2, width, units), whole(4, width, units)] + [whole(width, units)] * 2,
        scratch_shapes=[pltpu.VMEM((experts * capacity, width), bf16)] * 2,
        compiler_params=params(60),
        name="expert_weight_grads",
        cost_estimate=cost(25),
    )(dy, *xs, *acts, *dpres)


def combine_back_kernel(
    own_ref, hot_a, hot_b, p0a, p1a, p0b, p1b, residual_ref, dy_ref, gates_ref, routes_ref,
    router_ref, gain_ref, w_ref, slot_a, slot_b,
    dres_ref, branch_ref, small_ref, g0, g1, g2, g3, buf_a, buf_b, datt_buf,
):
    experts = router_ref.shape[0]
    table = [0.0] * experts
    last = slot_b.shape[1] - EXTRA
    for slot, hot, buf, lane in ((slot_a, hot_a, buf_a, 0), (slot_b, hot_b, buf_b, LANE_B)):
        size = hot.shape[0] // experts
        for e in range(experts):
            rows = slice(e * size, (e + 1) * size)
            buf[rows, :] = slot[e, 0:size, :]
            picked = mm(slot_b[e, last:, lane : lane + size], hot[rows, :])
            table[e] = table[e] + (picked[0:1] + picked[1:2] + picked[2:3])
    table = jnp.concatenate(table, axis=0)
    residual = residual_ref[...]
    count = residual.shape[0]
    scale = lax.rsqrt(jnp.mean(residual * residual, axis=1, keepdims=True) + norm_eps)
    unit = residual * scale
    gain = gain_ref[...]
    expert_row = iota((experts, count), 0)
    routes = [routes_ref[k : k + 1, :] for k in range(2)]
    gates = [gates_ref[k : k + 1, :] for k in range(2)]
    dgates = [
        jnp.sum(jnp.where(expert_row == r, table, 0.0), axis=0, keepdims=True) for r in routes
    ]
    mean = gates[0] * dgates[0] + gates[1] * dgates[1]
    dlogit = sum(
        jnp.where(expert_row == r, g * (d - mean), 0.0) for r, g, d in zip(routes, gates, dgates)
    )
    small_ref[...] = jnp.zeros_like(small_ref)
    small_ref[0:experts, :] = mm(dlogit, unit * gain, precision=precise)
    dnormed = mm(dlogit, router_ref[...], TN, precise)
    for gate, pick_a, pick_b in ((gates[0], p0a, p0b), (gates[1], p1a, p1b)):
        rows = mm(pick_a[...], buf_a[...]) + mm(pick_b[...], buf_b[...])
        dnormed = dnormed + column_of(gate) * rows
    small_ref[experts : experts + 1, :] = jnp.sum(dnormed * unit, axis=0, keepdims=True)
    scaled = dnormed * gain
    dres = dy_ref[...].astype(f32) + scale * (
        scaled - unit * jnp.mean(scaled * unit, axis=1, keepdims=True)
    )
    dres_ref[...] = dres
    branch = dres.astype(bf16)
    branch_ref[...] = branch
    datt_buf[...] = mm(w_ref[...], branch, NT).astype(bf16)
    for j, piece in enumerate((g0, g1, g2, g3)):
        size = piece.shape[0]
        piece[...] = datt_buf[pl.ds(pl.multiple_of((own_ref[0] ^ j) * size, size), size), :]


def combine_back(own, slots, hots, picks, residual, dy, gates, routes_t, router_t, gain, w_out):
    count, width = residual.shape
    experts = router_t.shape[0]
    shapes = [
        jax.ShapeDtypeStruct((count, width), f32),
        jax.ShapeDtypeStruct((count, width), bf16),
        jax.ShapeDtypeStruct((experts + 8, width), f32),
    ] + [jax.ShapeDtypeStruct((width // 4, count), bf16)] * 4
    results = pl.pallas_call(
        combine_back_kernel,
        out_shape=shapes,
        in_specs=[smem_spec()] + [vmem_spec()] * 15,
        out_specs=[vmem_spec()] * len(shapes),
        scratch_shapes=[pltpu.VMEM((hot.shape[0], width), bf16) for hot in hots]
        + [pltpu.VMEM((width, count), bf16)],
        compiler_params=params(60),
        name="combine_back",
        cost_estimate=cost(11),
    )(own, *hots, *picks, residual, dy, gates, routes_t, router_t, gain, w_out, *slots)
    return results[0], results[1], results[2], results[3:]


def out_grad_kernel(t0, t1, t2, t3, branch_ref, keep_ref, give_ref):
    branch = branch_ref[...]
    keep_ref[0] = mm(t0[...], branch)
    keep_ref[1] = mm(t2[...], branch)
    give_ref[0] = mm(t1[...], branch).astype(bf16)
    give_ref[1] = mm(t3[...], branch).astype(bf16)


def out_grads(parts, branch):
    shape = (2, parts[0].shape[0], branch.shape[1])
    return pl.pallas_call(
        out_grad_kernel,
        out_shape=[jax.ShapeDtypeStruct(shape, f32), jax.ShapeDtypeStruct(shape, bf16)],
        in_specs=[vmem_spec()] * 5,
        out_specs=[vmem_spec()] * 2,
        compiler_params=params(60),
        name="w_out_grads",
        cost_estimate=cost(3),
    )(*parts, branch)


def combine_kernel(p0a, p1a, p0b, p1b, residual_ref, gates_ref, out_ref, y_ref, buf_a, buf_b):
    experts, capacity, _ = out_ref.shape
    for (start, size), buf in zip(halves_of(capacity), (buf_a, buf_b)):
        for e in range(experts):
            buf[e * size : (e + 1) * size, :] = out_ref[e, start : start + size, :]
    total = residual_ref[...]
    for k, (pick_a, pick_b) in enumerate(((p0a, p0b), (p1a, p1b))):
        rows = mm(pick_a[...], buf_a[...]) + mm(pick_b[...], buf_b[...])
        total = total + column_of(gates_ref[k : k + 1, :]) * rows
    y_ref[...] = total.astype(bf16)


def combine(out, picks, residual, gates):
    experts, capacity, width = out.shape
    return pl.pallas_call(
        combine_kernel,
        out_shape=jax.ShapeDtypeStruct(residual.shape, bf16),
        in_specs=[vmem_spec()] * 7,
        out_specs=vmem_spec(),
        scratch_shapes=[
            pltpu.VMEM((experts * size, width), bf16) for _, size in halves_of(capacity)
        ],
        compiler_params=params(60),
        name="combine",
        cost_estimate=cost(6),
    )(*picks, residual, gates, out)


def spread_kernel(places_ref, d01, d2, w_ref, near_out, last_out, far_out, own_out, d_buf):
    step = pl.program_id(0)
    heads = d_buf.shape[0] // (3 * HEAD_DIM)
    for c, (part, n) in enumerate(((d01, 0), (d01, 3), (d2, 0))):
        for t in range(3):
            start = (t * heads + c) * HEAD_DIM
            d_buf[start : start + HEAD_DIM, :] = part[(n + t) * HEAD_DIM : (n + t + 1) * HEAD_DIM, :]
    dn = mm(d_buf[...], w_ref[...], TN)
    for n, out in enumerate((near_out, last_out, far_out, own_out)):

        @pl.when(step == n)
        def keep(out=out):
            out[...] = dn.astype(out.dtype)


def spread(places, parts, w_t):
    row_len = parts[0].shape[1]
    cols, width = w_t.shape
    steps = places.shape[0]
    count = row_len // steps
    tiles = [pl.BlockSpec((p.shape[0], count), lambda g, places: (0, places[g])) for p in parts]

    def whole(shape):
        return pl.BlockSpec(shape, lambda g, places: (0, 0), pipeline_mode=pl.Buffered(1))

    return pl.pallas_call(
        spread_kernel,
        out_shape=[jax.ShapeDtypeStruct((count, width), t) for t in (bf16, bf16, f32, f32)],
        grid_spec=pltpu.PrefetchScalarGridSpec(
            num_scalar_prefetch=1,
            grid=(steps,),
            in_specs=tiles + [whole((cols, width))],
            out_specs=[whole((count, width))] * 4,
            scratch_shapes=[pltpu.VMEM((cols, count), bf16)],
        ),
        compiler_params=params(40),
        name="spread_back",
        cost_estimate=cost(8),
    )(places, *parts, w_t)


def mix_kernel(taken, special, moved_ref, grad_ref, keep_ref, near_ref, far_ref, small_ref, out_ref):
    exps, rows, width = out_ref.shape
    sums = moved_ref[0, 0:taken].astype(f32)
    for e in range(1, exps):
        sums = sums + moved_ref[e, 0:taken].astype(f32)
    gout = keep_ref[0] + near_ref[0].astype(f32) + far_ref[...].astype(f32)
    out_rows = gout.shape[0] // exps
    pad = rows - taken - grad_ref.shape[2] - out_rows - 2 * special
    for e in range(exps):
        high, mid, _ = split_three(small_ref[e * special : (e + 1) * special, :])
        parts = [sums, grad_ref[e, 0].astype(f32), gout[e * out_rows : (e + 1) * out_rows]]
        parts += [high.astype(f32), mid.astype(f32)]
        if pad:
            parts.append(jnp.zeros((pad, width), f32))
        out_ref[e] = jnp.concatenate(parts, axis=0).astype(bf16)


def mix(moved, taken, grad, keep, near, far, small, special):
    exps, _, rows, width = grad.shape
    total = taken + rows + keep.shape[1] // exps + 2 * special
    return pl.pallas_call(
        functools.partial(mix_kernel, taken, special),
        out_shape=jax.ShapeDtypeStruct((exps, total + -total % 8, width), bf16),
        in_specs=[vmem_spec()] * 6,
        out_specs=vmem_spec(),
        compiler_params=params(50),
        name="mix_sums",
        cost_estimate=cost(2),
    )(moved, grad, keep, near, far, small)


def fold_kernel(start, taken, special, moved_ref, out_ref):
    exps, rows, width = out_ref.shape
    sums = moved_ref[0, start : start + taken].astype(f32)
    for e in range(1, exps):
        sums = sums + moved_ref[e, start : start + taken].astype(f32)
    body = taken - 2 * special
    high, mid, _ = split_three(
        sums[body : body + special] + sums[body + special : body + 2 * special]
    )
    parts = [sums[:body], high.astype(f32), mid.astype(f32)]
    if rows > taken:
        parts.append(jnp.zeros((rows - taken, width), f32))
    sums = jnp.concatenate(parts, axis=0).astype(bf16)
    for e in range(exps):
        out_ref[e] = sums


def fold(moved, start, taken, special):
    exps, _, width = moved.shape
    return pl.pallas_call(
        functools.partial(fold_kernel, start, taken, special),
        out_shape=jax.ShapeDtypeStruct((exps, taken + -taken % 8, width), bf16),
        in_specs=[vmem_spec()],
        out_specs=vmem_spec(),
        compiler_params=params(40),
        name="fold_sums",
        cost_estimate=cost(2),
    )(moved)


def lay_out_kernel(rows, out_rows, small_rows, own_ref, *refs):
    arrays, refs = refs[:8], refs[8:]
    w_ref, gain_ref, grad_ref, ggain_ref, gout_ref, small_ref, b0, b1, sems = refs
    hids, exps = b0.shape[0], b0.shape[1]
    step = pl.program_id(0)
    block = grad_ref.shape[0]

    @pl.when(step == 0)
    def fetch():
        copies = [
            pltpu.make_async_copy(arrays[4 * c + j], buf.at[own_ref[0] ^ j], sems.at[c, j])
            for c, buf in enumerate((b0, b1))
            for j in range(hids)
        ]
        for copy in copies:
            copy.start()
        for copy in copies:
            copy.wait()

    cols = pl.ds(pl.multiple_of(step * block, block), block)
    blocks = {}
    for h in range(hids):
        for c, (buf, start) in enumerate(((b0, 0), (b0, rows), (b1, 0))):
            pieces = [buf[h, e, start : start + rows, cols].astype(f32) for e in range(exps)]
            blocks[h, c] = jnp.concatenate(pieces, axis=0)
    stacked = [
        blocks[h, c][t * HEAD_DIM : (t + 1) * HEAD_DIM]
        for t in range(3)
        for h in range(hids)
        for c in range(3)
    ]
    grad = jnp.concatenate(stacked, axis=0).T
    grad_ref[...] = grad
    total = jnp.sum(grad * w_ref[...].astype(f32), axis=1, keepdims=True)
    ggain_ref[...] = row_of(total) / gain_ref[...]
    for h in range(hids):
        for e in range(exps):
            n = h * exps + e
            piece = b1[h, e, rows : rows + out_rows, cols]
            gout_ref[n * out_rows : (n + 1) * out_rows, :] = piece.astype(f32)
    start = rows + out_rows
    for e in range(exps):
        total = 0.0
        for h in range(hids):
            high = b1[h, e, start : start + small_rows, cols].astype(f32)
            low = b1[h, e, start + small_rows : start + 2 * small_rows, cols].astype(f32)
            total = total + (high + low)
        small_ref[e * small_rows : (e + 1) * small_rows, :] = total


def lay_out(own, chunks, rows, out_rows, small_rows, w_qkv, gain, block=256):
    width, cols = w_qkv.shape
    smalls = chunks[0][0].shape[0] * small_rows
    arrays = [a for chunk in chunks for a in chunk]
    tile = pl.BlockSpec((block, cols), lambda g: (g, 0))
    row = pl.BlockSpec((1, block), lambda g: (0, g))
    return pl.pallas_call(
        functools.partial(lay_out_kernel, rows, out_rows, small_rows),
        out_shape=[
            jax.ShapeDtypeStruct((width, cols), f32),
            jax.ShapeDtypeStruct((1, width), f32),
            jax.ShapeDtypeStruct((width, width), f32),
            jax.ShapeDtypeStruct((smalls, width), f32),
        ],
        grid=(width // block,),
        in_specs=[smem_spec()] + [pl.BlockSpec(memory_space=pl.ANY)] * 8 + [tile, row],
        out_specs=[
            tile, row, pl.BlockSpec((width, block), lambda g: (0, g)),
            pl.BlockSpec((smalls, block), lambda g: (0, g)),
        ],
        scratch_shapes=[pltpu.VMEM((4,) + chunk[0].shape, bf16) for chunk in chunks]
        + [pltpu.SemaphoreType.DMA((2, 4))],
        compiler_params=params(50),
        name="lay_out_sums",
        cost_estimate=cost(10),
    )(own, *arrays, w_qkv, gain)


def adam_update(weight, gradient, first_moment, second_moment, live_mask):
    first_next = beta_one * first_moment + (1.0 - beta_one) * gradient
    second_next = beta_two * second_moment + (1.0 - beta_two) * gradient * gradient
    first_hat = first_next / (1.0 - beta_one**adam_steps)
    second_hat = second_next / (1.0 - beta_two**adam_steps)
    weight_next = weight - learn_rate * first_hat / (jnp.sqrt(second_hat) + adam_eps)
    return (
        jnp.where(live_mask, weight_next, weight),
        jnp.where(live_mask, first_next, first_moment),
        jnp.where(live_mask, second_next, second_moment),
    )


def expert_update_kernel(live_ref, own_ref, near_ref, far_ref, weight_ref, first_ref, second_ref, *outs):
    live = live_ref[0] > 0
    grad = own_ref[0] + near_ref[0].astype(f32) + far_ref[...].astype(f32)
    grad = jnp.where(live, grad, 0.0)
    outs[0][...] = grad
    updated = adam_update(weight_ref[...], grad, first_ref[...], second_ref[...], live)
    for out, value in zip(outs[1:], updated):
        out[...] = value


def expert_update(live, own, near, number, far, weight, first_moment, second_moment, block=128):
    tile = pl.BlockSpec((block, weight.shape[1]), lambda g: (g, 0))
    stacked = pl.BlockSpec((1, block, weight.shape[1]), lambda g: (number, g, 0))
    return pl.pallas_call(
        expert_update_kernel,
        out_shape=[jax.ShapeDtypeStruct(weight.shape, f32)] * 4,
        grid=(weight.shape[0] // block,),
        in_specs=[smem_spec(), stacked, stacked] + [tile] * 4,
        out_specs=[tile] * 4,
        compiler_params=params(60),
        name="expert_update",
        cost_estimate=cost(8),
    )(live, own, near, far, weight, first_moment, second_moment)


def tie(value, other):
    return lax.optimization_barrier((value, other))[0]


def exchange(value, axis):
    return lax.all_to_all(value, axis, split_axis=0, concat_axis=0, tiled=True)


def split_sum(value, axis, distance):
    pairs = value.reshape((value.shape[0] // 2, 2) + value.shape[1:])
    low = (lax.axis_index(axis) & distance) == 0
    keep = jnp.where(low, pairs[:, 0], pairs[:, 1])
    give = jnp.where(low, pairs[:, 1], pairs[:, 0]).astype(bf16)
    return keep + swap(give, axis, distance).astype(f32)


def halves(value):
    high = lax.reduce_precision(value, 8, 7)
    return high.astype(bf16), (value - high).astype(bf16)


def pad_rows(value):
    return jnp.pad(value, ((0, 0), (0, -value.shape[1] % 8), (0, 0)))


def gather_hid(value):
    far = swap(value, "hid", 2)
    near = swap(value, "hid", 1)
    return value, near, far, swap(far, "hid", 1)


def body(
    tokens, cotangent, routes, segments, lengths, gain_attn, gain_moe, w_qkv, w_out, router_w,
    router_first, router_second, up_w, down_w, up_first, up_second, down_first, down_second,
):
    exp_count = lax.axis_size("exp")
    hid_count = lax.axis_size("hid")
    hid = lax.axis_index("hid")
    exp_index = lax.axis_index("exp")
    own = jnp.stack([hid, exp_index]).astype(jnp.int32)
    x_own = tokens[0]
    dy = cotangent[0]
    count, width = x_own.shape
    experts = router_w.shape[1]
    frozen_count = experts // 2
    capacity = max(2, 3 * count // experts)
    group = width // hid_count
    heads = group // HEAD_DIM
    is_new = exp_index >= frozen_count

    x_far = [swap(x_own, "hid", 2)]
    x_near = swap(x_own, "hid", 1)
    routes_t = routes[0].T
    hots, picks, dy_send = make_tables(routes_t, dy, experts, capacity)
    seg_row = segments[0]
    info = jnp.stack(
        [
            jnp.sum((seg_row < 1).astype(jnp.int32)),
            jnp.sum((seg_row < 2).astype(jnp.int32)),
            lengths[0],
        ]
    )
    up_low = up_w[0].astype(bf16)
    down_low = down_w[0].astype(bf16)
    router_t = router_w.T
    first = project_qkv(own, (x_own, x_near), gain_attn[None], w_qkv)
    x_far, (x_near, info, dy_send, up_low, down_low, router_t, routes_t) = (
        lax.optimization_barrier(
            (x_far, (x_near, info, dy_send, up_low, down_low, router_t, routes_t))
        )
    )
    x_last = [swap(half, "hid", 1) for half in x_far]
    dy_all = exchange(dy_send, "exp")

    up_far = swap(up_low, "hid", 2)
    up_near, down_near = (swap(tie(low, x_last), "hid", 1) for low in (up_low, down_low))

    w_t = first[8]
    second = project_qkv(own, (*x_far, *x_last), gain_attn[None], w_t, True)
    a_parts, qkv_parts, k_parts, v_parts = (
        (*first[n : n + 2], *second[n : n + 2]) for n in (0, 2, 4, 6)
    )
    out_heads, logs, keys, pieces = attend(info, own, k_parts, qkv_parts)
    pieces, (up_far, up_near, down_near) = lax.optimization_barrier(
        (pieces, (up_far, up_near, down_near))
    )
    att_parts = [pieces[0]] + [swap(pieces[j], "hid", j) for j in range(1, hid_count)]
    att_parts, down_low = lax.optimization_barrier((att_parts, down_low))
    down_far = swap(down_low, "hid", 2)

    residual, gates, *sends = make_dispatch(
        own, att_parts, x_own, w_out, gain_moe[None], router_t, routes_t, hots
    )
    up_far, down_far = tie((up_far, down_far), residual)
    up_last, down_last = swap(up_far, "hid", 1), swap(down_far, "hid", 1)
    weights = (up_low, down_low, up_near, down_near, up_far, down_far, up_last, down_last)
    sends = tie(sends, dy_all)
    x_rows = [exchange(send, "exp") for send in sends]

    results = [None]
    for half, ((start, size), x) in enumerate(zip(halves_of(capacity), x_rows)):
        results.append(run_experts(half, start, size, x, dy_all, weights, results[-1]))
    outs = results[2][0]
    slots, acts, dpres = ([r[n] for r in results[1:]] for n in (1, 2, 3))
    slot_back = [exchange(slot, "exp") for slot in slots]

    own_part, near_part, far_up, far_down = weight_grads(x_rows, dy_all, acts, dpres)
    slot_back, near_part = lax.optimization_barrier((slot_back, near_part))
    near_part = swap(near_part, "hid", 1)

    dres, branch, small, datt_parts = combine_back(
        own, slot_back, hots, picks, residual, dy, gates, routes_t, router_t, gain_moe[None], w_out
    )
    out_back = exchange(tie(outs, slot_back), "exp")
    datt_parts, near_part = lax.optimization_barrier((datt_parts, near_part))
    datt_parts = [datt_parts[0]] + [swap(datt_parts[j], "hid", j) for j in range(1, hid_count)]
    gout, gout_near = out_grads(att_parts, branch)

    out_rows = width // (hid_count * exp_count)
    small_rows = -(-(experts + 1) // exp_count)
    missing = max(0, exp_count * small_rows - small.shape[0])
    small = jnp.pad(small, ((0, missing), (0, 0)))
    gout_near = swap(gout_near, "hid", 1)
    far_up = (far_up + near_part[2].astype(f32)).astype(bf16)
    far_down = (far_down + near_part[3].astype(f32)).astype(bf16)
    far_up, far_down = tie((far_up, far_down), datt_parts)
    far_up = swap(far_up, "hid", 2)
    rows = 3 * HEAD_DIM // exp_count
    given = (info, own, keys, v_parts, qkv_parts, datt_parts, out_heads, logs, a_parts)
    dqkv_first, grads_first = attend_back(0, heads - 1, exp_count, *given)
    gout_near = tie(gout_near, dqkv_first)
    gout_far = swap((gout[1] + gout_near[1].astype(f32)).astype(bf16), "hid", 2)
    grads_first, out_back, far_up, gout_far = lax.optimization_barrier(
        (grads_first, out_back, far_up, gout_far)
    )
    far_down = swap(tie(far_down, gout_far), "hid", 2)
    first = exchange(pad_rows(grads_first.reshape(exp_count, -1, width)), "exp")
    dqkv_last, grads_last = attend_back(heads - 1, 1, exp_count, *given)
    dqkv = [dqkv_first, dqkv_last]
    known = (heads - 1) * rows
    first_sums = mix(first, known, grads_last, gout, gout_near, gout_far, small, small_rows)
    second = exchange(first_sums, "exp")

    dqkv, far_down = tie((dqkv, far_down), first_sums)
    places = jnp.stack([hid ^ j for j in (1, 3, 2, 0)]).astype(jnp.int32)
    near_dn, last_dn, far_dn, own_dn = spread(places, dqkv, w_t)
    near_dn, last_dn = swap(near_dn, "hid", 1), swap(last_dn, "hid", 1)
    far_dn = (far_dn + last_dn.astype(f32)).astype(bf16)
    out_back = tie(out_back, far_dn)
    far_dn = swap(far_dn, "hid", 2)

    out_tokens = combine(out_back, picks, residual, gates)
    second, out_tokens = lax.optimization_barrier((second, out_tokens))
    last_sums = fold(second, known, rows + out_rows + 2 * small_rows, small_rows)
    far_dn, far_up = tie((far_dn, far_up), last_sums)
    live = is_new.astype(jnp.int32).reshape(1)
    grad_up, up_next, up_first_next, up_second_next = expert_update(
        live, own_part, near_part, 0, far_up, up_w[0], up_first[0], up_second[0]
    )
    dnormed = own_dn + near_dn.astype(f32) + far_dn.astype(f32)
    x = x_own.astype(f32)
    scale = lax.rsqrt(jnp.mean(x * x, axis=-1, keepdims=True) + norm_eps)
    unit = x * scale
    scaled = dnormed * gain_attn
    grad_tokens = (
        dres + scale * (scaled - unit * jnp.mean(scaled * unit, axis=-1, keepdims=True))
    ).astype(bf16)
    third = exchange(last_sums, "exp")
    third, grad_tokens, up_next = lax.optimization_barrier((third, grad_tokens, up_next))
    far_down = tie(far_down, third)
    gathered = gather_hid(second[:, :known])
    grad_down = own_part[1] + near_part[1].astype(f32) + far_down.astype(f32)
    grad_down = jnp.where(is_new, grad_down, 0.0)
    down_next, down_first_next, down_second_next = adam_update(
        down_w[0], grad_down, down_first[0], down_second[0], is_new
    )
    gathered = (gathered, gather_hid(third))
    grad_qkv, grad_gain_attn, grad_out_proj, small = lay_out(
        own, gathered, rows, out_rows, small_rows, w_qkv, gain_attn[None]
    )
    grad_gain_moe = small[experts]
    live_columns = (jnp.arange(experts, dtype=jnp.int32) >= frozen_count)[None, :]
    grad_router = jnp.where(live_columns, small[:experts].T, 0.0)
    router_new, router_first_next, router_second_next = adam_update(
        router_w[:, frozen_count:], grad_router[:, frozen_count:], router_first, router_second, True
    )
    router_next = jnp.concatenate([router_w[:, :frozen_count], router_new], axis=1)
    grad_gain_attn = grad_gain_attn[0]
    return (
        out_tokens[None],
        grad_tokens[None],
        grad_qkv,
        grad_out_proj,
        grad_gain_attn,
        grad_gain_moe,
        grad_router,
        router_next,
        router_first_next,
        router_second_next,
        grad_up[None],
        grad_down[None],
        up_next[None],
        down_next[None],
        up_first_next[None],
        up_second_next[None],
        down_first_next[None],
        down_second_next[None],
    )


def solution(mesh):
    tok = P("exp", "hid", None)
    up = P("exp", None, "hid")
    return jax.shard_map(
        body,
        mesh=mesh,
        in_specs=(tok, tok, tok, P("exp", None), P("exp")) + (P(),) * 7
        + (up, tok, up, up, tok, tok),
        out_specs=(tok, tok) + (P(),) * 8 + (up, tok, up, tok, up, up, tok, tok),
        check_vma=False,
    )
```
